256 devices in a mesh: dp: 32 (over x_lo, z, core), feat: 8 (over x_hi, y).
Axes of the slice: x: 4 (x_hi: 2, x_lo: 2; x = x_hi * 2 + x_lo), y: 4, z: 8, core: 2. Of those that a mesh axis runs over, the one named last changes fastest.
Arguments:
- student: bfloat16 [16384, 2048], P('dp'), may hold values from -6 to 6
- weight: bfloat16 [2048, 4096], P('dp', 'feat'), may hold values from -0.125 to 0.125
- teacher: bfloat16 [16384, 4096], P('dp', 'feat'), may hold values from -6 to 6
Outputs:
- loss: float32 [], replicated
- grad_weight: float32 [2048, 4096], P('dp', 'feat')
The draws below stay inside these ranges and needn't reach their ends.
All inputs are finite; a program needn't handle non-finite values.
Results may differ from the reference program's by a relative error of at most 0.0022.
The reference program's roundings to bfloat16 on the way (of `student_normal`, `teacher_normal`, `slope` and `delta`) count: a program that leaves them out, or rounds other values in their place, can miss the bound.
Values may be sent and summed in bfloat16 or wider, within the bound.
A program may use at most 64 MiB of HBM per device.

```python
import jax
import jax.numpy as jnp
from jax import lax

D_IN = 2048
WIDTH = 4096
TOKENS = 16384


def spiked(values, key, source, target, blocks, factor):
    owner, partner = [(jnp.arange(values.shape[axis_at]) // (values.shape[axis_at] // blocks)).reshape([-1 if axis == axis_at else 1 for axis in range(values.ndim)]) for axis_at in (source, target)]
    chosen = jax.random.permutation(key, blocks)[partner]
    strong = (owner == chosen) | (owner == (partner + blocks // 2) % blocks)
    return jnp.where(strong, factor * values, values)


def levels(stream_key, extent, pieces, smallest, top_value):
    factor_of = 1.0
    for axis_at, blocks in pieces:
        draws = jax.random.uniform(jax.random.fold_in(jax.random.fold_in(stream_key, 6), axis_at), (blocks,), jnp.float32, smallest / len(pieces), top_value / len(pieces))
        factor_of = factor_of * jnp.repeat(jnp.exp(draws), extent[axis_at] // blocks).reshape((-1,) + (1,) * (len(extent) - 1 - axis_at))
    return factor_of


def scatter_about(key, shape, deviation, most, shards=(), kind=jnp.bfloat16):
    values = deviation * jax.random.normal(key, shape, jnp.float32)
    if shards:
        values = values * levels(key, shape, shards, -0.22, 0.18)
    return jnp.clip(values, -most, most).astype(kind)


def bell_draw_with(own_key, dims, scale, bound, shards, heavy, held_as=jnp.bfloat16):
    drawn = scale * jax.random.normal(own_key, dims, jnp.float32)
    if shards:
        drawn = drawn * levels(own_key, dims, shards, -0.22, 0.18)
    return jnp.clip(spiked(drawn, jax.random.fold_in(own_key, 3), *heavy), -bound, bound).astype(held_as)


def setup_inputs(seed: int = 0) -> dict:
    keys = jax.random.split(jax.random.key(seed), 4)
    return {
        "student": scatter_about(keys[0], (TOKENS, D_IN), 1.0, 6.0, ((0, 32),)),
        "weight": scatter_about(keys[1], (D_IN, WIDTH), D_IN ** -0.5, 0.125, ((0, 32), (1, 8))),
        "teacher": bell_draw_with(keys[2], (TOKENS, WIDTH), 1.0, 6.0, ((0, 32), (1, 8)), (0, 1, 32, 2.75)),
    }


OFF_WEIGHT = 0.5
NORM_EPS = 1e-05
LOSS_SCALE = 128.0

def column_norm(values, total):
    center = lax.optimization_barrier(jnp.sum(values, axis=0)) / total
    spread = lax.optimization_barrier(jnp.sum(values * values, axis=0)) / total - center * center
    recip = lax.rsqrt(spread + NORM_EPS)
    return ((values - center) * recip, recip)

def reference(student, weight, teacher):
    total = student.shape[0]
    projected = jnp.dot(student, weight, preferred_element_type=jnp.float32)
    student_float, recip = column_norm(projected, total)
    student_normal = student_float.astype(jnp.bfloat16)
    teacher_float, teacher_recip = column_norm(teacher.astype(jnp.float32), total)
    teacher_normal = teacher_float.astype(jnp.bfloat16)
    corr = jnp.dot(student_normal.T, teacher_normal, preferred_element_type=jnp.float32) / total
    index_line = jnp.arange(corr.shape[0], dtype=jnp.int32)
    on_diag = index_line[:, None] == index_line[None, :]
    loss_sum = jnp.sum(jnp.where(on_diag, (1.0 - corr) ** 2, OFF_WEIGHT * corr * corr))
    slope = jnp.where(on_diag, -2.0 * (1.0 - corr), 2.0 * OFF_WEIGHT * corr).astype(jnp.bfloat16)
    upstream = jnp.dot(teacher_normal, slope.T, preferred_element_type=jnp.float32) / total
    mean_grad = lax.optimization_barrier(jnp.sum(upstream, axis=0)) / total
    mean_cross = lax.optimization_barrier(jnp.sum(upstream * student_float, axis=0)) / total
    delta = (recip * (upstream - mean_grad - student_float * mean_cross)).astype(jnp.bfloat16)
    grad_weight = LOSS_SCALE * jnp.dot(student.T, delta, preferred_element_type=jnp.float32)
    return (loss_sum / corr.shape[0], grad_weight)
```

```python
import functools

import jax
import jax.numpy as jnp
from jax import lax
from jax.experimental import pallas as pl
from jax.experimental.pallas import tpu as pltpu
from jax.sharding import PartitionSpec as P

OFF_WEIGHT = 0.5
NORM_EPS = 1e-05
LOSS_SCALE = 128.0
F32 = jnp.float32
BF16 = jnp.bfloat16
MESH = pl.DeviceIdType.MESH


def arms(n):
    return ((n // 2, n // 2 - 1), (n // 2 - 1, n // 2))


def around(at, n):
    return lax.rem(at + n, n)


def kernel(
    nz, ny, x_ref, w_ref, t_ref, loss_ref, g_ref,
    tb, tn, xp, wb, pj, sT, cc, cb, xs, xr, sl, uu, gg, gb, gxs, gxr, gcs, gcr,
    ar_t, ar_p, ar_u, tst, lacc, lf, lc,
    tc_s, tc_r, tx_s, tx_r, ty_s, ty_r, xc_s, xc_r, wc_s, wc_r, wx_s, wx_r, wz_s, wz_r,
    cz_s, cz_r, cx_s, cx_r, sx_s, sx_r, sz_s, sz_r, gz_s, gz_r, gx_s, gx_r, gc_s, gc_r,
    at_s, at_r, ap_s, ap_r, au_s, au_r, ts_s, ts_r, lf_s, lf_r, lc_s, lc_r,
):
    d = lax.axis_index("dp")
    f = lax.axis_index("feat")
    chips = 2 * nz
    feats = 2 * ny
    core = lax.rem(d, 2)
    chip = lax.div(d, 2)
    z = lax.rem(chip, nz)
    xl = lax.div(chip, nz)
    y = lax.rem(f, ny)
    xh = lax.div(f, ny)
    rows = x_ref.shape[0]
    cols = w_ref.shape[1]
    half = cols // 2
    total_rows = float(rows * 2 * chips)
    width_all = cols * feats

    mate = (d + 1 - 2 * core, f)

    def dp_at(chip_at):
        return (chip_at * 2 + core, f)

    def z_at(at):
        return dp_at(xl * nz + at)

    def y_at(at):
        return (d, xh * ny + at)

    x_mate = dp_at((1 - xl) * nz + z)
    h_mate = (d, (1 - xh) * ny + y)

    sent = []

    def copy(src, dst, s, r, to):
        return pltpu.make_async_remote_copy(
            src_ref=src, dst_ref=dst, send_sem=s, recv_sem=r, device_id=to, device_id_type=MESH
        )

    def send(src, dst, s, r, to):
        c = copy(src, dst, s, r, to)
        c.start()
        sent.append(c)

    def arrived(dst, s, r, to):
        copy(dst, dst, s, r, to).wait_recv()

    def ag_step(s, n, pos, at, slot, ss, rs, streams=(0, 1)):
        for st in streams:
            for dr in (0, 1):
                if s < arms(n)[st][dr]:
                    sgn = 1 - 2 * dr
                    p = around(pos - sgn * s, n)
                    if s > 0:
                        arrived(slot(st, p), ss.at[st, dr, s - 1], rs.at[st, dr, s - 1], mate)
                    send(
                        slot(st, p), slot(st, p), ss.at[st, dr, s], rs.at[st, dr, s],
                        at(around(pos + sgn, n)),
                    )

    def ag_end(n, pos, slot, ss, rs, streams=(0, 1)):
        for st in streams:
            for dr in (0, 1):
                h = arms(n)[st][dr]
                if h:
                    p = around(pos - (1 - 2 * dr) * h, n)
                    arrived(slot(st, p), ss.at[st, dr, h - 1], rs.at[st, dr, h - 1], mate)

    def rs_step(s, n, pos, at, buf, local, ss, rs):
        for st in (1, 0):
            for dr in (0, 1):
                h = arms(n)[st][dr]
                if s < h:
                    sgn = 1 - 2 * dr
                    p = around(pos + sgn * (h - s), n)
                    v = local(st, p)
                    if s > 0:
                        arrived(buf.at[st, dr, s], ss.at[st, dr, s - 1], rs.at[st, dr, s - 1], mate)
                        v = v + buf[st, dr, s].astype(F32)
                    buf[st, dr, s] = v.astype(buf.dtype)
                    send(
                        buf.at[st, dr, s], buf.at[st, dr, s + 1], ss.at[st, dr, s], rs.at[st, dr, s],
                        at(around(pos + sgn, n)),
                    )

    def rs_total(st, n, pos, buf, local, ss, rs):
        v = local(st, pos)
        for dr in (0, 1):
            h = arms(n)[st][dr]
            if h:
                arrived(buf.at[st, dr, h], ss.at[st, dr, h - 1], rs.at[st, dr, h - 1], mate)
                v = v + buf[st, dr, h].astype(F32)
        return v

    def ar_copy(buf, ss, rs, k):
        return copy(buf.at[chip], buf.at[chip], ss.at[k - 1], rs.at[k - 1], dp_at(around(chip + k, chips)))

    def ar_start(buf, ss, rs):
        @pl.loop(1, chips)
        def _(k):
            ar_copy(buf, ss, rs, k).start()

    def ar_wait(buf, ss, rs):
        @pl.loop(1, chips)
        def _(k):
            arrived(buf.at[around(chip - k, chips)], ss.at[k - 1], rs.at[k - 1], mate)

        return jnp.sum(buf[...], axis=0)

    def ar_sent(buf, ss, rs):
        @pl.loop(1, chips)
        def _(k):
            ar_copy(buf, ss, rs, k).wait_send()

    def f_copy(buf, ss, rs, k):
        return copy(buf.at[f], buf.at[f], ss.at[k - 1], rs.at[k - 1], (d, around(f + k, feats)))

    def f_start(buf, ss, rs):
        @pl.loop(1, feats)
        def _(k):
            f_copy(buf, ss, rs, k).start()

    def f_wait(buf, ss, rs):
        @pl.loop(1, feats)
        def _(k):
            arrived(buf.at[around(f - k, feats)], ss.at[k - 1], rs.at[k - 1], mate)

    def f_sent(buf, ss, rs):
        @pl.loop(1, feats)
        def _(k):
            f_copy(buf, ss, rs, k).wait_send()

    def norm_of(sums, squares):
        center = sums / total_rows
        spread = squares / total_rows - center * center
        return center, lax.rsqrt(spread + NORM_EPS)

    barrier = pltpu.get_barrier_semaphore()

    def greet(to):
        pl.semaphore_signal(barrier, inc=1, device_id=to, device_id_type=MESH)

    greet(mate)

    @pl.loop(1, feats)
    def _(k):
        greet((d, around(f + k, feats)))

    @pl.loop(1, chips)
    def _(k):
        greet(dp_at(around(chip + k, chips)))

    my_cols = pl.ds(pl.multiple_of(core * half, half), half)
    mate_cols = pl.ds(pl.multiple_of((1 - core) * half, half), half)
    wb[xl, z, core] = w_ref[:, my_cols]
    tb[0, y, 0] = t_ref[...]
    pl.semaphore_wait(barrier, feats + chips - 1)

    send(w_ref.at[:, mate_cols], wb.at[xl, z, core], wc_s, wc_r, mate)
    send(t_ref, tb.at[0, y, 1], tc_s.at[0, 0], tc_r.at[0, 0], mate)

    def t_slot(st, p):
        return tb.at[st, p, 0]

    def t_next(s, streams):
        ag_step(s, ny, y, y_at, t_slot, ty_s, ty_r, streams)

    t_next(0, (0,))
    send(t_ref, tb.at[1, y, 0], tx_s, tx_r, h_mate)
    send(x_ref, xp, xc_s, xc_r, mate)

    comes = []
    for st in (0, 1):
        order = [(0, None)]
        for s in range(ny // 2):
            for dr in (0, 1):
                if s < arms(ny)[st][dr]:
                    order.append((-(1 - 2 * dr) * (s + 1), (dr, s)))
        comes.append(order)

    def t_hand(st, e):
        off, _ = comes[st][e]
        p = around(y + off, ny)
        send(tb.at[st, p, 0], tb.at[st, p, 1], tc_s.at[st, e], tc_r.at[st, e], mate)

    def t_come(st, e):
        off, (dr, s) = comes[st][e]
        arrived(tb.at[st, around(y + off, ny), 0], ty_s.at[st, dr, s], ty_r.at[st, dr, s], mate)

    def t_normal(st, e, wait_mate=True):
        off, _ = comes[st][e]
        p = around(y + off, ny)
        if wait_mate:
            arrived(tb.at[st, p, 1], tc_s.at[st, e], tc_r.at[st, e], mate)
        at = (xh if st == 0 else 1 - xh) * ny + p
        center = tst[at, 0:1, :]
        recip = tst[at, 1:2, :]
        for slot in (0, 1):

            @pl.loop(0, rows // 64)
            def _(i):
                here = pl.multiple_of(i * 64, 64)
                v = tb[st, p, slot, pl.ds(here, 64), :].astype(F32)
                there = pl.multiple_of(slot * rows + i * 64, 64)
                tn[st, p, pl.ds(there, 64), :] = ((v - center) * recip).astype(BF16)

    def w_slot(st, p):
        return wb.at[xl if st == 0 else 1 - xl, p]

    def w_next(s, streams=(0, 1)):
        ag_step(s, nz, z, z_at, w_slot, wz_s, wz_r, streams)

    arrived(wb.at[xl, z, 1 - core], wc_s, wc_r, mate)
    send(wb.at[xl, z], wb.at[xl, z], wx_s, wx_r, x_mate)
    w_next(0, (0,))

    arrived(tb.at[0, y, 1], tc_s.at[0, 0], tc_r.at[0, 0], mate)

    def t_sum(i, carry):
        a, b = carry
        for slot in (0, 1):
            v = tb[0, y, slot, pl.ds(pl.multiple_of(i * 64, 64), 64), :].astype(F32).reshape(8, 8, cols)
            a = a + jnp.sum(v, axis=0)
            b = b + jnp.sum(v * v, axis=0)
        return a, b

    zero = jnp.zeros((8, cols), F32)
    a, b = lax.fori_loop(0, rows // 64, t_sum, (zero, zero))
    ar_t[chip] = zero
    ar_t[chip, 0:1, :] = jnp.sum(a, axis=0, keepdims=True)
    ar_t[chip, 1:2, :] = jnp.sum(b, axis=0, keepdims=True)
    ar_start(ar_t, at_s, at_r)

    arrived(wb.at[1 - xl, z], wx_s, wx_r, mate)
    w_next(0, (1,))
    w_next(1)

    sums = ar_wait(ar_t, at_s, at_r)
    center, recip = norm_of(sums[0:1], sums[1:2])
    tst[f] = zero
    tst[f, 0:1, :] = center
    tst[f, 1:2, :] = recip
    f_start(tst, ts_s, ts_r)

    for s in range(2, nz // 2):
        w_next(s)
    ag_end(nz, z, w_slot, wz_s, wz_r)

    if len(comes[0]) > 1:
        t_come(0, 1)
        if ny > 2:
            ag_step_own = around(y - 1, ny)
            send(
                tb.at[0, ag_step_own, 0], tb.at[0, ag_step_own, 0],
                ty_s.at[0, 0, 1], ty_r.at[0, 0, 1], y_at(around(y + 1, ny)),
            )
        t_hand(0, 1)
    arrived(tb.at[1, y, 0], tx_s, tx_r, mate)
    t_next(0, (1,))
    t_hand(1, 0)

    arrived(xp, xc_s, xc_r, mate)
    wide = wb.shape[0] * wb.shape[1] * wb.shape[2] * wb.shape[3]
    tile = min(256, rows)
    tiles = rows // tile

    def project(ref, base):
        def body(i, carry):
            a, b = carry
            here = pl.multiple_of(i * tile, tile)
            v = jnp.dot(
                ref[pl.ds(here, tile), :], wb[...].reshape(wide, half), preferred_element_type=F32
            )
            pj[pl.ds(pl.multiple_of(base + i * tile, tile), tile), :] = v
            v = v.reshape(tile // 8, 8, half)
            return a + jnp.sum(v, axis=0), b + jnp.sum(v * v, axis=0)

        return body

    narrow = jnp.zeros((8, half), F32)
    carry = lax.fori_loop(0, tiles, project(x_ref, 0), (narrow, narrow))
    a, b = lax.fori_loop(0, tiles, project(xp, rows), carry)
    ar_p[chip] = zero
    ar_p[chip, 0:1, 0:half] = jnp.sum(a, axis=0, keepdims=True)
    ar_p[chip, 0:1, half:cols] = jnp.sum(b, axis=0, keepdims=True)
    ar_start(ar_p, ap_s, ap_r)

    f_wait(tst, ts_s, ts_r)
    t_normal(0, 0, wait_mate=False)
    if len(comes[0]) > 2:
        t_come(0, 2)
        t_hand(0, 2)
    for e in range(1, min(3, len(comes[0]))):
        t_normal(0, e)

    sums = ar_wait(ar_p, ap_s, ap_r)
    p_center, p_recip = norm_of(sums[0:1, 0:half], sums[0:1, half:cols])
    all_tiles = 2 * tiles
    for i in range(all_tiles):
        v = (pj[i * tile:(i + 1) * tile, :] - p_center) * p_recip
        pj[i * tile:(i + 1) * tile, :] = v
        sT[:, i * tile:(i + 1) * tile] = v.T.astype(BF16)

    span = (ny // 2) * cols

    def correlate(g):
        for h in (0, 1):

            @pl.loop(0, ny // 2)
            def _(j):
                v = jnp.dot(sT[...], tn[g, h * (ny // 2) + j], preferred_element_type=F32)
                cc[g, h, :, pl.ds(pl.multiple_of(j * cols, cols), cols)] = v

    piece = half // nz

    def c_local(g):
        def local(st, p):
            h = xl if st == 0 else 1 - xl
            return cc[g, h, pl.ds(pl.multiple_of(p * piece, piece), piece), :]

        return local

    def c_step(g, s):
        rs_step(s, nz, z, z_at, cb.at[g], c_local(g), cz_s.at[g], cz_r.at[g])

    def c_over(g):
        v = rs_total(1, nz, z, cb.at[g], c_local(g), cz_s.at[g], cz_r.at[g])
        xs[g] = v.astype(xs.dtype)
        send(xs.at[g], xr.at[g], cx_s.at[g], cx_r.at[g], x_mate)

    def slope(g):
        v = rs_total(0, nz, z, cb.at[g], c_local(g), cz_s.at[g], cz_r.at[g])
        arrived(xr.at[g], cx_s.at[g], cx_r.at[g], mate)
        share = (v + xr[g].astype(F32)) / total_rows
        student_index = f * cols + core * half + z * piece + lax.broadcasted_iota(jnp.int32, share.shape, 0)
        group = xh if g == 0 else 1 - xh
        teacher_index = (group * 2 + xl) * span + lax.broadcasted_iota(jnp.int32, share.shape, 1)
        on_diag = student_index == teacher_index
        part = jnp.where(on_diag, (1.0 - share) ** 2, OFF_WEIGHT * share * share)
        lacc[g] = jnp.sum(part.reshape(piece // 8, 8, span), axis=0)
        sl[g, xl, z] = jnp.where(on_diag, -2.0 * (1.0 - share), 2.0 * OFF_WEIGHT * share).astype(BF16)
        send(sl.at[g, xl, z], sl.at[g, xl, z], sx_s.at[g], sx_r.at[g], x_mate)

    def s_slot(g):
        return lambda st, p: sl.at[g, xl if st == 0 else 1 - xl, p]

    def s_step(g, s, streams=(0, 1)):
        ag_step(s, nz, z, z_at, s_slot(g), sz_s.at[g], sz_r.at[g], streams)

    def s_end(g):
        ag_end(nz, z, s_slot(g), sz_s.at[g], sz_r.at[g])

    def s_other(g):
        arrived(sl.at[g, 1 - xl, z], sx_s.at[g], sx_r.at[g], mate)
        s_step(g, 0, (1,))

    def upstream(g):
        @pl.loop(0, all_tiles)
        def _(i):
            here = pl.ds(pl.multiple_of(i * tile, tile), tile)
            v = None if g == 0 else uu[here, :]
            for j in range(ny):
                h, k = j // (ny // 2), j % (ny // 2)
                rhs = sl[g, h, :, :, k * cols:(k + 1) * cols].reshape(half, cols)
                w = lax.dot_general(
                    tn[g, j, here, :], rhs, (((1,), (1,)), ((), ())), preferred_element_type=F32
                )
                v = w if v is None else v + w
            uu[here, :] = v

    for e in range(3, len(comes[0])):
        t_come(0, e)
        t_hand(0, e)
        t_normal(0, e)
    correlate(0)
    c_step(0, 0)
    if len(comes[1]) > 2:
        t_come(1, 2)
        p1 = around(y + 1, ny)
        send(
            tb.at[1, p1, 0], tb.at[1, p1, 0], ty_s.at[1, 1, 1], ty_r.at[1, 1, 1],
            y_at(around(y - 1, ny)),
        )
        t_hand(1, 2)
    t_normal(1, 0)
    if len(comes[1]) > 1:
        t_come(1, 1)
        t_hand(1, 1)
    for s in range(1, nz // 2):
        c_step(0, s)
    for e in range(1, min(3, len(comes[1]))):
        t_normal(1, e)
    c_over(0)
    for e in range(3, len(comes[1])):
        t_come(1, e)
        t_hand(1, e)
        t_normal(1, e)
    correlate(1)
    c_step(1, 0)
    slope(0)
    s_step(0, 0, (0,))
    s_other(0)
    for s in range(1, nz // 2):
        c_step(1, s)
        s_step(0, s)
    c_over(1)
    s_end(0)
    upstream(0)
    slope(1)
    s_step(1, 0, (0,))
    s_other(1)
    for s in range(1, nz // 2):
        s_step(1, s)
    s_end(1)
    upstream(1)

    def u_sum(i, carry):
        a, b = carry
        here = pl.ds(pl.multiple_of(i * tile, tile), tile)
        v = uu[here, :] / total_rows
        uu[here, :] = v
        w = v * pj[here, :]
        return (
            a + jnp.sum(v.reshape(tile // 8, 8, half), axis=0),
            b + jnp.sum(w.reshape(tile // 8, 8, half), axis=0),
        )

    a, b = lax.fori_loop(0, all_tiles, u_sum, (narrow, narrow))
    ar_u[chip] = zero
    ar_u[chip, 0:1, 0:half] = jnp.sum(a, axis=0, keepdims=True)
    ar_u[chip, 0:1, half:cols] = jnp.sum(b, axis=0, keepdims=True)
    part = jnp.sum(lacc[0] + lacc[1], axis=0, keepdims=True)
    for k in range(span // cols):
        ar_u[chip, 1:2, :] += part[:, k * cols:(k + 1) * cols]
    ar_start(ar_u, au_s, au_r)
    sums = ar_wait(ar_u, au_s, au_r)
    mean_g = sums[0:1, 0:half] / total_rows
    mean_x = sums[0:1, half:cols] / total_rows
    for i in range(all_tiles):
        v = uu[i * tile:(i + 1) * tile, :]
        v = p_recip * (v - mean_g - pj[i * tile:(i + 1) * tile, :] * mean_x)
        sT[:, i * tile:(i + 1) * tile] = v.T.astype(BF16)

    strip = gg.shape[3]
    pairs = nz // 2
    for h in (0, 1):

        @pl.loop(0, pairs)
        def _(j):
            here = pl.ds(pl.multiple_of(h * nz * strip + j * 2 * strip, 2 * strip), 2 * strip)
            v = jnp.dot(sT[:, 0:rows], x_ref[:, here], preferred_element_type=F32)
            v = v + jnp.dot(sT[:, rows:2 * rows], xp[:, here], preferred_element_type=F32)
            gg[h, 2 * j] = v[:, 0:strip]
            gg[h, 2 * j + 1] = v[:, strip:2 * strip]

    def g_local(st, p):
        return gg[xl if st == 0 else 1 - xl, p]

    rs_step(0, nz, z, z_at, gb, g_local, gz_s, gz_r)

    v = sums[1:2, 0:128]
    for k in range(1, cols // 128):
        v = v + sums[1:2, k * 128:(k + 1) * 128]
    lf[f] = jnp.broadcast_to(v, (8, 128))
    f_start(lf, lf_s, lf_r)

    for s in range(1, nz // 2):
        rs_step(s, nz, z, z_at, gb, g_local, gz_s, gz_r)
    gxs[...] = rs_total(1, nz, z, gb, g_local, gz_s, gz_r).astype(gxs.dtype)
    send(gxs, gxr, gx_s, gx_r, x_mate)
    f_wait(lf, lf_s, lf_r)
    lc[0] = jnp.sum(lf[...], axis=0)
    send(lc.at[0], lc.at[1], lc_s, lc_r, mate)
    v = rs_total(0, nz, z, gb, g_local, gz_s, gz_r)
    arrived(gxr, gx_s, gx_r, mate)
    v = (LOSS_SCALE * (v + gxr[...].astype(F32))).T
    mine = strip // 2
    low, high = v[0:mine], v[mine:strip]
    first = core == 0
    gcs[...] = jnp.where(first, high, low)
    send(gcs, gcr, gc_s, gc_r, mate)
    g_ref[:, my_cols] = jnp.where(first, low, high)
    arrived(lc.at[1], lc_s, lc_r, mate)
    v = jnp.sum(lc[0] + lc[1], axis=1, keepdims=True) / width_all
    loss_ref[...] = jnp.broadcast_to(v, (8, 128))
    arrived(gcr, gc_s, gc_r, mate)
    g_ref[:, mate_cols] = gcr[...]

    for c in sent:
        c.wait_send()
    ar_sent(ar_t, at_s, at_r)
    ar_sent(ar_p, ap_s, ap_r)
    ar_sent(ar_u, au_s, au_r)
    f_sent(tst, ts_s, ts_r)
    f_sent(lf, lf_s, lf_r)


def shards(nz, ny, student, weight, teacher):
    rows, wide = student.shape
    strip_w, cols = weight.shape
    half = cols // 2
    span = (ny // 2) * cols
    chips, feats = 2 * nz, 2 * ny
    steps = nz // 2 + 1
    strip = wide // chips
    piece = half // nz
    V = pltpu.VMEM
    D = pltpu.SemaphoreType.DMA
    data = [
        V((2, ny, 2, rows, cols), BF16),
        V((2, ny, 2 * rows, cols), BF16),
        V((rows, wide), BF16),
        V((2, nz, 2, strip_w, half), BF16),
        V((2 * rows, half), F32),
        V((half, 2 * rows), BF16),
        V((2, 2, half, span), F32),
        V((2, 2, 2, steps, piece, span), BF16),
        V((2, piece, span), BF16),
        V((2, piece, span), BF16),
        V((2, 2, nz, piece, span), BF16),
        V((2 * rows, half), F32),
        V((2, nz, half, strip), F32),
        V((2, 2, steps, half, strip), F32),
        V((half, strip), F32),
        V((half, strip), F32),
        V((strip // 2, half), F32),
        V((strip // 2, half), F32),
        V((chips, 8, cols), F32),
        V((chips, 8, cols), F32),
        V((chips, 8, cols), F32),
        V((feats, 8, cols), F32),
        V((2, 8, span), F32),
        V((feats, 8, 128), F32),
        V((2, 8, 128), F32),
    ]
    sems = []
    for shape in (
        (2, ny), (), (2, 2, ny // 2), (), (), (), (2, 2, nz // 2),
        (2, 2, 2, nz // 2), (2,), (2,), (2, 2, 2, nz // 2), (2, 2, nz // 2), (), (),
        (chips - 1,), (chips - 1,), (chips - 1,), (feats - 1,), (feats - 1,), (),
    ):
        sems += [D(shape), D(shape)]
    vm = pl.BlockSpec(memory_space=pltpu.VMEM)
    loss, grad = pl.pallas_call(
        functools.partial(kernel, nz, ny),
        out_shape=(
            jax.ShapeDtypeStruct((8, 128), F32),
            jax.ShapeDtypeStruct((strip_w, cols), F32),
        ),
        in_specs=[vm] * 3,
        out_specs=(vm, vm),
        scratch_shapes=data + sems,
        compiler_params=pltpu.CompilerParams(
            collective_id=0, has_side_effects=True, vmem_limit_bytes=56 * 1024 * 1024
        ),
    )(student, weight, teacher)
    return loss[0, 0], grad


def solution(mesh):
    placed = (P("dp", None), P("dp", "feat"), P("dp", "feat"))
    nz, ny = mesh.shape["dp"] // 4, mesh.shape["feat"] // 2
    return jax.shard_map(
        functools.partial(shards, nz, ny), mesh=mesh, in_specs=placed,
        out_specs=(P(), P("dp", "feat")), check_vma=False,
    )
```

```python
import functools

import jax
import jax.numpy as jnp
from jax import lax
from jax.experimental import pallas as pl
from jax.experimental.pallas import tpu as pltpu
from jax.sharding import PartitionSpec as P

OFF_WEIGHT = 0.5
NORM_EPS = 1e-05
LOSS_SCALE = 128.0
F32 = jnp.float32
BF16 = jnp.bfloat16
MESH = pl.DeviceIdType.MESH


def arms(n):
    return ((n // 2, n // 2 - 1), (n // 2 - 1, n // 2))


def around(at, n):
    return lax.rem(at + n, n)


def kernel(
    nz, ny, x_hbm, w_hbm, t_hbm, loss_ref, g_ref,
    x_ref, tb, tn, rl, xp, wb, pj, sT, cc, ca, cb, xs, xr, bs, br, sl, uu, dT, gg, ga, gb, gxs, gxr, gbr, gcs, gcr,
    ar_t, ar_p, ar_u, tst, lacc, lf, lc,
    out_s, in_s, ar_s, ar_r, tc_r, tx_r, ty_r, xc_r, wc_r, wx_r, wz_r, wy_r,
    ca_r, cx_r, cb_r, bx_r, sx_r, sz_r, sb_r, sy_r, ga_r, gx_r, gb_r, gy_r, gc_r, lc_r,
):
    d = lax.axis_index("dp")
    f = lax.axis_index("feat")
    chips = 2 * nz
    feats = 2 * ny
    core = lax.rem(d, 2)
    chip = lax.div(d, 2)
    z = lax.rem(chip, nz)
    xl = lax.div(chip, nz)
    y = lax.rem(f, ny)
    xh = lax.div(f, ny)
    rows = x_ref.shape[0]
    cols = w_hbm.shape[1]
    half = cols // 2
    total_rows = float(rows * 2 * chips)
    width_all = cols * feats

    mate = (d + 1 - 2 * core, f)

    def dp_at(chip_at):
        return (chip_at * 2 + core, f)

    def z_at(at):
        return dp_at(xl * nz + at)

    def y_at(at):
        return (d, xh * ny + at)

    x_mate = dp_at((1 - xl) * nz + z)
    cross = ((1 - xl) * nz + z) * 2 + core
    x_diag = (cross, (1 - xh) * ny + y)
    x_next = (cross, jnp.where(xl == 0, xh, 1 - xh) * ny + y)
    x_prev = (cross, jnp.where(xl == 0, 1 - xh, xh) * ny + y)

    weigh = {}
    CHIP, WEIGHT, TEACH, CORR, GRAD = range(5)

    def copy(src, dst, s, r, to):
        return pltpu.make_async_remote_copy(
            src_ref=src, dst_ref=dst, send_sem=s, recv_sem=r, device_id=to, device_id_type=MESH
        )

    def send(kind, src, dst, r, to):
        copy(src, dst, out_s.at[kind], r, to).start()
        size = src.dtype.itemsize
        for n in src.shape:
            size *= n
        weigh[kind] = weigh.get(kind, 0) + size

    def arrived(dst, r):
        copy(dst, dst, out_s.at[0], r, mate).wait_recv()

    top = nz // 2

    def hop(k):
        return z_at(around(z + k, nz))

    def ag_go(kind, slot, rs):
        for k, r in ((2, 2), (-2, 3), (1, 0), (-1, 1)):
            send(kind, slot(z), slot(z), rs.at[r], hop(k))

    def ag_on(kind, slot, rs, far=None):
        for dr in (0, 1):
            sgn = 1 - 2 * dr
            block = slot(around(z - 2 * sgn, nz))
            arrived(block, rs.at[2 + dr])
            if far is None:
                side = block.shape[-1] // 2
                part = block.at[:, pl.ds(dr * side, side)]
                send(kind, part, part, rs.at[6 + dr], hop(2 * sgn))
            elif far == dr:
                send(kind, block, block, rs.at[6], hop(2 * sgn))
            send(kind, block, block, rs.at[4 + dr], hop(sgn))

    def ag_near(slot, rs):
        for dr in (0, 1):
            arrived(slot(around(z - 1 + 2 * dr, nz)), rs.at[dr])

    def ag_end(slot, rs, far=None):
        for dr in (0, 1):
            arrived(slot(around(z - 3 + 6 * dr, nz)), rs.at[4 + dr])
        block = slot(around(z + top, nz))
        if far is None:
            side = block.shape[-1] // 2
            for dr in (0, 1):
                arrived(block.at[:, pl.ds(dr * side, side)], rs.at[6 + dr])
        else:
            arrived(block, rs.at[6])

    def agx_to(kind, slot, rs, off):
        block = slot(around(z + off, nz))
        send(kind, block, block, rs.at[off + 3], x_mate)

    def agx_go(kind, slot, rs, xrs):
        ag_go(kind, slot, rs)
        agx_to(kind, slot, xrs, 0)

    def agx_on(kind, slot, rs, xrs):
        ag_on(kind, slot, rs)
        for off in (-2, 2):
            agx_to(kind, slot, xrs, off)
        ag_near(slot, rs)
        for off in (-1, 1):
            agx_to(kind, slot, xrs, off)

    def agx_end(kind, slot, rs, xrs):
        ag_end(slot, rs)
        for off in (-3, 3, top):
            agx_to(kind, slot, xrs, off)

    def agx_last(slot, xrs):
        for off in (0, -2, 2, -1, 1, -3, 3, top):
            arrived(slot(around(z + off, nz)), xrs.at[off + 3])

    def far_step(kind, buf, local, rs):
        for dr in (0, 1):
            buf[dr, 2, dr] = local(dr, around(z + top, nz)).astype(buf.dtype)
            send(kind, buf.at[dr, 2, dr], buf.at[dr, 3, dr], rs.at[dr, 1], hop(2 - 4 * dr))
        for dr in (0, 1):
            sgn = 1 - 2 * dr
            for st in (0, 1):
                buf[dr, 0, st] = local(st, around(z + 3 * sgn, nz)).astype(buf.dtype)
            send(kind, buf.at[dr, 0], buf.at[dr, 1], rs.at[dr, 0], hop(sgn))

    def mid_step(kind, buf, local, rs):
        for dr in (0, 1):
            sgn = 1 - 2 * dr
            arrived(buf.at[dr, 1], rs.at[dr, 0])
            arrived(buf.at[dr, 3, dr], rs.at[dr, 1])
            for st in (0, 1):
                v = local(st, around(z + 2 * sgn, nz)) + buf[dr, 1, st].astype(F32)
                if st == dr:
                    v = v + buf[dr, 3, dr].astype(F32)
                buf[dr, 4, st] = v.astype(buf.dtype)
            send(kind, buf.at[dr, 4], buf.at[dr, 5], rs.at[dr, 2], hop(2 * sgn))

    def near_step(kind, buf, local, rs):
        for dr in (0, 1):
            sgn = 1 - 2 * dr
            for st in (0, 1):
                buf[dr, 6, st] = local(st, around(z + sgn, nz)).astype(buf.dtype)
            send(kind, buf.at[dr, 6], buf.at[dr, 7], rs.at[dr, 3], hop(sgn))

    def sum_end(buf, rs):
        for dr in (0, 1):
            arrived(buf.at[dr, 7], rs.at[dr, 3])
            arrived(buf.at[dr, 5], rs.at[dr, 2])

    def sum_total(st, buf, local):
        v = local(st, z)
        for dr in (0, 1):
            v = v + buf[dr, 5, st].astype(F32) + buf[dr, 7, st].astype(F32)
        return v

    def rs_step(kind, s, buf, local, rs):
        for dr in (0, 1):
            sgn = 1 - 2 * dr
            p = around(z + sgn * (top - s), nz)
            if s == 1:
                arrived(buf.at[dr, s, dr], rs.at[dr, s - 1])
            elif s > 1:
                arrived(buf.at[dr, s], rs.at[dr, s - 1])
            for st in (dr,) if s == 0 else (0, 1):
                v = local(st, p)
                if s > 1 or (s == 1 and st == dr):
                    v = v + buf[dr, s, st].astype(F32)
                buf[dr, s, st] = v.astype(buf.dtype)
            to = z_at(around(z + sgn, nz))
            if s == 0:
                send(kind, buf.at[dr, 0, dr], buf.at[dr, 1, dr], rs.at[dr, 0], to)
            else:
                send(kind, buf.at[dr, s], buf.at[dr, s + 1], rs.at[dr, s], to)

    def rs_end(buf, rs):
        for dr in (0, 1):
            arrived(buf.at[dr, top], rs.at[dr, top - 1])

    def rs_total(st, buf, local):
        return local(st, z) + buf[0, top, st].astype(F32) + buf[1, top, st].astype(F32)

    need = [top, 3, -3, 2, -2, 1, -1, 0]

    def need_at(k):
        return around(z + need[k], nz)

    def x_wait(ks, dst, rs):
        for k in ks:
            arrived(dst.at[need_at(k)], rs.at[k])

    def ar_copy(buf, i, k):
        return copy(buf.at[chip], buf.at[chip], ar_s.at[i], ar_r.at[i], dp_at(around(chip + k, chips)))

    def ar_start(buf, i):
        @pl.loop(1, chips)
        def _(k):
            ar_copy(buf, i, k).start()

    def ar_wait(buf, i):
        arrived(buf.at[pl.ds(0, chips - 1)], ar_r.at[i])
        return jnp.sum(buf[...], axis=0)

    def ar_sent(buf, i, n):
        there = buf.at[pl.ds(0, n - 1)]
        copy(there, there, ar_s.at[i], ar_r.at[i], mate).wait_send()

    def f_start(buf, i):
        @pl.loop(1, feats)
        def _(k):
            copy(buf.at[f], buf.at[f], ar_s.at[i], ar_r.at[i], (d, around(f + k, feats))).start()

    def f_wait(buf, i):
        arrived(buf.at[pl.ds(0, feats - 1)], ar_r.at[i])

    lanes = cols // 128

    def pack(buf, at, row, v):
        for k in range(v.shape[1] // 128):
            buf[at, row + k:row + k + 1, :] = v[:, k * 128:(k + 1) * 128]

    def spread_out(v, row, n):
        return jnp.concatenate([v[row + k:row + k + 1, :] for k in range(n // 128)], axis=1)

    def norm_of(sums, squares):
        center = sums / total_rows
        spread = squares / total_rows - center * center
        return center, lax.rsqrt(spread + NORM_EPS)

    barrier = pltpu.get_barrier_semaphore()

    def greet(to):
        pl.semaphore_signal(barrier, inc=1, device_id=to, device_id_type=MESH)

    greet(mate)
    greet(x_diag)

    @pl.loop(1, feats)
    def _(k):
        greet((d, around(f + k, feats)))

    @pl.loop(1, chips)
    def _(k):
        greet(dp_at(around(chip + k, chips)))

    my_cols = pl.ds(pl.multiple_of(core * half, half), half)
    mate_cols = pl.ds(pl.multiple_of((1 - core) * half, half), half)
    w_in = pltpu.make_async_copy(w_hbm.at[:, my_cols], wb.at[xl, z, core], in_s.at[0])
    t_in = pltpu.make_async_copy(t_hbm, tb.at[0, y, 0], in_s.at[1])
    x_in = pltpu.make_async_copy(x_hbm, x_ref, in_s.at[2])
    w_in.start()
    t_in.start()
    x_in.start()
    pl.semaphore_wait(barrier, feats + chips)

    send(WEIGHT, w_hbm.at[:, mate_cols], wb.at[xl, z, core], wc_r, mate)
    send(TEACH, t_hbm, tb.at[0, y, 1], tc_r.at[0, 0], mate)

    mid = rows // 2
    right, left = y_at(around(y + 1, ny)), y_at(around(y - 1, ny))
    offs = (0, -1, 1, 2)

    def t_at(st, e):
        return tb.at[st, around(y + offs[e], ny), 0]

    def t_hand(st, e):
        send(TEACH, t_at(st, e), tb.at[st, around(y + offs[e], ny), 1], tc_r.at[st, e], mate)

    def t_round(st, src):
        send(TEACH, src, t_at(st, 0), ty_r.at[st, 0, 0], right)
        send(TEACH, src, t_at(st, 0), ty_r.at[st, 1, 0], left)

    def t_pass(st):
        arrived(t_at(st, 1), ty_r.at[st, 0, 0])
        high = t_at(st, 1).at[pl.ds(0, mid)]
        send(TEACH, high, high, ty_r.at[st, 0, 1], right)
        arrived(t_at(st, 2), ty_r.at[st, 1, 0])
        low = t_at(st, 2).at[pl.ds(mid, mid)]
        send(TEACH, low, low, ty_r.at[st, 1, 1], left)
        t_hand(st, 1)
        t_hand(st, 2)

    def t_far(st):
        arrived(t_at(st, 3).at[pl.ds(0, mid)], ty_r.at[st, 0, 1])
        arrived(t_at(st, 3).at[pl.ds(mid, mid)], ty_r.at[st, 1, 1])
        t_hand(st, 3)

    quad = rows // 4
    ways = (x_next, x_prev)

    def t_cross(i):
        for dr in (0, 1):
            part = t_hbm.at[pl.ds((2 * dr + i) * quad, quad)]
            send(TEACH, part, rl.at[dr, i], tx_r.at[dr, i], ways[dr])

    def t_relay(i):
        for dr in (0, 1):
            arrived(rl.at[dr, i], tx_r.at[dr, i])
            there = t_at(1, 0).at[pl.ds((2 * dr + i) * quad, quad)]
            send(TEACH, rl.at[dr, i], there, tx_r.at[dr, 2 + i], ways[dr])

    def t_over():
        for i in (0, 1):
            for dr in (0, 1):
                arrived(t_at(1, 0).at[pl.ds((2 * dr + i) * quad, quad)], tx_r.at[dr, 2 + i])
        t_round(1, t_at(1, 0))
        t_hand(1, 0)

    t_round(0, t_hbm)
    send(CHIP, x_hbm, xp, xc_r, mate)

    def t_normal(st, e, wait_mate=True):
        p = around(y + offs[e], ny)
        if wait_mate:
            arrived(tb.at[st, p, 1], tc_r.at[st, e])
        at = (xh if st == 0 else 1 - xh) * ny + p
        center = spread_out(tst[at], 0, cols)
        recip = spread_out(tst[at], lanes, cols)
        for slot in (0, 1):

            @pl.loop(0, rows // 64)
            def _(i):
                here = pl.multiple_of(i * 64, 64)
                v = tb[st, p, slot, pl.ds(here, 64), :].astype(F32)
                there = pl.multiple_of(slot * rows + i * 64, 64)
                tn[st, p, pl.ds(there, 64), :] = ((v - center) * recip).astype(BF16)

    def w_own(p):
        return wb.at[xl, p, 0]

    def w_other(p):
        return wb.at[1 - xl, p, 0]

    def w_late(p):
        return wb.at[xl, p, 1]

    def w_last(p):
        return wb.at[1 - xl, p, 1]

    w_in.wait()
    arrived(wb.at[xl, z, 1 - core], wc_r)
    send(WEIGHT, w_own(z), w_own(z), wx_r, x_mate)
    ag_go(WEIGHT, w_own, wz_r.at[0])
    agx_go(WEIGHT, w_late, wz_r.at[2], wy_r)

    t_in.wait()
    arrived(tb.at[0, y, 1], tc_r.at[0, 0])

    def t_sum(i, carry):
        a, b = carry
        for slot in (0, 1):
            v = tb[0, y, slot, pl.ds(pl.multiple_of(i * 64, 64), 64), :].astype(F32).reshape(8, 8, cols)
            a = a + jnp.sum(v, axis=0)
            b = b + jnp.sum(v * v, axis=0)
        return a, b

    zero = jnp.zeros((8, cols), F32)
    a, b = lax.fori_loop(0, rows // 64, t_sum, (zero, zero))
    pack(ar_t, chip, 0, jnp.sum(a, axis=0, keepdims=True))
    pack(ar_t, chip, lanes, jnp.sum(b, axis=0, keepdims=True))
    ar_start(ar_t, 0)
    t_cross(0)

    arrived(w_other(z), wx_r)
    ag_go(WEIGHT, w_other, wz_r.at[1])
    ag_on(WEIGHT, w_own, wz_r.at[0], 0)
    agx_on(WEIGHT, w_late, wz_r.at[2], wy_r)
    t_cross(1)
    sums = ar_wait(ar_t, 0)
    center, recip = norm_of(sums[0:lanes], sums[lanes:2 * lanes])
    tst[f, 0:lanes, :] = center
    tst[f, lanes:2 * lanes, :] = recip
    f_start(tst, 4)

    t_relay(0)
    ag_on(WEIGHT, w_other, wz_r.at[1], 1)
    agx_end(WEIGHT, w_late, wz_r.at[2], wy_r)
    t_relay(1)
    t_pass(0)
    ag_near(w_own, wz_r.at[0])
    ag_end(w_own, wz_r.at[0], 0)
    ag_near(w_other, wz_r.at[1])
    ag_end(w_other, wz_r.at[1], 1)
    agx_last(w_last, wy_r)

    x_in.wait()
    arrived(xp, xc_r)
    wide = wb.shape[0] * wb.shape[1] * wb.shape[2] * wb.shape[3]
    tile = min(256, rows)
    tiles = rows // tile

    def project(ref, base):
        def body(i, carry):
            a, b = carry
            here = pl.multiple_of(i * tile, tile)
            v = jnp.dot(
                ref[pl.ds(here, tile), :], wb[...].reshape(wide, half), preferred_element_type=F32
            )
            pj[pl.ds(pl.multiple_of(base + i * tile, tile), tile), :] = v
            v = v.reshape(tile // 8, 8, half)
            return a + jnp.sum(v, axis=0), b + jnp.sum(v * v, axis=0)

        return body

    narrow = jnp.zeros((8, half), F32)
    carry = lax.fori_loop(0, tiles, project(x_ref, 0), (narrow, narrow))
    a, b = lax.fori_loop(0, tiles, project(xp, rows), carry)
    ar_p[chip] = jnp.zeros((8, 128), F32)
    pack(ar_p, chip, 0, jnp.sum(a, axis=0, keepdims=True))
    pack(ar_p, chip, lanes // 2, jnp.sum(b, axis=0, keepdims=True))
    ar_start(ar_p, 1)
    t_far(0)
    t_over()

    f_wait(tst, 4)
    t_normal(0, 0, wait_mate=False)
    t_normal(0, 1)
    t_normal(0, 2)

    sums = ar_wait(ar_p, 1)
    p_center, p_recip = norm_of(spread_out(sums, 0, half), spread_out(sums, lanes // 2, half))
    all_tiles = 2 * tiles
    for i in range(all_tiles):
        v = (pj[i * tile:(i + 1) * tile, :] - p_center) * p_recip
        pj[i * tile:(i + 1) * tile, :] = v
        sT[:, i * tile:(i + 1) * tile] = v.T.astype(BF16)

    span = (ny // 2) * cols

    def correlate(g):
        for h in (0, 1):

            @pl.loop(0, ny // 2)
            def _(j):
                v = jnp.dot(sT[...], tn[g, h * (ny // 2) + j], preferred_element_type=F32)
                cc[g, h, :, pl.ds(pl.multiple_of(j * cols, cols), cols)] = v

    quarter = half // 2
    piece = quarter // nz

    def rows_of(a, p):
        return pl.ds(pl.multiple_of(a * quarter + p * piece, piece), piece)

    side = span // 2

    def sides(st):
        return slice(st * side, (st + 1) * side)

    def ca_local(g):
        return lambda st, p: cc[g, xl if st == 0 else 1 - xl, rows_of(0, p), :]

    def ca_far(g):
        far_step(CORR, ca.at[g], ca_local(g), ca_r.at[g])

    def ca_mid(g):
        mid_step(CORR, ca.at[g], ca_local(g), ca_r.at[g])

    def ca_near(g):
        near_step(CORR, ca.at[g], ca_local(g), ca_r.at[g])

    def ca_over(g):
        sum_end(ca.at[g], ca_r.at[g])
        xs[g] = sum_total(1, ca.at[g], ca_local(g)).astype(xs.dtype)
        send(CORR, xs.at[g], xr.at[g], cx_r.at[g], x_mate)

    def cb_over(a, g):
        bs[g, a] = cc[g, 1 - xl, a * quarter:(a + 1) * quarter, :].astype(BF16).reshape(nz, piece, span)
        for k in range(nz):
            send(CORR, bs.at[g, a, need_at(k)], br.at[g, a, need_at(k)], bx_r.at[g, a, k], x_mate)

    def cb_local(a, g):
        return lambda st, p: cc[g, xl, rows_of(a, p), sides(st)] + br[g, a, p, :, sides(st)].astype(F32)

    def cb_far(a, g):
        x_wait((0, 1, 2), br.at[g, a], bx_r.at[g, a])
        far_step(CORR, cb.at[g, a], cb_local(a, g), cb_r.at[g, a])

    def cb_mid(a, g):
        x_wait((3, 4), br.at[g, a], bx_r.at[g, a])
        mid_step(CORR, cb.at[g, a], cb_local(a, g), cb_r.at[g, a])

    def cb_near(a, g):
        x_wait((5, 6), br.at[g, a], bx_r.at[g, a])
        near_step(CORR, cb.at[g, a], cb_local(a, g), cb_r.at[g, a])

    def slope(a, g):
        if (a, g) == (0, 1):
            v = sum_total(0, ca.at[g], ca_local(g))
            arrived(xr.at[g], cx_r.at[g])
            v = v + xr[g].astype(F32)
        else:
            sum_end(cb.at[g, a], cb_r.at[g, a])
            x_wait((7,), br.at[g, a], bx_r.at[g, a])
            v = jnp.concatenate([sum_total(st, cb.at[g, a], cb_local(a, g)) for st in (0, 1)], axis=1)
        share = v / total_rows
        student_index = (
            f * cols + core * half + a * quarter + z * piece
            + lax.broadcasted_iota(jnp.int32, share.shape, 0)
        )
        group = xh if g == 0 else 1 - xh
        teacher_index = (group * 2 + xl) * span + lax.broadcasted_iota(jnp.int32, share.shape, 1)
        on_diag = student_index == teacher_index
        part = jnp.where(on_diag, (1.0 - share) ** 2, OFF_WEIGHT * share * share)
        lacc[g, a] = jnp.sum(part.reshape(piece // 8, 8, span), axis=0)
        sl[g, xl, a, z] = jnp.where(on_diag, -2.0 * (1.0 - share), 2.0 * OFF_WEIGHT * share).astype(BF16)
        if (a, g) == (0, 1):
            there = sl.at[g, xl, 0, z]
            send(CORR, there, there, sx_r.at[g], x_mate)
            ag_go(CORR, sa_own(g), sz_r.at[g, 0])
        else:
            agx_go(CORR, sb_own(a, g), sb_r.at[g, a], sy_r.at[g, a])

    def sa_own(g):
        return lambda p: sl.at[g, xl, 0, p]

    def sa_mate(g):
        return lambda p: sl.at[g, 1 - xl, 0, p]

    def sb_own(a, g):
        return lambda p: sl.at[g, xl, a, p]

    def sb_mate(a, g):
        return lambda p: sl.at[g, 1 - xl, a, p]

    def sa_other(g):
        arrived(sl.at[g, 1 - xl, 0, z], sx_r.at[g])
        ag_go(CORR, sa_mate(g), sz_r.at[g, 1])

    def sa_on(g):
        ag_on(CORR, sa_own(g), sz_r.at[g, 0], 0)

    def sa_on_other(g):
        ag_on(CORR, sa_mate(g), sz_r.at[g, 1], 1)

    def sa_end(g):
        for st, slot in ((0, sa_own(g)), (1, sa_mate(g))):
            ag_near(slot, sz_r.at[g, st])
            ag_end(slot, sz_r.at[g, st], st)

    def sb_on(a, g):
        agx_on(CORR, sb_own(a, g), sb_r.at[g, a], sy_r.at[g, a])

    def sb_end(a, g):
        agx_end(CORR, sb_own(a, g), sb_r.at[g, a], sy_r.at[g, a])

    def sb_last(a, g):
        agx_last(sb_mate(a, g), sy_r.at[g, a])

    def row_tile(i):
        return pl.ds(pl.multiple_of(i * tile, tile), tile)

    def times_slope(v, g, here, a=None):
        for j in range(ny):
            h, k = j // (ny // 2), j % (ny // 2)
            cut = slice(k * cols, (k + 1) * cols)
            rhs = sl[g, h, :, :, :, cut] if a is None else sl[g, h, a, :, :, cut]
            w = lax.dot_general(
                tn[g, j, here, :], rhs.reshape(half if a is None else quarter, cols),
                (((1,), (1,)), ((), ())), preferred_element_type=F32,
            )
            v = w if v is None else v + w
        return v

    def upstream_first():
        @pl.loop(0, all_tiles)
        def _(i):
            v = times_slope(None, 0, row_tile(i))
            uu[0, row_tile(i), :] = v[:, 0:quarter]
            uu[1, row_tile(i), :] = v[:, quarter:half]

    def upstream_last(a):
        cut = slice(a * quarter, (a + 1) * quarter)

        def body(i, carry):
            here = row_tile(i)
            v = times_slope(uu[a, here, :], 1, here, a) / total_rows
            uu[a, here, :] = v
            w = v * pj[here, cut]
            fold = (tile // 8, 8, quarter)
            return carry[0] + jnp.sum(v.reshape(fold), axis=0), carry[1] + jnp.sum(w.reshape(fold), axis=0)

        none = jnp.zeros((8, quarter), F32)
        b, c = lax.fori_loop(0, all_tiles, body, (none, none))
        ar_u[a, chip] = jnp.zeros((8, 128), F32)
        pack(ar_u.at[a], chip, 0, jnp.sum(b, axis=0, keepdims=True))
        pack(ar_u.at[a], chip, lanes // 4, jnp.sum(c, axis=0, keepdims=True))
        if a == 1:
            part = jnp.sum(lacc[0, 0] + lacc[0, 1] + lacc[1, 0] + lacc[1, 1], axis=0, keepdims=True)
            part = sum(part[:, k * cols:(k + 1) * cols] for k in range(span // cols))
            pack(ar_u.at[a], chip, lanes, part)
        ar_start(ar_u.at[a], 2 + a)

    strip = gg.shape[4]
    pairs = nz // 2

    def gradient(a):
        cut = slice(a * quarter, (a + 1) * quarter)
        sums = ar_wait(ar_u.at[a], 2 + a)
        mean_g = spread_out(sums, 0, quarter) / total_rows
        mean_x = spread_out(sums, lanes // 4, quarter) / total_rows
        for i in range(all_tiles):
            here = slice(i * tile, (i + 1) * tile)
            v = p_recip[:, cut] * (uu[a, here, :] - mean_g - pj[here, cut] * mean_x)
            dT[a, :, here] = v.T.astype(BF16)
        for h in (0, 1):

            @pl.loop(0, pairs)
            def _(j):
                here = pl.ds(pl.multiple_of(h * nz * strip + j * 2 * strip, 2 * strip), 2 * strip)
                v = jnp.dot(dT[a, :, 0:rows], x_ref[:, here], preferred_element_type=F32)
                v = v + jnp.dot(dT[a, :, rows:2 * rows], xp[:, here], preferred_element_type=F32)
                gg[a, h, 2 * j] = v[:, 0:strip]
                gg[a, h, 2 * j + 1] = v[:, strip:2 * strip]

        return sums

    band = quarter // 2

    def ga_local(i):
        return lambda st, p: gg[0, xl if st == 0 else 1 - xl, p, i * band:(i + 1) * band, :]

    def ga_step(s):
        for i in (0, 1):
            rs_step(GRAD, s, ga.at[i], ga_local(i), ga_r.at[i])

    def ga_over():
        for i in (0, 1):
            rs_end(ga.at[i], ga_r.at[i])
            gxs[i] = rs_total(1, ga.at[i], ga_local(i))
            send(GRAD, gxs.at[i], gxr.at[i], gx_r.at[i], x_mate)

    def gb_over():
        for k in range(nz):
            send(GRAD, gg.at[1, 1 - xl, need_at(k)], gbr.at[need_at(k)], gy_r.at[k], x_mate)

    def gb_local(st, p):
        part = slice(st * band, (st + 1) * band)
        return gg[1, xl, p, part, :] + gbr[p, part, :]

    def gb_far():
        x_wait((0, 1, 2), gbr, gy_r)
        far_step(GRAD, gb, gb_local, gb_r)

    def gb_mid():
        x_wait((3, 4), gbr, gy_r)
        mid_step(GRAD, gb, gb_local, gb_r)

    def gb_near():
        x_wait((5, 6), gbr, gy_r)
        near_step(GRAD, gb, gb_local, gb_r)

    mine = strip // 2
    first = core == 0

    def g_core(a):
        if a == 0:
            parts = []
            for i in (0, 1):
                v = rs_total(0, ga.at[i], ga_local(i))
                arrived(gxr.at[i], gx_r.at[i])
                parts.append(v + gxr[i])
            v = jnp.concatenate(parts, axis=0)
        else:
            sum_end(gb, gb_r)
            x_wait((7,), gbr, gy_r)
            v = jnp.concatenate([sum_total(st, gb, gb_local) for st in (0, 1)], axis=0)
        v = (LOSS_SCALE * v).T
        low, high = v[0:mine], v[mine:strip]
        gcs[a] = jnp.where(first, high, low)
        send(GRAD, gcs.at[a], gcr.at[a], gc_r.at[a], mate)
        g_ref[:, pl.ds(pl.multiple_of(core * half + a * quarter, quarter), quarter)] = jnp.where(first, low, high)

    def g_last(a):
        arrived(gcr.at[a], gc_r.at[a])
        g_ref[:, pl.ds(pl.multiple_of((1 - core) * half + a * quarter, quarter), quarter)] = gcr[a]

    t_normal(0, 3)
    correlate(0)
    cb_over(0, 0)
    cb_over(1, 0)
    t_normal(1, 0)
    cb_far(0, 0)
    t_pass(1)
    cb_far(1, 0)
    cb_mid(0, 0)
    cb_near(0, 0)
    t_normal(1, 1)
    t_normal(1, 2)
    cb_mid(1, 0)
    cb_near(1, 0)
    t_far(1)
    slope(0, 0)
    t_normal(1, 3)
    correlate(1)
    ca_far(1)
    cb_over(1, 1)
    ca_near(1)
    slope(1, 0)
    sb_on(0, 0)
    ca_mid(1)
    cb_far(1, 1)
    sb_on(1, 0)
    sb_end(0, 0)
    cb_mid(1, 1)
    cb_near(1, 1)
    ca_over(1)
    sb_end(1, 0)
    slope(0, 1)
    slope(1, 1)
    sb_last(0, 0)
    sb_last(1, 0)
    upstream_first()
    sa_other(1)
    sa_on(1)
    sb_on(1, 1)
    sa_on_other(1)
    sb_end(1, 1)
    sa_end(1)
    upstream_last(0)
    sb_last(1, 1)
    upstream_last(1)
    gradient(0)
    ga_step(0)
    sums = gradient(1)
    gb_over()
    ga_step(1)
    gb_far()
    lf[f] = jnp.broadcast_to(jnp.sum(sums[lanes:2 * lanes], axis=0, keepdims=True), (8, 128))
    f_start(lf, 5)
    ga_step(2)
    gb_mid()
    gb_near()
    ga_step(3)
    f_wait(lf, 5)
    lc[0] = jnp.sum(lf[...], axis=0)
    copy(lc.at[0], lc.at[1], ar_s.at[6], lc_r, mate).start()
    ga_over()
    g_core(1)
    g_core(0)
    arrived(lc.at[1], lc_r)
    loss_ref[0, 0] = jnp.sum((lc[0] + lc[1])[0:1]) / width_all
    g_last(1)
    g_last(0)
    ar_sent(ar_t, 0, chips)
    ar_sent(ar_p, 1, chips)
    ar_sent(ar_u.at[0], 2, chips)
    ar_sent(ar_u.at[1], 3, chips)
    ar_sent(tst, 4, feats)
    ar_sent(lf, 5, feats)
    copy(lc.at[0], lc.at[1], ar_s.at[6], lc_r, mate).wait_send()
    for kind, size in weigh.items():
        there = {WEIGHT: pj, TEACH: tn, CORR: cc}.get(kind, cc.at[0])
        line = there.dtype.itemsize
        for n in there.shape[:-2] + there.shape[-1:]:
            line *= n
        assert size % line == 0 and size // line % 8 == 0
        there = there.at[(slice(None),) * (len(there.shape) - 2) + (pl.ds(0, size // line),)]
        copy(there, there, out_s.at[kind], lc_r, mate).wait_send()


def shards(nz, ny, student, weight, teacher):
    rows, wide = student.shape
    strip_w, cols = weight.shape
    half = cols // 2
    span = (ny // 2) * cols
    chips, feats = 2 * nz, 2 * ny
    steps = nz // 2 + 1
    top = nz // 2
    strip = wide // chips
    quarter = half // 2
    piece = quarter // nz
    V = pltpu.VMEM
    D = pltpu.SemaphoreType.DMA
    data = [
        V((rows, wide), BF16),
        V((2, ny, 2, rows, cols), BF16),
        V((2, ny, 2 * rows, cols), BF16),
        V((2, 2, rows // 4, cols), BF16),
        V((rows, wide), BF16),
        V((2, nz, 2, strip_w, half), BF16),
        V((2 * rows, half), F32),
        V((half, 2 * rows), BF16),
        V((2, 2, half, span), F32),
        V((2, 2, 8, 2, piece, span), BF16),
        V((2, 2, 2, 8, 2, piece, span // 2), BF16),
        V((2, piece, span), BF16),
        V((2, piece, span), BF16),
        V((2, 2, nz, piece, span), BF16),
        V((2, 2, nz, piece, span), BF16),
        V((2, 2, 2, nz, piece, span), BF16),
        V((2, 2 * rows, quarter), F32),
        V((2, quarter, 2 * rows), BF16),
        V((2, 2, nz, quarter, strip), F32),
        V((2, 2, steps, 2, quarter // 2, strip), F32),
        V((2, 8, 2, quarter // 2, strip), F32),
        V((2, quarter // 2, strip), F32),
        V((2, quarter // 2, strip), F32),
        V((nz, quarter, strip), F32),
        V((2, strip // 2, quarter), F32),
        V((2, strip // 2, quarter), F32),
        V((chips, 8, 128), F32),
        V((chips, 8, 128), F32),
        V((2, chips, 8, 128), F32),
        V((feats, 8, 128), F32),
        V((2, 2, 8, span), F32),
        V((feats, 8, 128), F32),
        V((2, 8, 128), F32),
    ]
    sems = [
        D(shape) for shape in (
            (5,), (3,), (7,), (6,),
            (2, ny), (2, 4), (2, 2, 2), (), (), (), (3, nz), (nz,),
            (2, 2, 4), (2,), (2, 2, 2, 4), (2, 2, nz),
            (2,), (2, 2, 7), (2, 2, nz), (2, 2, nz),
            (2, 2, top), (2,), (2, 4), (nz,), (2,), (),
        )
    ]
    vm = pl.BlockSpec(memory_space=pltpu.VMEM)
    sm = pl.BlockSpec(memory_space=pltpu.SMEM)
    far = pl.BlockSpec(memory_space=pl.ANY)
    loss, grad = pl.pallas_call(
        functools.partial(kernel, nz, ny),
        out_shape=(
            jax.ShapeDtypeStruct((1, 1), F32),
            jax.ShapeDtypeStruct((strip_w, cols), F32),
        ),
        in_specs=[far] * 3,
        out_specs=(sm, vm),
        scratch_shapes=data + sems,
        compiler_params=pltpu.CompilerParams(
            collective_id=0, has_side_effects=True, vmem_limit_bytes=56 * 1024 * 1024
        ),
    )(student, weight, teacher)
    return loss.reshape(()), grad


def solution(mesh):
    placed = (P("dp", None), P("dp", "feat"), P("dp", "feat"))
    nz, ny = mesh.shape["dp"] // 4, mesh.shape["feat"] // 2
    return jax.shard_map(
        functools.partial(shards, nz, ny), mesh=mesh, in_specs=placed,
        out_specs=(P(), P("dp", "feat")), check_vma=False,
    )
```

```python
import functools

import jax
import jax.numpy as jnp
from jax import lax
from jax.experimental import pallas as pl
from jax.experimental.pallas import tpu as pltpu
from jax.sharding import PartitionSpec as P

OFF_WEIGHT = 0.5
NORM_EPS = 1e-05
LOSS_SCALE = 128.0
F32 = jnp.float32
BF16 = jnp.bfloat16
MESH = pl.DeviceIdType.MESH


def around(at, n):
    return lax.rem(at + n, n)


def kernel(
    nz, ny, x_hbm, w_hbm, t_hbm, loss_ref, g_ref,
    x_ref, tb, tn, rl, xp, wb, pj, sT, cc, ca, cb, xs, xr, bs, br, sl, uu, gg, gs, gr, ga, gb, gxs, gxr, gcs, gcr,
    ar_t, ar_p, ar_u, ar_n, tst, nst, rowsum, lacc, lf, lc,
    out_s, in_s, ar_s, ar_r, tc_r, tx_r, to_r, ty_r, xc_r, wc_r, wx_r, wz_r, wy_r,
    ca_r, cx_r, cb_r, bx_r, sx_r, sz_r, sb_r, sy_r, ga_r, gx_r, gy_r, gb_r, gc_r, lc_r,
):
    d = lax.axis_index("dp")
    f = lax.axis_index("feat")
    chips = 2 * nz
    feats = 2 * ny
    core = lax.rem(d, 2)
    chip = lax.div(d, 2)
    z = lax.rem(chip, nz)
    xl = lax.div(chip, nz)
    y = lax.rem(f, ny)
    xh = lax.div(f, ny)
    rows = x_ref.shape[0]
    cols = w_hbm.shape[1]
    half = cols // 2
    total_rows = float(rows * 2 * chips)
    width_all = cols * feats

    mate = (d + 1 - 2 * core, f)

    def dp_at(chip_at):
        return (chip_at * 2 + core, f)

    def z_at(at):
        return dp_at(xl * nz + at)

    def y_at(at):
        return (d, xh * ny + at)

    x_mate = dp_at((1 - xl) * nz + z)
    cross = ((1 - xl) * nz + z) * 2 + core
    x_diag = (cross, (1 - xh) * ny + y)
    x_next = (cross, jnp.where(xl == 0, xh, 1 - xh) * ny + y)
    x_prev = (cross, jnp.where(xl == 0, 1 - xh, xh) * ny + y)

    weigh = {}
    CHIP, WEIGHT, TEACH, CROSS, CORR, GRAD = range(6)

    def copy(src, dst, s, r, to):
        return pltpu.make_async_remote_copy(
            src_ref=src, dst_ref=dst, send_sem=s, recv_sem=r, device_id=to, device_id_type=MESH
        )

    def send(kind, src, dst, r, to):
        copy(src, dst, out_s.at[kind], r, to).start()
        size = src.dtype.itemsize
        for n in src.shape:
            size *= n
        weigh[kind] = weigh.get(kind, 0) + size

    def arrived(dst, r):
        copy(dst, dst, out_s.at[0], r, mate).wait_recv()

    top = nz // 2

    def hop(k):
        return z_at(around(z + k, nz))

    def arrived_all(ref, n, r):
        arrived(ref.at[pl.ds(0, n)], r)

    def ag_go(kind, slot, rs):
        for k, r in ((2, 2), (-2, 3), (1, 0), (-1, 0)):
            send(kind, slot(z), slot(z), rs.at[r], hop(k))

    def ag_on(kind, slot, rs, far=None):
        for dr in (0, 1):
            sgn = 1 - 2 * dr
            block = slot(around(z - 2 * sgn, nz))
            arrived(block, rs.at[2 + dr])
            if far is None:
                side = block.shape[-1] // 2
                part = block.at[:, pl.ds(dr * side, side)]
                send(kind, part, part, rs.at[1], hop(2 * sgn))
            elif far == dr:
                send(kind, block, block, rs.at[1], hop(2 * sgn))
            send(kind, block, block, rs.at[1], hop(sgn))

    def ag_end(like, rs):
        arrived_all(like, 2, rs.at[0])
        arrived_all(like, 3, rs.at[1])

    def agx_to(kind, slot, xr, offs):
        for off in offs:
            block = slot(around(z + off, nz))
            send(kind, block, block, xr, x_mate)

    def agx_go(kind, slot, rs, xr):
        ag_go(kind, slot, rs)
        agx_to(kind, slot, xr, (0,))

    def agx_on(kind, slot, rs, xr, like):
        ag_on(kind, slot, rs)
        agx_to(kind, slot, xr, (-2, 2))
        arrived_all(like, 2, rs.at[0])
        agx_to(kind, slot, xr, (-1, 1))

    def agx_end(kind, slot, rs, xr, like):
        arrived_all(like, 3, rs.at[1])
        agx_to(kind, slot, xr, (-3, 3, top))

    def far_step(kind, buf, local, rs):
        for dr in (0, 1):
            buf[dr, 2, 0] = local(dr, around(z + top, nz)).astype(buf.dtype)
            send(kind, buf.at[dr, 2, 0], buf.at[dr, 1, 0], rs.at[dr], hop(2 - 4 * dr))
        for dr in (0, 1):
            sgn = 1 - 2 * dr
            for st in (0, 1):
                buf[dr, 0, st] = local(st, around(z + 3 * sgn, nz)).astype(buf.dtype)
            send(kind, buf.at[dr, 0, pl.ds(0, 2)], buf.at[dr, 1, pl.ds(1, 2)], rs.at[dr], hop(sgn))

    def mid_step(kind, buf, local, rs):
        for dr in (0, 1):
            sgn = 1 - 2 * dr
            arrived(buf.at[dr, 1], rs.at[dr])
            for st in (0, 1):
                v = local(st, around(z + 2 * sgn, nz)) + buf[dr, 1, 1 + st].astype(F32)
                if st == dr:
                    v = v + buf[dr, 1, 0].astype(F32)
                buf[dr, 3, st] = v.astype(buf.dtype)
            send(kind, buf.at[dr, 3, pl.ds(0, 2)], buf.at[dr, 4, pl.ds(0, 2)], rs.at[2], hop(2 * sgn))

    def near_step(kind, buf, local, rs):
        for dr in (0, 1):
            sgn = 1 - 2 * dr
            for st in (0, 1):
                buf[dr, 6, st] = local(st, around(z + sgn, nz)).astype(buf.dtype)
            send(kind, buf.at[dr, 6, pl.ds(0, 2)], buf.at[dr, 5, pl.ds(0, 2)], rs.at[2], hop(sgn))

    def sum_end(buf, rs):
        arrived(buf.at[:, pl.ds(4, 2), pl.ds(0, 2)], rs.at[2])

    def sum_total(st, buf, local):
        v = local(st, z)
        for dr in (0, 1):
            v = v + buf[dr, 4, st].astype(F32) + buf[dr, 5, st].astype(F32)
        return v

    def ring_step(kind, s, buf, local, rs):
        for dr in (0, 1):
            sgn = 1 - 2 * dr
            p = around(z + sgn * (top - s), nz)
            if s == 1:
                arrived(buf.at[dr, s, dr], rs.at[dr, s - 1])
            elif s > 1:
                arrived(buf.at[dr, s], rs.at[dr, s - 1])
            for st in (dr,) if s == 0 else (0, 1):
                v = local(st, p)
                if s > 1 or (s == 1 and st == dr):
                    v = v + buf[dr, s, st]
                buf[dr, s, st] = v
            if s == 0:
                send(kind, buf.at[dr, 0, dr], buf.at[dr, 1, dr], rs.at[dr, 0], hop(sgn))
            else:
                send(kind, buf.at[dr, s], buf.at[dr, s + 1], rs.at[dr, s], hop(sgn))

    def ring_end(buf, rs):
        for dr in (0, 1):
            arrived(buf.at[dr, top], rs.at[dr, top - 1])

    def ring_total(st, buf, local):
        return local(st, z) + buf[0, top, st] + buf[1, top, st]

    need = [top, 3, -3, 2, -2, 1, -1, 0]

    def need_at(k):
        return around(z + need[k], nz)

    def x_group(k):
        return (0, 0, 0, 1, 1, 2, 2, 3)[k]

    def x_wait(i, dst, rs):
        arrived_all(dst, (3, 2, 2, 1)[i], rs.at[i])

    def ar_copy(buf, i, k):
        return copy(buf.at[chip], buf.at[chip], ar_s.at[i], ar_r.at[i], dp_at(around(chip + k, chips)))

    def ar_start(buf, i):
        for k in range(1, chips):
            ar_copy(buf, i, k).start()

    def ar_wait(buf, i):
        arrived(buf.at[pl.ds(0, chips - 1)], ar_r.at[i])
        return jnp.sum(buf[...], axis=0)

    def ar_sent(buf, i, n):
        there = buf.at[pl.ds(0, n - 1)]
        copy(there, there, ar_s.at[i], ar_r.at[i], mate).wait_send()

    def f_start(buf, i):
        @pl.loop(1, feats)
        def _(k):
            copy(buf.at[f], buf.at[f], ar_s.at[i], ar_r.at[i], (d, around(f + k, feats))).start()

    def f_wait(buf, i):
        arrived(buf.at[pl.ds(0, feats - 1)], ar_r.at[i])

    lanes = cols // 128

    def pack(buf, at, row, v):
        for k in range(v.shape[1] // 128):
            buf[at, row + k:row + k + 1, :] = v[:, k * 128:(k + 1) * 128]

    def spread_out(v, row, n):
        return jnp.concatenate([v[row + k:row + k + 1, :] for k in range(n // 128)], axis=1)

    def norm_of(sums, squares):
        center = sums / total_rows
        spread = squares / total_rows - center * center
        return center, lax.rsqrt(spread + NORM_EPS)

    barrier = pltpu.get_barrier_semaphore()

    def greet(to):
        pl.semaphore_signal(barrier, inc=1, device_id=to, device_id_type=MESH)

    greet(mate)
    greet(x_diag)

    @pl.loop(1, feats)
    def _(k):
        greet((d, around(f + k, feats)))

    @pl.loop(1, chips)
    def _(k):
        greet(dp_at(around(chip + k, chips)))

    my_cols = pl.ds(pl.multiple_of(core * half, half), half)
    mate_cols = pl.ds(pl.multiple_of((1 - core) * half, half), half)
    w_in = pltpu.make_async_copy(w_hbm.at[:, my_cols], wb.at[xl, z, core], in_s.at[0])
    t_in = pltpu.make_async_copy(t_hbm, tb.at[0, y, 0], in_s.at[1])
    x_in = pltpu.make_async_copy(x_hbm, x_ref, in_s.at[2])
    w_in.start()
    t_in.start()
    x_in.start()
    rowsum[...] = jnp.zeros_like(rowsum)
    pl.semaphore_wait(barrier, feats + chips)

    send(WEIGHT, w_hbm.at[:, mate_cols], wb.at[xl, z, core], wc_r, mate)
    send(TEACH, t_hbm, tb.at[0, y, 1], tc_r.at[0, 0], mate)

    mid = rows // 2
    right, left = y_at(around(y + 1, ny)), y_at(around(y - 1, ny))
    offs = (0, -1, 1, 2)

    def t_at(st, e):
        return tb.at[st, around(y + offs[e], ny), 0]

    def t_hand(st, e):
        send(TEACH, t_at(st, e), tb.at[st, around(y + offs[e], ny), 1], tc_r.at[st, e], mate)

    def t_round(st, src):
        send(TEACH, src, t_at(st, 0), ty_r.at[st, 0], right)
        send(TEACH, src, t_at(st, 0), ty_r.at[st, 1], left)

    def t_pass(st):
        arrived(t_at(st, 1), ty_r.at[st, 0])
        high = t_at(st, 1).at[pl.ds(0, mid)]
        send(TEACH, high, high, ty_r.at[st, 2], right)
        arrived(t_at(st, 2), ty_r.at[st, 1])
        low = t_at(st, 2).at[pl.ds(mid, mid)]
        send(TEACH, low, low, ty_r.at[st, 2], left)
        t_hand(st, 1)
        t_hand(st, 2)

    def t_far(st):
        arrived(t_at(st, 3), ty_r.at[st, 2])
        t_hand(st, 3)

    quad = rows // 4
    ways = (x_next, x_prev)

    def t_cross(i):
        for dr in (0, 1):
            part = t_hbm.at[pl.ds((2 * dr + i) * quad, quad)]
            send(CROSS, part, rl.at[dr, i], tx_r.at[dr, i], ways[dr])

    def t_relay(i):
        for dr in (0, 1):
            arrived(rl.at[dr, i], tx_r.at[dr, i])
            there = t_at(1, 0).at[pl.ds((2 * dr + i) * quad, quad)]
            send(CROSS, rl.at[dr, i], there, to_r, ways[dr])

    def t_over():
        arrived(t_at(1, 0), to_r)
        t_round(1, t_at(1, 0))
        t_hand(1, 0)

    t_cross(0)
    t_round(0, t_hbm)
    send(CHIP, x_hbm, xp, xc_r, mate)

    def t_normal(st, e, wait_mate=True):
        p = around(y + offs[e], ny)
        if wait_mate:
            arrived(tb.at[st, p, 1], tc_r.at[st, e])
        at = (xh if st == 0 else 1 - xh) * ny + p
        center = spread_out(tst[at], 0, cols)
        recip = spread_out(tst[at], lanes, cols)
        for slot in (0, 1):

            @pl.loop(0, rows // 64)
            def _(i):
                here = pl.multiple_of(i * 64, 64)
                v = tb[st, p, slot, pl.ds(here, 64), :].astype(F32)
                there = pl.multiple_of(slot * rows + i * 64, 64)
                tn[st, p, pl.ds(there, 64), :] = ((v - center) * recip).astype(BF16)

    def w_own(p):
        return wb.at[xl, p, 0]

    def w_other(p):
        return wb.at[1 - xl, p, 0]

    def w_late(p):
        return wb.at[xl, p, 1]

    w_like = wb.at[0, :, 0]

    w_in.wait()
    arrived(wb.at[xl, z, 1 - core], wc_r)
    send(WEIGHT, w_own(z), w_own(z), wx_r, x_mate)
    ag_go(WEIGHT, w_own, wz_r.at[0])
    agx_go(WEIGHT, w_late, wz_r.at[2], wy_r)
    t_cross(1)

    t_in.wait()
    arrived(tb.at[0, y, 1], tc_r.at[0, 0])

    def t_sum(i, carry):
        a, b = carry
        for slot in (0, 1):
            v = tb[0, y, slot, pl.ds(pl.multiple_of(i * 64, 64), 64), :].astype(F32).reshape(8, 8, cols)
            a = a + jnp.sum(v, axis=0)
            b = b + jnp.sum(v * v, axis=0)
        return a, b

    zero = jnp.zeros((8, cols), F32)
    a, b = lax.fori_loop(0, rows // 64, t_sum, (zero, zero))
    pack(ar_t, chip, 0, jnp.sum(a, axis=0, keepdims=True))
    pack(ar_t, chip, lanes, jnp.sum(b, axis=0, keepdims=True))
    ar_start(ar_t, 0)

    arrived(w_other(z), wx_r)
    ag_go(WEIGHT, w_other, wz_r.at[1])
    t_relay(0)
    ag_on(WEIGHT, w_own, wz_r.at[0], 0)
    agx_on(WEIGHT, w_late, wz_r.at[2], wy_r, w_like)
    t_relay(1)
    ag_on(WEIGHT, w_other, wz_r.at[1], 1)
    t_pass(0)
    agx_end(WEIGHT, w_late, wz_r.at[2], wy_r, w_like)
    sums = ar_wait(ar_t, 0)
    center, recip = norm_of(sums[0:lanes], sums[lanes:2 * lanes])
    tst[f, 0:lanes, :] = center
    tst[f, lanes:2 * lanes, :] = recip
    f_start(tst, 3)
    ag_end(w_like, wz_r.at[0])

    x_in.wait()
    arrived(xp, xc_r)
    wide = wb.shape[1] * wb.shape[2] * wb.shape[3]
    tile = min(256, rows)
    tiles = rows // tile
    narrow = jnp.zeros((8, half), F32)

    def project(ref, base, h, last):
        deep = pl.ds(pl.multiple_of(h * wide, wide), wide)

        def body(i, carry):
            here = pl.ds(pl.multiple_of(i * tile, tile), tile)
            there = pl.ds(pl.multiple_of(base + i * tile, tile), tile)
            v = jnp.dot(ref[here, deep], wb[h].reshape(wide, half), preferred_element_type=F32)
            if last:
                v = v + pj[there, :]
            pj[there, :] = v
            if not last:
                return carry
            v = v.reshape(tile // 8, 8, half)
            return carry[0] + jnp.sum(v, axis=0), carry[1] + jnp.sum(v * v, axis=0)

        return body

    lax.fori_loop(0, tiles, project(x_ref, 0, xl, False), 0)
    lax.fori_loop(0, tiles, project(xp, rows, xl, False), 0)
    t_over()
    ag_end(w_like, wz_r.at[1])
    arrived(wb.at[1 - xl, :, 1], wy_r)
    carry = lax.fori_loop(0, tiles, project(x_ref, 0, 1 - xl, True), (narrow, narrow))
    a, b = lax.fori_loop(0, tiles, project(xp, rows, 1 - xl, True), carry)
    ar_p[chip] = jnp.zeros((8, 128), F32)
    pack(ar_p, chip, 0, jnp.sum(a, axis=0, keepdims=True))
    pack(ar_p, chip, lanes // 2, jnp.sum(b, axis=0, keepdims=True))
    ar_start(ar_p, 1)
    t_far(0)
    f_wait(tst, 3)
    t_normal(0, 0, wait_mate=False)

    def n_sum(i, total):
        v = tn[0, y, pl.ds(pl.multiple_of(i * 64, 64), 64), :].astype(F32)
        return total + jnp.sum(v.reshape(8, 8, cols), axis=0)

    n_sums = lax.fori_loop(0, 2 * rows // 64, n_sum, zero)
    ar_n[chip] = jnp.zeros((8, 128), F32)
    pack(ar_n, chip, 0, jnp.sum(n_sums, axis=0, keepdims=True))
    ar_start(ar_n, 5)
    t_normal(0, 1)
    t_normal(0, 2)

    sums = ar_wait(ar_p, 1)
    p_center, p_recip = norm_of(spread_out(sums, 0, half), spread_out(sums, lanes // 2, half))
    all_tiles = 2 * tiles
    for i in range(all_tiles):
        v = (pj[i * tile:(i + 1) * tile, :] - p_center) * p_recip
        pj[i * tile:(i + 1) * tile, :] = v
        sT[:, i * tile:(i + 1) * tile] = v.T.astype(BF16)

    span = (ny // 2) * cols

    def correlate(g, h):
        @pl.loop(0, ny // 2)
        def _(j):
            v = jnp.dot(sT[...], tn[g, h * (ny // 2) + j], preferred_element_type=F32)
            cc[g, h, :, pl.ds(pl.multiple_of(j * cols, cols), cols)] = v

    quarter = half // 2
    piece = quarter // nz

    def rows_of(a, p):
        return pl.ds(pl.multiple_of(a * quarter + p * piece, piece), piece)

    side = span // 2

    def sides(st):
        return slice(st * side, (st + 1) * side)

    def ca_local(g):
        return lambda st, p: cc[g, xl if st == 0 else 1 - xl, rows_of(0, p), :]

    def ca_far(g):
        far_step(CORR, ca.at[g], ca_local(g), ca_r.at[g])

    def ca_mid(g):
        mid_step(CORR, ca.at[g], ca_local(g), ca_r.at[g])

    def ca_near(g):
        near_step(CORR, ca.at[g], ca_local(g), ca_r.at[g])

    def ca_over(g):
        sum_end(ca.at[g], ca_r.at[g])
        xs[g] = sum_total(1, ca.at[g], ca_local(g)).astype(xs.dtype)
        send(CORR, xs.at[g], xr.at[g], cx_r.at[g], x_mate)

    def cb_over(g):
        bs[g] = cc[g, 1 - xl, quarter:half, :].astype(BF16).reshape(nz, piece, span)
        for k in range(nz):
            send(CORR, bs.at[g, need_at(k)], br.at[g, need_at(k)], bx_r.at[g, x_group(k)], x_mate)

    def cb_local(g):
        return lambda st, p: cc[g, xl, rows_of(1, p), sides(st)] + br[g, p, :, sides(st)].astype(F32)

    def cb_far(g):
        x_wait(0, br.at[g], bx_r.at[g])
        far_step(CORR, cb.at[g], cb_local(g), cb_r.at[g])

    def cb_mid(g):
        x_wait(1, br.at[g], bx_r.at[g])
        mid_step(CORR, cb.at[g], cb_local(g), cb_r.at[g])

    def cb_near(g):
        x_wait(2, br.at[g], bx_r.at[g])
        near_step(CORR, cb.at[g], cb_local(g), cb_r.at[g])

    def slope(a, g):
        if a == 0:
            v = sum_total(0, ca.at[g], ca_local(g))
            arrived(xr.at[g], cx_r.at[g])
            v = v + xr[g].astype(F32)
        else:
            sum_end(cb.at[g], cb_r.at[g])
            x_wait(3, br.at[g], bx_r.at[g])
            v = jnp.concatenate([sum_total(st, cb.at[g], cb_local(g)) for st in (0, 1)], axis=1)
        share = v / total_rows
        student_index = (
            f * cols + core * half + a * quarter + z * piece
            + lax.broadcasted_iota(jnp.int32, share.shape, 0)
        )
        group = xh if g == 0 else 1 - xh
        teacher_index = (group * 2 + xl) * span + lax.broadcasted_iota(jnp.int32, share.shape, 1)
        on_diag = student_index == teacher_index
        part = jnp.where(on_diag, (1.0 - share) ** 2, OFF_WEIGHT * share * share)
        lacc[g, a] = jnp.sum(part.reshape(piece // 8, 8, span), axis=0)
        lean = jnp.where(on_diag, -2.0 * (1.0 - share), 2.0 * OFF_WEIGHT * share).astype(BF16)
        sl[g, xl, a, z] = lean
        lean = lean.astype(F32)
        at = group * ny + xl * (ny // 2)
        n_row = jnp.concatenate([spread_out(nst[at + k], 0, cols) for k in range(ny // 2)], axis=1)
        here = pl.ds(pl.multiple_of(z * piece, piece), piece)
        for k, v in ((a, lean * n_row), (2 + a, lean * share)):
            v = jnp.broadcast_to(jnp.sum(v, axis=1, keepdims=True), (piece, 128))
            rowsum[k, here, :] = v if g == 0 else rowsum[k, here, :] + v
        if (a, g) == (0, 1):
            there = sl.at[g, xl, 0, z]
            send(CORR, there, there, sx_r, x_mate)
            ag_go(CORR, sa_own(g), sz_r.at[0])
        else:
            agx_go(CORR, sb_own(a, g), sb_r.at[g, a], sy_r.at[g, a])

    def sa_own(g):
        return lambda p: sl.at[g, xl, 0, p]

    def sa_mate(g):
        return lambda p: sl.at[g, 1 - xl, 0, p]

    def sb_own(a, g):
        return lambda p: sl.at[g, xl, a, p]

    def sa_other(g):
        arrived(sl.at[g, 1 - xl, 0, z], sx_r)
        ag_go(CORR, sa_mate(g), sz_r.at[1])

    def sa_on(g):
        ag_on(CORR, sa_own(g), sz_r.at[0], 0)

    def sa_on_other(g):
        ag_on(CORR, sa_mate(g), sz_r.at[1], 1)

    def sa_end(g):
        ag_end(sl.at[g, 0, 0], sz_r.at[0])
        ag_end(sl.at[g, 0, 0], sz_r.at[1])

    def sb_on(a, g):
        agx_on(CORR, sb_own(a, g), sb_r.at[g, a], sy_r.at[g, a], sl.at[g, xl, a])

    def sb_end(a, g):
        agx_end(CORR, sb_own(a, g), sb_r.at[g, a], sy_r.at[g, a], sl.at[g, xl, a])

    def sb_last(a, g):
        arrived(sl.at[g, 1 - xl, a], sy_r.at[g, a])

    def row_tile(i):
        return pl.ds(pl.multiple_of(i * tile, tile), tile)

    def times_slope(v, g, here):
        for j in range(ny):
            h, k = j // (ny // 2), j % (ny // 2)
            rhs = sl[g, h, :, :, :, k * cols:(k + 1) * cols].reshape(half, cols)
            w = lax.dot_general(
                tn[g, j, here, :], rhs, (((1,), (1,)), ((), ())), preferred_element_type=F32
            )
            v = w if v is None else v + w
        return v

    def upstream_first():
        @pl.loop(0, all_tiles)
        def _(i):
            uu[row_tile(i), :] = times_slope(None, 0, row_tile(i))

    def u_start():
        for k in range(4):
            ar_u[chip, k:k + 1, :] = rowsum[k].T[0:1]
        part = jnp.sum(lacc[0, 0] + lacc[0, 1] + lacc[1, 0] + lacc[1, 1], axis=0, keepdims=True)
        part = sum(part[:, k * cols:(k + 1) * cols] for k in range(span // cols))
        pack(ar_u, chip, lanes, part)
        ar_start(ar_u, 2)

    def delta():
        sums = ar_wait(ar_u, 2)
        mean_g = spread_out(sums, 0, half) / (total_rows * total_rows)
        mean_x = spread_out(sums, lanes // 2, half) / total_rows

        @pl.loop(0, all_tiles)
        def _(i):
            here = row_tile(i)
            v = times_slope(uu[here, :], 1, here) / total_rows
            v = p_recip * (v - mean_g - pj[here, :] * mean_x)
            sT[:, pl.ds(pl.multiple_of(i * tile, tile), tile)] = v.T.astype(BF16)

        return sums

    strip = gg.shape[3]
    band = quarter // 2

    def gradient(h, out):
        @pl.loop(0, nz // 2)
        def _(j):
            here = pl.ds(pl.multiple_of(h * nz * strip + j * 2 * strip, 2 * strip), 2 * strip)
            v = jnp.dot(sT[:, 0:rows], x_ref[:, here], preferred_element_type=F32)
            v = v + jnp.dot(sT[:, rows:2 * rows], xp[:, here], preferred_element_type=F32)
            v = v.astype(out.dtype)
            for a in (0, 1):
                for k in (0, 1):
                    out[a, 2 * j + k] = v[a * quarter:(a + 1) * quarter, k * strip:(k + 1) * strip]

    def ga_local(i):
        part = slice(i * band, (i + 1) * band)
        return lambda st, p: (gg if st == 0 else gs)[0, p, part, :]

    def ga_step(s):
        for i in (0, 1):
            ring_step(GRAD, s, ga.at[i], ga_local(i), ga_r.at[i])

    def ga_over():
        for i in (0, 1):
            ring_end(ga.at[i], ga_r.at[i])
            gxs[i] = ring_total(1, ga.at[i], ga_local(i))
            send(GRAD, gxs.at[i], gxr.at[i], gx_r.at[i], x_mate)

    def gb_over():
        for k in range(nz):
            send(GRAD, gs.at[1, need_at(k)], gr.at[need_at(k)], gy_r.at[x_group(k)], x_mate)

    def gb_local(st, p):
        part = slice(st * band, (st + 1) * band)
        return gg[1, p, part, :] + gr[p, part, :]

    def gb_far():
        x_wait(0, gr, gy_r)
        far_step(GRAD, gb, gb_local, gb_r)

    def gb_mid():
        x_wait(1, gr, gy_r)
        mid_step(GRAD, gb, gb_local, gb_r)

    def gb_near():
        x_wait(2, gr, gy_r)
        near_step(GRAD, gb, gb_local, gb_r)

    mine = strip // 2
    first = core == 0

    def g_core(a):
        if a == 0:
            parts = []
            for i in (0, 1):
                v = ring_total(0, ga.at[i], ga_local(i))
                arrived(gxr.at[i], gx_r.at[i])
                parts.append(v + gxr[i])
        else:
            sum_end(gb, gb_r)
            x_wait(3, gr, gy_r)
            parts = [sum_total(st, gb, gb_local) for st in (0, 1)]
        v = jnp.concatenate(parts, axis=0)
        v = (LOSS_SCALE * v).T
        low, high = v[0:mine], v[mine:strip]
        gcs[a] = jnp.where(first, high, low)
        send(GRAD, gcs.at[a], gcr.at[a], gc_r.at[a], mate)
        g_ref[:, pl.ds(pl.multiple_of(core * half + a * quarter, quarter), quarter)] = jnp.where(first, low, high)

    def g_last(a):
        arrived(gcr.at[a], gc_r.at[a])
        g_ref[:, pl.ds(pl.multiple_of((1 - core) * half + a * quarter, quarter), quarter)] = gcr[a]

    t_normal(0, 3)
    correlate(0, 1 - xl)
    cb_over(0)
    correlate(0, xl)
    ca_far(0)
    ca_near(0)
    t_normal(1, 0)
    nst[f] = ar_wait(ar_n, 5)
    f_start(nst, 6)
    cb_far(0)
    ca_mid(0)
    t_pass(1)
    cb_mid(0)
    cb_near(0)
    ca_over(0)
    t_normal(1, 1)
    t_normal(1, 2)
    t_far(1)
    f_wait(nst, 6)
    slope(1, 0)
    slope(0, 0)
    t_normal(1, 3)
    correlate(1, 1 - xl)
    cb_over(1)
    correlate(1, xl)
    ca_far(1)
    ca_near(1)
    cb_far(1)
    ca_mid(1)
    sb_on(0, 0)
    sb_on(1, 0)
    cb_mid(1)
    cb_near(1)
    ca_over(1)
    sb_end(0, 0)
    sb_end(1, 0)
    slope(0, 1)
    slope(1, 1)
    u_start()
    sa_other(1)
    sa_on(1)
    sb_on(1, 1)
    sa_on_other(1)
    sb_last(0, 0)
    sb_last(1, 0)
    upstream_first()
    sb_end(1, 1)
    sa_end(1)
    sb_last(1, 1)
    sums = delta()
    gradient(1 - xl, gs)
    gb_over()
    gradient(xl, gg)
    ga_step(0)
    lf[f] = jnp.broadcast_to(jnp.sum(sums[lanes:2 * lanes], axis=0, keepdims=True), (8, 128))
    f_start(lf, 4)
    ga_step(1)
    gb_far()
    ga_step(2)
    gb_mid()
    ga_step(3)
    gb_near()
    f_wait(lf, 4)
    lc[0] = jnp.sum(lf[...], axis=0)
    copy(lc.at[0], lc.at[1], ar_s.at[7], lc_r, mate).start()
    ga_over()
    g_core(1)
    g_core(0)
    arrived(lc.at[1], lc_r)
    loss_ref[0, 0] = jnp.sum((lc[0] + lc[1])[0:1]) / width_all
    g_last(1)
    g_last(0)
    ar_sent(ar_t, 0, chips)
    ar_sent(ar_p, 1, chips)
    ar_sent(ar_u, 2, chips)
    ar_sent(ar_n, 5, chips)
    ar_sent(nst, 6, feats)
    ar_sent(tst, 3, feats)
    ar_sent(lf, 4, feats)
    copy(lc.at[0], lc.at[1], ar_s.at[7], lc_r, mate).wait_send()
    for kind, size in weigh.items():
        there = {WEIGHT: pj, TEACH: tn, CORR: cc}.get(kind, cc.at[0])
        line = there.dtype.itemsize
        for n in there.shape[:-2] + there.shape[-1:]:
            line *= n
        assert size % line == 0 and size // line % 8 == 0
        there = there.at[(slice(None),) * (len(there.shape) - 2) + (pl.ds(0, size // line),)]
        copy(there, there, out_s.at[kind], lc_r, mate).wait_send()


def shards(nz, ny, student, weight, teacher):
    rows, wide = student.shape
    strip_w, cols = weight.shape
    half = cols // 2
    span = (ny // 2) * cols
    chips, feats = 2 * nz, 2 * ny
    strip = wide // chips
    quarter = half // 2
    piece = quarter // nz
    V = pltpu.VMEM
    D = pltpu.SemaphoreType.DMA
    data = [
        V((rows, wide), BF16),
        V((2, ny, 2, rows, cols), BF16),
        V((2, ny, 2 * rows, cols), BF16),
        V((2, 2, rows // 4, cols), BF16),
        V((rows, wide), BF16),
        V((2, nz, 2, strip_w, half), BF16),
        V((2 * rows, half), F32),
        V((half, 2 * rows), BF16),
        V((2, 2, half, span), F32),
        V((2, 2, 7, 3, piece, span), BF16),
        V((2, 2, 7, 3, piece, span // 2), BF16),
        V((2, piece, span), BF16),
        V((2, piece, span), BF16),
        V((2, nz, piece, span), BF16),
        V((2, nz, piece, span), BF16),
        V((2, 2, 2, nz, piece, span), BF16),
        V((2 * rows, half), F32),
        V((2, nz, quarter, strip), F32),
        V((2, nz, quarter, strip), F32),
        V((nz, quarter, strip), F32),
        V((2, 2, nz // 2 + 1, 2, quarter // 2, strip), F32),
        V((2, 7, 3, quarter // 2, strip), F32),
        V((2, quarter // 2, strip), F32),
        V((2, quarter // 2, strip), F32),
        V((2, strip // 2, quarter), F32),
        V((2, strip // 2, quarter), F32),
        V((chips, 8, 128), F32),
        V((chips, 8, 128), F32),
        V((chips, 8, 128), F32),
        V((chips, 8, 128), F32),
        V((feats, 8, 128), F32),
        V((feats, 8, 128), F32),
        V((4, 128, 128), F32),
        V((2, 2, 8, span), F32),
        V((feats, 8, 128), F32),
        V((2, 8, 128), F32),
    ]
    sems = [
        D(shape) for shape in (
            (6,), (3,), (8,), (7,),
            (2, ny), (2, 2), (), (2, 3), (), (), (), (3, 4), (),
            (2, 3), (2,), (2, 3), (2, 4),
            (), (2, 4), (2, 2, 4), (2, 2),
            (2, 2, nz // 2), (2,), (4,), (3,), (2,), (),
        )
    ]
    vm = pl.BlockSpec(memory_space=pltpu.VMEM)
    sm = pl.BlockSpec(memory_space=pltpu.SMEM)
    far = pl.BlockSpec(memory_space=pl.ANY)
    loss, grad = pl.pallas_call(
        functools.partial(kernel, nz, ny),
        out_shape=(
            jax.ShapeDtypeStruct((1, 1), F32),
            jax.ShapeDtypeStruct((strip_w, cols), F32),
        ),
        in_specs=[far] * 3,
        out_specs=(sm, vm),
        scratch_shapes=data + sems,
        compiler_params=pltpu.CompilerParams(
            collective_id=0, has_side_effects=True, vmem_limit_bytes=56 * 1024 * 1024
        ),
    )(student, weight, teacher)
    return loss.reshape(()), grad


def solution(mesh):
    placed = (P("dp", None), P("dp", "feat"), P("dp", "feat"))
    nz, ny = mesh.shape["dp"] // 4, mesh.shape["feat"] // 2
    return jax.shard_map(
        functools.partial(shards, nz, ny), mesh=mesh, in_specs=placed,
        out_specs=(P(), P("dp", "feat")), check_vma=False,
    )
```

```python
import functools

import jax
import jax.numpy as jnp
from jax import lax
from jax.experimental import pallas as pl
from jax.experimental.pallas import tpu as pltpu
from jax.sharding import PartitionSpec as P

OFF_WEIGHT = 0.5
NORM_EPS = 1e-05
LOSS_SCALE = 128.0
F32 = jnp.float32
BF16 = jnp.bfloat16
MESH = pl.DeviceIdType.MESH


def around(at, n):
    return lax.rem(at + n, n)


def kernel(
    nz, ny, x_hbm, w_hbm, t_hbm, loss_ref, g_ref,
    x_ref, tb, tn, rl, xp, wb, pj, sT,
    cc0, cc1, ca0, ca1, cb0, cb1, xs0, xs1, xr0, xr1, bs0, bs1, br0, br1, sl0, sl1, uu, gg, gs, gr, ga, gb, gxs, gxr, gcs, gcr,
    ar_t, ar_p, ar_u, ar_n, tst, nst, rowsum, lacc, lf, lc,
    out_s, in_s, ar_s, ar_r, tc_r, tx_r, to_r, ty_r, xc_r, wc_r, wx_r, wz_r,
    ca_r, cx_r, cb_r, bx_r, sx_r, sz_r, sr_r, sb_r, sy_r, ga_r, gx_r, gy_r, gb_r, gc_r, lc_r,
):
    cc, ca, cb, xs = (cc0, cc1), (ca0, ca1), (cb0, cb1), (xs0, xs1)
    xr, bs, br, sl = (xr0, xr1), (bs0, bs1), (br0, br1), (sl0, sl1)
    d = lax.axis_index("dp")
    f = lax.axis_index("feat")
    chips = 2 * nz
    feats = 2 * ny
    core = lax.rem(d, 2)
    chip = lax.div(d, 2)
    z = lax.rem(chip, nz)
    xl = lax.div(chip, nz)
    y = lax.rem(f, ny)
    xh = lax.div(f, ny)
    rows = x_ref.shape[0]
    cols = w_hbm.shape[1]
    half = cols // 2
    total_rows = float(rows * 2 * chips)
    width_all = cols * feats

    mate = (d + 1 - 2 * core, f)

    def dp_at(chip_at):
        return (chip_at * 2 + core, f)

    def z_at(at):
        return dp_at(xl * nz + at)

    def y_at(at):
        return (d, xh * ny + at)

    x_mate = dp_at((1 - xl) * nz + z)
    cross = ((1 - xl) * nz + z) * 2 + core
    x_diag = (cross, (1 - xh) * ny + y)
    x_next = (cross, jnp.where(xl == 0, xh, 1 - xh) * ny + y)
    x_prev = (cross, jnp.where(xl == 0, 1 - xh, xh) * ny + y)

    weigh = {}
    CHIP, WEIGHT, TEACH, CROSS, CORR, GRAD, LAST = range(7)

    def copy(src, dst, s, r, to):
        return pltpu.make_async_remote_copy(
            src_ref=src, dst_ref=dst, send_sem=s, recv_sem=r, device_id=to, device_id_type=MESH
        )

    def send(kind, src, dst, r, to):
        copy(src, dst, out_s.at[kind], r, to).start()
        size = src.dtype.itemsize
        for n in src.shape:
            size *= n
        weigh[kind] = weigh.get(kind, 0) + size

    def arrived(dst, r):
        copy(dst, dst, out_s.at[0], r, mate).wait_recv()

    top = nz // 2

    def hop(k):
        return z_at(around(z + k, nz))

    def arrived_all(ref, n, r):
        arrived(ref.at[pl.ds(0, n)], r)

    def ag_go(kind, slot, rs):
        for k, r in ((2, 2), (-2, 3), (1, 0), (-1, 0)):
            send(kind, slot(z), slot(z), rs.at[r], hop(k))

    def ag_on(kind, slot, rs, far=None):
        for dr in (0, 1):
            sgn = 1 - 2 * dr
            block = slot(around(z - 2 * sgn, nz))
            arrived(block, rs.at[2 + dr])
            if far is None:
                side = block.shape[-1] // 2
                part = block.at[:, pl.ds(dr * side, side)]
                send(kind, part, part, rs.at[1], hop(2 * sgn))
            elif far == dr:
                send(kind, block, block, rs.at[1], hop(2 * sgn))
            send(kind, block, block, rs.at[1], hop(sgn))

    def ag_end(like, rs):
        arrived_all(like, 2, rs.at[0])
        arrived_all(like, 3, rs.at[1])

    def agx_to(kind, slot, xr, offs):
        for off in offs:
            block = slot(around(z + off, nz))
            send(kind, block, block, xr, x_mate)

    def agx_go(kind, slot, rs, xr):
        ag_go(kind, slot, rs)
        agx_to(kind, slot, xr, (0,))

    def agx_on(kind, slot, rs, xr, like):
        ag_on(kind, slot, rs)
        agx_to(kind, slot, xr, (-2, 2))
        arrived_all(like, 2, rs.at[0])
        agx_to(kind, slot, xr, (-1, 1))

    def agx_end(kind, slot, rs, xr, like):
        arrived_all(like, 3, rs.at[1])
        agx_to(kind, slot, xr, (-3, 3, top))

    def far_step(kind, buf, local, rs):
        for dr in (0, 1):
            buf[dr, 2, 0] = local(dr, around(z + top, nz)).astype(buf.dtype)
            send(kind, buf.at[dr, 2, 0], buf.at[dr, 1, 0], rs.at[dr], hop(2 - 4 * dr))
        for dr in (0, 1):
            sgn = 1 - 2 * dr
            for st in (0, 1):
                buf[dr, 0, st] = local(st, around(z + 3 * sgn, nz)).astype(buf.dtype)
            send(kind, buf.at[dr, 0, pl.ds(0, 2)], buf.at[dr, 1, pl.ds(1, 2)], rs.at[dr], hop(sgn))

    def mid_step(kind, buf, local, rs):
        for dr in (0, 1):
            sgn = 1 - 2 * dr
            arrived(buf.at[dr, 1], rs.at[dr])
            for st in (0, 1):
                v = local(st, around(z + 2 * sgn, nz)) + buf[dr, 1, 1 + st].astype(F32)
                if st == dr:
                    v = v + buf[dr, 1, 0].astype(F32)
                buf[dr, 3, st] = v.astype(buf.dtype)
            send(kind, buf.at[dr, 3, pl.ds(0, 2)], buf.at[dr, 4, pl.ds(0, 2)], rs.at[2], hop(2 * sgn))

    def near_step(kind, buf, local, rs):
        for dr in (0, 1):
            sgn = 1 - 2 * dr
            for st in (0, 1):
                buf[dr, 6, st] = local(st, around(z + sgn, nz)).astype(buf.dtype)
            send(kind, buf.at[dr, 6, pl.ds(0, 2)], buf.at[dr, 5, pl.ds(0, 2)], rs.at[2], hop(sgn))

    def sum_end(buf, rs):
        arrived(buf.at[:, pl.ds(4, 2), pl.ds(0, 2)], rs.at[2])

    def sum_total(st, buf, local):
        v = local(st, z)
        for dr in (0, 1):
            v = v + buf[dr, 4, st].astype(F32) + buf[dr, 5, st].astype(F32)
        return v

    def ring_step(kind, s, buf, local, rs):
        for dr in (0, 1):
            sgn = 1 - 2 * dr
            p = around(z + sgn * (top - s), nz)
            if s == 1:
                arrived(buf.at[dr, s, dr], rs.at[dr, s - 1])
            elif s > 1:
                arrived(buf.at[dr, s], rs.at[dr, s - 1])
            for st in (dr,) if s == 0 else (0, 1):
                v = local(st, p)
                if s > 1 or (s == 1 and st == dr):
                    v = v + buf[dr, s, st].astype(F32)
                buf[dr, s, st] = v.astype(buf.dtype)
            if s == 0:
                send(kind, buf.at[dr, 0, dr], buf.at[dr, 1, dr], rs.at[dr, 0], hop(sgn))
            else:
                send(kind, buf.at[dr, s], buf.at[dr, s + 1], rs.at[dr, s], hop(sgn))

    def ring_end(buf, rs):
        for dr in (0, 1):
            arrived(buf.at[dr, top], rs.at[dr, top - 1])

    def ring_total(st, buf, local):
        return local(st, z) + buf[0, top, st].astype(F32) + buf[1, top, st].astype(F32)

    need = [top, 3, -3, 2, -2, 1, -1, 0]

    def need_at(k):
        return around(z + need[k], nz)

    def x_group(k):
        return (0, 0, 0, 1, 1, 2, 2, 3)[k]

    def x_wait(i, dst, rs):
        arrived_all(dst, (3, 2, 2, 1)[i], rs.at[i])

    def ar_copy(buf, i, k):
        return copy(buf.at[chip], buf.at[chip], ar_s.at[i], ar_r.at[i], dp_at(around(chip + k, chips)))

    def ar_start(buf, i):
        for k in range(1, chips):
            ar_copy(buf, i, k).start()

    def ar_wait(buf, i):
        arrived(buf.at[pl.ds(0, chips - 1)], ar_r.at[i])
        return jnp.sum(buf[...], axis=0)

    def ar_sent(buf, i, n):
        there = buf.at[pl.ds(0, n - 1)]
        copy(there, there, ar_s.at[i], ar_r.at[i], mate).wait_send()

    def f_start(buf, i):
        @pl.loop(1, feats)
        def _(k):
            copy(buf.at[f], buf.at[f], ar_s.at[i], ar_r.at[i], (d, around(f + k, feats))).start()

    def f_wait(buf, i):
        arrived(buf.at[pl.ds(0, feats - 1)], ar_r.at[i])

    lanes = cols // 128

    def pack(buf, at, row, v):
        for k in range(v.shape[1] // 128):
            buf[at, row + k:row + k + 1, :] = v[:, k * 128:(k + 1) * 128]

    def spread_out(v, row, n):
        return jnp.concatenate([v[row + k:row + k + 1, :] for k in range(n // 128)], axis=1)

    def norm_of(sums, squares):
        center = sums / total_rows
        spread = squares / total_rows - center * center
        return center, lax.rsqrt(spread + NORM_EPS)

    barrier = pltpu.get_barrier_semaphore()

    def greet(to):
        pl.semaphore_signal(barrier, inc=1, device_id=to, device_id_type=MESH)

    greet(mate)
    greet(x_diag)

    @pl.loop(1, feats)
    def _(k):
        greet((d, around(f + k, feats)))

    @pl.loop(1, chips)
    def _(k):
        greet(dp_at(around(chip + k, chips)))

    my_cols = pl.ds(pl.multiple_of(core * half, half), half)
    mate_cols = pl.ds(pl.multiple_of((1 - core) * half, half), half)
    w_in = pltpu.make_async_copy(w_hbm.at[:, my_cols], wb.at[xl, z, core], in_s.at[0])
    t_in = pltpu.make_async_copy(t_hbm, tb.at[0, y, 0], in_s.at[1])
    x_in = pltpu.make_async_copy(x_hbm, x_ref, in_s.at[2])
    w_in.start()
    t_in.start()
    x_in.start()
    rowsum[...] = jnp.zeros_like(rowsum)
    pl.semaphore_wait(barrier, feats + chips)

    send(WEIGHT, w_hbm.at[:, mate_cols], wb.at[xl, z, core], wc_r, mate)
    send(TEACH, t_hbm, tb.at[0, y, 1], tc_r.at[0, 0], mate)

    mid = rows // 2
    right, left = y_at(around(y + 1, ny)), y_at(around(y - 1, ny))
    offs = (0, -1, 1, 2)

    def t_at(st, e):
        return tb.at[st, around(y + offs[e], ny), 0]

    def t_hand(st, e):
        send(TEACH, t_at(st, e), tb.at[st, around(y + offs[e], ny), 1], tc_r.at[st, e], mate)

    high, low = pl.ds(0, mid), pl.ds(mid, mid)

    def t_round(st, src):
        there = t_at(st, 0)
        send(TEACH, src.at[high], there.at[high], ty_r.at[st, 0], right)
        send(TEACH, src.at[low], there.at[low], ty_r.at[st, 1], left)
        send(TEACH, src.at[low], there.at[low], ty_r.at[st, 3], right)
        send(TEACH, src.at[high], there.at[high], ty_r.at[st, 4], left)

    def t_pass(st):
        for e, part, to in ((1, high, right), (2, low, left)):
            part = t_at(st, e).at[part]
            arrived(part, ty_r.at[st, e - 1])
            send(TEACH, part, part, ty_r.at[st, 2], to)

    def t_near(st):
        for e, part in ((1, low), (2, high)):
            arrived(t_at(st, e).at[part], ty_r.at[st, e + 2])
            t_hand(st, e)

    def t_far(st):
        arrived(t_at(st, 3), ty_r.at[st, 2])
        t_hand(st, 3)

    quad = rows // 4
    ways = (x_next, x_prev)

    def t_cross(i):
        for dr in (0, 1):
            part = t_hbm.at[pl.ds((2 * dr + i) * quad, quad)]
            send(CROSS, part, rl.at[dr, i], tx_r.at[dr, i], ways[dr])

    def t_relay(i):
        for dr in (0, 1):
            arrived(rl.at[dr, i], tx_r.at[dr, i])
            there = t_at(1, 0).at[pl.ds((2 * dr + i) * quad, quad)]
            send(CROSS, rl.at[dr, i], there, to_r, ways[dr])

    def t_over():
        arrived(t_at(1, 0), to_r)
        t_round(1, t_at(1, 0))
        t_hand(1, 0)

    t_round(0, t_hbm)
    send(CHIP, x_hbm, xp, xc_r, mate)

    def t_normal(st, e, wait_mate=True):
        p = around(y + offs[e], ny)
        if wait_mate:
            arrived(tb.at[st, p, 1], tc_r.at[st, e])
        at = (xh if st == 0 else 1 - xh) * ny + p
        center = spread_out(tst[at], 0, cols)
        recip = spread_out(tst[at], lanes, cols)
        for slot in (0, 1):

            @pl.loop(0, rows // 64)
            def _(i):
                here = pl.multiple_of(i * 64, 64)
                v = tb[st, p, slot, pl.ds(here, 64), :].astype(F32)
                there = pl.multiple_of(slot * rows + i * 64, 64)
                tn[st, p, pl.ds(there, 64), :] = ((v - center) * recip).astype(BF16)

    def w_own(p):
        return wb.at[xl, p]

    def w_other(p):
        return wb.at[1 - xl, p]

    w_in.wait()
    arrived(wb.at[xl, z, 1 - core], wc_r)
    send(WEIGHT, w_own(z), w_own(z), wx_r, x_mate)
    ag_go(WEIGHT, w_own, wz_r.at[0])
    t_cross(0)
    t_cross(1)

    t_in.wait()
    arrived(tb.at[0, y, 1], tc_r.at[0, 0])

    def t_sum(i, carry):
        a, b = carry
        for slot in (0, 1):
            v = tb[0, y, slot, pl.ds(pl.multiple_of(i * 64, 64), 64), :].astype(F32).reshape(8, 8, cols)
            a = a + jnp.sum(v, axis=0)
            b = b + jnp.sum(v * v, axis=0)
        return a, b

    zero = jnp.zeros((8, cols), F32)
    a, b = lax.fori_loop(0, rows // 64, t_sum, (zero, zero))
    pack(ar_t, chip, 0, jnp.sum(a, axis=0, keepdims=True))
    pack(ar_t, chip, lanes, jnp.sum(b, axis=0, keepdims=True))
    ar_start(ar_t, 0)

    arrived(w_other(z), wx_r)
    ag_go(WEIGHT, w_other, wz_r.at[1])
    t_relay(0)
    ag_on(WEIGHT, w_own, wz_r.at[0], 0)
    t_pass(0)
    t_relay(1)
    ag_on(WEIGHT, w_other, wz_r.at[1], 1)
    sums = ar_wait(ar_t, 0)
    center, recip = norm_of(sums[0:lanes], sums[lanes:2 * lanes])
    tst[f, 0:lanes, :] = center
    tst[f, lanes:2 * lanes, :] = recip
    f_start(tst, 3)
    t_near(0)

    ag_end(wb.at[xl], wz_r.at[0])
    x_in.wait()
    arrived(xp, xc_r)
    t_over()
    wide = wb.shape[1] * wb.shape[2] * wb.shape[3]
    tile = min(256, rows)
    tiles = rows // tile
    narrow = jnp.zeros((8, half), F32)

    def project(ref, base, h, last):
        deep = pl.ds(pl.multiple_of(h * wide, wide), wide)

        def body(i, carry):
            here = pl.ds(pl.multiple_of(i * tile, tile), tile)
            there = pl.ds(pl.multiple_of(base + i * tile, tile), tile)
            v = jnp.dot(ref[here, deep], wb[h].reshape(wide, half), preferred_element_type=F32)
            if last:
                v = v + pj[there, :]
            pj[there, :] = v
            if not last:
                return carry
            v = v.reshape(tile // 8, 8, half)
            return carry[0] + jnp.sum(v, axis=0), carry[1] + jnp.sum(v * v, axis=0)

        return body

    lax.fori_loop(0, tiles, project(x_ref, 0, xl, False), 0)
    lax.fori_loop(0, tiles, project(xp, rows, xl, False), 0)
    ag_end(wb.at[1 - xl], wz_r.at[1])
    carry = lax.fori_loop(0, tiles, project(x_ref, 0, 1 - xl, True), (narrow, narrow))
    a, b = lax.fori_loop(0, tiles, project(xp, rows, 1 - xl, True), carry)
    ar_p[chip] = jnp.zeros((8, 128), F32)
    pack(ar_p, chip, 0, jnp.sum(a, axis=0, keepdims=True))
    pack(ar_p, chip, lanes // 2, jnp.sum(b, axis=0, keepdims=True))
    ar_start(ar_p, 1)
    t_far(0)
    f_wait(tst, 3)
    t_normal(0, 0, wait_mate=False)

    def n_sum(i, total):
        v = tn[0, y, pl.ds(pl.multiple_of(i * 64, 64), 64), :].astype(F32)
        return total + jnp.sum(v.reshape(8, 8, cols), axis=0)

    n_sums = lax.fori_loop(0, 2 * rows // 64, n_sum, zero)
    ar_n[chip] = jnp.zeros((8, 128), F32)
    pack(ar_n, chip, 0, jnp.sum(n_sums, axis=0, keepdims=True))
    ar_start(ar_n, 5)
    t_normal(0, 1)
    t_normal(0, 2)

    t_normal(1, 0)
    sums = ar_wait(ar_p, 1)
    p_center, p_recip = norm_of(spread_out(sums, 0, half), spread_out(sums, lanes // 2, half))
    all_tiles = 2 * tiles
    for i in range(all_tiles):
        v = (pj[i * tile:(i + 1) * tile, :] - p_center) * p_recip
        pj[i * tile:(i + 1) * tile, :] = v
        sT[:, i * tile:(i + 1) * tile] = v.T.astype(BF16)

    def half_cols(h):
        return pl.ds(pl.multiple_of(h * half, half), half)

    def correlate(g, h):
        def block(ref, at, n):
            cc[g][h, :, at:at + n] = jnp.dot(sT[...], ref, preferred_element_type=F32)

        if g == 0:
            for j in range(ny // 2):
                block(tn[0, h * (ny // 2) + j], j * cols, cols)
            block(tn[1, y, :, half_cols(h)], ny // 2 * cols, half)
        else:
            block(tn[1, around(y - 1 + 2 * h, ny)], 0, cols)
            block(tn[1, around(y + 2, ny), :, half_cols(h)], cols, half)

    quarter = half // 2
    piece = quarter // nz

    def rows_of(a, p):
        return pl.ds(pl.multiple_of(a * quarter + p * piece, piece), piece)

    def sides(g, st):
        side = cc[g].shape[2] // 2
        return slice(st * side, (st + 1) * side)

    def ca_local(g):
        return lambda st, p: cc[g][xl if st == 0 else 1 - xl, rows_of(0, p), :]

    def ca_far(g):
        far_step(CORR, ca[g], ca_local(g), ca_r.at[g, 0])

    def ca_mid(g):
        mid_step(CORR, ca[g], ca_local(g), ca_r.at[g, 0])

    def ca_near(g):
        near_step(CORR, ca[g], ca_local(g), ca_r.at[g, 0])

    def ca_ring(s):
        ring_step(CORR, s, ca[0], ca_local(0), ca_r.at[0])

    def ca_total(g, st):
        return (ring_total, sum_total)[g](st, ca[g], ca_local(g))

    def ca_over(g):
        (ring_end, sum_end)[g](ca[g], (ca_r.at[0], ca_r.at[1, 0])[g])
        xs[g][...] = ca_total(g, 1).astype(BF16)
        send(CORR, xs[g], xr[g], cx_r.at[g], x_mate)

    def cb_over(g):
        bs[g][...] = cc[g][1 - xl, quarter:half, :].astype(BF16).reshape(bs[g].shape)
        for k in range(nz):
            send(CORR, bs[g].at[need_at(k)], br[g].at[need_at(k)], bx_r.at[g, (k + 1) // 2 if g == 0 else x_group(k)], x_mate)

    def cb_local(g):
        return lambda st, p: cc[g][xl, rows_of(1, p), sides(g, st)] + br[g][p, :, sides(g, st)].astype(F32)

    def cb_ring(s):
        arrived_all(br[0], 2 if 0 < s < top else 1, bx_r.at[0, s])
        if s < top:
            ring_step(CORR, s, cb[0], cb_local(0), cb_r.at[0])

    def cb_total(g, st):
        return (ring_total, sum_total)[g](st, cb[g], cb_local(g))

    def cb_far(g):
        x_wait(0, br[g], bx_r.at[g])
        far_step(CORR, cb[g], cb_local(g), cb_r.at[g, 0])

    def cb_mid(g):
        x_wait(1, br[g], bx_r.at[g])
        mid_step(CORR, cb[g], cb_local(g), cb_r.at[g, 0])

    def cb_near(g):
        x_wait(2, br[g], bx_r.at[g])
        near_step(CORR, cb[g], cb_local(g), cb_r.at[g, 0])

    def slope(a, g):
        if a == 0:
            v = ca_total(g, 0)
            arrived(xr[g], cx_r.at[g])
            v = v + xr[g][...].astype(F32)
        else:
            (ring_end, sum_end)[g](cb[g], (cb_r.at[0], cb_r.at[1, 0])[g])
            if g == 0:
                cb_ring(top)
            else:
                x_wait(3, br[g], bx_r.at[g])
            v = jnp.concatenate([cb_total(g, st) for st in (0, 1)], axis=1)
        share = v / total_rows
        student_index = (
            f * cols + core * half + a * quarter + z * piece
            + lax.broadcasted_iota(jnp.int32, share.shape, 0)
        )
        col = lax.broadcasted_iota(jnp.int32, share.shape, 1)
        whole = ny // 2 * cols
        teacher_index = jnp.where(col < whole, (xh * 2 + xl) * whole + col, -1) if g == 0 else -1 - col
        on_diag = student_index == teacher_index
        part = jnp.where(on_diag, (1.0 - share) ** 2, OFF_WEIGHT * share * share)
        part = jnp.sum(part.reshape(piece // 8, 8, part.shape[1]), axis=0)
        lacc[g, a] = sum(part[:, k:k + 128] for k in range(0, part.shape[1], 128))
        lean = jnp.where(on_diag, -2.0 * (1.0 - share), 2.0 * OFF_WEIGHT * share).astype(BF16)
        sl[g][xl, a, z] = lean
        lean = lean.astype(F32)
        other = (1 - xh) * ny
        if g == 0:
            at = xh * ny + xl * (ny // 2)
            blocks, last = [at + k for k in range(ny // 2)], other + y
        else:
            blocks, last = [other + around(y - 1 + 2 * xl, ny)], other + around(y + 2, ny)
        n_row = [spread_out(nst[b], 0, cols) for b in blocks]
        last = spread_out(nst[last], 0, cols)
        n_row.append(jnp.where(xl == 0, last[:, 0:half], last[:, half:cols]))
        n_row = jnp.concatenate(n_row, axis=1)
        here = pl.ds(pl.multiple_of(z * piece, piece), piece)
        for k, v in ((a, lean * n_row), (2 + a, lean * share)):
            v = jnp.broadcast_to(jnp.sum(v, axis=1, keepdims=True), (piece, 128))
            rowsum[k, here, :] = v if g == 0 else rowsum[k, here, :] + v

    def slope_go(a, g):
        if (a, g) == (0, 1):
            there = sl[g].at[xl, 0, z]
            send(CORR, there, there, sx_r, x_mate)
            ag_go(CORR, sa_own(g), sz_r.at[0])
        else:
            if g == 0:
                s_ring(a, 0)
            else:
                agx_go(CORR, sb_own(a, g), sb_r, sy_r.at[g, a])

    def s_ring(a, s):
        own = sb_own(a, 0)
        side = sl[0].shape[-1] // 2
        if s == 0:
            agx_to(CORR, own, sy_r.at[0, a], (0,))
        for dr in (0, 1):
            sgn = 1 - 2 * dr
            block = own(around(z - sgn * s, nz))
            half_of = block.at[:, pl.ds(dr * side, side)]
            if s > 0:
                arrived(block if s < top else half_of, sr_r.at[a, dr, s - 1])
            if s < top:
                part = block if s < top - 1 else half_of
                send(CORR, part, part, sr_r.at[a, dr, s], hop(sgn))
        if s > 0:
            agx_to(CORR, own, sy_r.at[0, a], (-s, s) if s < top else (top,))

    def sa_own(g):
        return lambda p: sl[g].at[xl, 0, p]

    def sa_mate(g):
        return lambda p: sl[g].at[1 - xl, 0, p]

    def sb_own(a, g):
        return lambda p: sl[g].at[xl, a, p]

    def sa_other(g):
        arrived(sl[g].at[1 - xl, 0, z], sx_r)
        ag_go(CORR, sa_mate(g), sz_r.at[1])

    def sa_on(g):
        ag_on(CORR, sa_own(g), sz_r.at[0], 0)

    def sa_on_other(g):
        ag_on(CORR, sa_mate(g), sz_r.at[1], 1)

    def sa_end(g):
        ag_end(sl[g].at[0, 0], sz_r.at[0])
        ag_end(sl[g].at[0, 0], sz_r.at[1])

    def sb_on(a, g):
        agx_on(CORR, sb_own(a, g), sb_r, sy_r.at[g, a], sl[g].at[xl, a])

    def sb_end(a, g):
        agx_end(CORR, sb_own(a, g), sb_r, sy_r.at[g, a], sl[g].at[xl, a])

    def sb_last(a, g):
        arrived(sl[g].at[1 - xl, a], sy_r.at[g, a])

    def row_tile(i):
        return pl.ds(pl.multiple_of(i * tile, tile), tile)

    def times_slope(v, g, h, here):
        if g == 0:
            terms = [(tn[0, h * (ny // 2) + j, here, :], j * cols, cols) for j in range(ny // 2)]
            terms.append((tn[1, y, here, half_cols(h)], ny // 2 * cols, half))
        else:
            terms = [(tn[1, around(y - 1 + 2 * h, ny), here, :], 0, cols)]
            terms.append((tn[1, around(y + 2, ny), here, half_cols(h)], cols, half))
        for lhs, at, n in terms:
            rhs = sl[g][h, :, :, :, at:at + n].reshape(half, n)
            w = lax.dot_general(lhs, rhs, (((1,), (1,)), ((), ())), preferred_element_type=F32)
            v = w if v is None else v + w
        return v

    def upstream(first, *parts):
        @pl.loop(0, all_tiles)
        def _(i):
            v = None if first else uu[row_tile(i), :]
            for g, h in parts:
                v = times_slope(v, g, h, row_tile(i))
            uu[row_tile(i), :] = v

    def u_start():
        for k in range(4):
            ar_u[chip, k:k + 1, :] = rowsum[k].T[0:1]
        ar_u[chip, lanes:2 * lanes, :] = jnp.zeros((lanes, 128), F32)
        part = lacc[0, 0] + lacc[0, 1] + lacc[1, 0] + lacc[1, 1]
        ar_u[chip, lanes:lanes + 1, :] = jnp.sum(part, axis=0, keepdims=True)
        ar_start(ar_u, 2)

    def delta():
        sums = ar_wait(ar_u, 2)
        mean_g = spread_out(sums, 0, half) / (total_rows * total_rows)
        mean_x = spread_out(sums, lanes // 2, half) / total_rows

        @pl.loop(0, all_tiles)
        def _(i):
            here = row_tile(i)
            v = times_slope(uu[here, :], 1, 1 - xl, here) / total_rows
            v = p_recip * (v - mean_g - pj[here, :] * mean_x)
            sT[:, pl.ds(pl.multiple_of(i * tile, tile), tile)] = v.T.astype(BF16)

        return sums

    strip = gg.shape[2]

    def gradient(h, out):
        @pl.loop(0, nz // 2)
        def _(j):
            here = pl.ds(pl.multiple_of(h * nz * strip + j * 2 * strip, 2 * strip), 2 * strip)
            v = jnp.dot(sT[:, 0:rows], x_ref[:, here], preferred_element_type=F32)
            v = v + jnp.dot(sT[:, rows:2 * rows], xp[:, here], preferred_element_type=F32)
            for k in (0, 1):
                out[2 * j + k] = v[:, k * strip:(k + 1) * strip]

    band, wide_band = ga.shape[4], gb.shape[3]
    split = 2 * band

    def ga_local(i):
        part = slice(i * band, (i + 1) * band)
        return lambda st, p: (gg if st == 0 else gs)[p, part, :]

    def ga_step(s):
        for i in (0, 1):
            ring_step(GRAD, s, ga.at[i], ga_local(i), ga_r.at[i])

    def ga_over():
        for i in (0, 1):
            ring_end(ga.at[i], ga_r.at[i])
            gxs[i] = ring_total(1, ga.at[i], ga_local(i))
            send(GRAD, gxs.at[i], gxr.at[i], gx_r.at[i], x_mate)

    def gb_over():
        for k in range(nz):
            part = gs.at[need_at(k), pl.ds(split, half - split)]
            send(GRAD, part, gr.at[need_at(k)], gy_r.at[(k + 1) // 2], x_mate)

    def gb_wait(s):
        arrived_all(gr, 2 if 0 < s < top else 1, gy_r.at[s])

    def gb_local(st, p):
        low = st * wide_band
        return gg[p, split + low:split + low + wide_band, :] + gr[p, low:low + wide_band, :]

    def gb_step(s):
        gb_wait(s)
        ring_step(GRAD, s, gb, gb_local, gb_r)

    mine = strip // 2
    first = core == 0

    def g_core():
        parts = []
        for i in (0, 1):
            v = ring_total(0, ga.at[i], ga_local(i))
            arrived(gxr.at[i], gx_r.at[i])
            parts.append(v + gxr[i])
        ring_end(gb, gb_r)
        gb_wait(top)
        parts += [ring_total(st, gb, gb_local) for st in (0, 1)]
        v = (LOSS_SCALE * jnp.concatenate(parts, axis=0)).T
        low, high = v[0:mine], v[mine:strip]
        gcs[...] = jnp.where(first, high, low)
        send(LAST, gcs, gcr, gc_r, mate)
        g_ref[:, my_cols] = jnp.where(first, low, high)

    def g_last():
        arrived(gcr, gc_r)
        g_ref[:, mate_cols] = gcr[...]

    t_normal(0, 3)
    t_pass(1)
    correlate(0, 1 - xl)
    cb_over(0)
    correlate(0, xl)
    ca_ring(0)
    nst[f] = ar_wait(ar_n, 5)
    f_start(nst, 6)
    cb_ring(0)
    ca_ring(1)
    t_near(1)
    cb_ring(1)
    ca_ring(2)
    cb_ring(2)
    t_far(1)
    t_normal(1, 1)
    t_normal(1, 2)
    ca_ring(3)
    t_normal(1, 3)
    cb_ring(3)
    correlate(1, 1 - xl)
    cb_over(1)
    correlate(1, xl)
    ca_far(1)
    ca_near(1)
    ca_over(0)
    cb_far(1)
    ca_mid(1)
    f_wait(nst, 6)
    slope(1, 0)
    slope(0, 0)
    slope_go(0, 0)
    cb_mid(1)
    slope_go(1, 0)
    cb_near(1)
    ca_over(1)
    s_ring(0, 1)
    s_ring(1, 1)
    slope(0, 1)
    slope_go(0, 1)
    s_ring(0, 2)
    slope(1, 1)
    slope_go(1, 1)
    u_start()
    s_ring(1, 2)
    sa_other(1)
    s_ring(0, 3)
    sa_on(1)
    s_ring(1, 3)
    sb_on(1, 1)
    s_ring(0, 4)
    sa_on_other(1)
    s_ring(1, 4)
    sb_end(1, 1)
    upstream(True, (0, xl))
    sa_end(1)
    sb_last(0, 0)
    sb_last(1, 0)
    upstream(False, (1, xl), (0, 1 - xl))
    sb_last(1, 1)
    sums = delta()
    gradient(1 - xl, gs)
    gb_over()
    gradient(xl, gg)
    ga_step(0)
    lf[f] = jnp.broadcast_to(jnp.sum(sums[lanes:2 * lanes], axis=0, keepdims=True), (8, 128))
    f_start(lf, 4)
    gb_step(0)
    ga_step(1)
    gb_step(1)
    ga_step(2)
    gb_step(2)
    ga_step(3)
    gb_step(3)
    f_wait(lf, 4)
    lc[0] = jnp.sum(lf[...], axis=0)
    copy(lc.at[0], lc.at[1], ar_s.at[7], lc_r, mate).start()
    ga_over()
    g_core()
    arrived(lc.at[1], lc_r)
    loss_ref[0, 0] = jnp.sum((lc[0] + lc[1])[0:1]) / width_all
    g_last()
    ar_sent(ar_t, 0, chips)
    ar_sent(ar_p, 1, chips)
    ar_sent(ar_u, 2, chips)
    ar_sent(ar_n, 5, chips)
    ar_sent(nst, 6, feats)
    ar_sent(tst, 3, feats)
    ar_sent(lf, 4, feats)
    copy(lc.at[0], lc.at[1], ar_s.at[7], lc_r, mate).wait_send()
    for kind, size in weigh.items():
        there = pj if kind in (WEIGHT, LAST) else tn
        line = there.dtype.itemsize
        for n in there.shape[:-2] + there.shape[-1:]:
            line *= n
        assert size % line == 0 and size // line % 16 == 0
        there = there.at[(slice(None),) * (len(there.shape) - 2) + (pl.ds(0, size // line),)]
        copy(there, there, out_s.at[kind], lc_r, mate).wait_send()


def shards(nz, ny, student, weight, teacher):
    rows, wide = student.shape
    strip_w, cols = weight.shape
    half = cols // 2
    spans = ((ny + 1) * cols // 2, (ny - 1) * cols // 2)
    chips, feats = 2 * nz, 2 * ny
    strip = wide // chips
    quarter = half // 2
    piece = quarter // nz
    band = 7 * half // 32
    V = pltpu.VMEM
    D = pltpu.SemaphoreType.DMA
    data = [
        V((rows, wide), BF16),
        V((2, ny, 2, rows, cols), BF16),
        V((2, ny, 2 * rows, cols), BF16),
        V((2, 2, rows // 4, cols), BF16),
        V((rows, wide), BF16),
        V((2, nz, 2, strip_w, half), BF16),
        V((2 * rows, half), F32),
        V((half, 2 * rows), BF16),
        *[V((2, half, n), F32) for n in spans],
        V((2, nz // 2 + 1, 2, piece, spans[0]), BF16),
        V((2, 7, 3, piece, spans[1]), BF16),
        V((2, nz // 2 + 1, 2, piece, spans[0] // 2), BF16),
        V((2, 7, 3, piece, spans[1] // 2), BF16),
        *[V((piece, n), BF16) for n in spans],
        *[V((piece, n), BF16) for n in spans],
        *[V((nz, piece, n), BF16) for n in spans],
        *[V((nz, piece, n), BF16) for n in spans],
        *[V((2, 2, nz, piece, n), BF16) for n in spans],
        V((2 * rows, half), F32),
        V((nz, half, strip), F32),
        V((nz, half, strip), F32),
        V((nz, half - 2 * band, strip), F32),
        V((2, 2, nz // 2 + 1, 2, band, strip), F32),
        V((2, nz // 2 + 1, 2, half // 2 - band, strip), F32),
        V((2, band, strip), F32),
        V((2, band, strip), F32),
        V((strip // 2, half), F32),
        V((strip // 2, half), F32),
        V((chips, 8, 128), F32),
        V((chips, 8, 128), F32),
        V((chips, 8, 128), F32),
        V((chips, 8, 128), F32),
        V((feats, 8, 128), F32),
        V((feats, 8, 128), F32),
        V((4, 128, 128), F32),
        V((2, 2, 8, 128), F32),
        V((feats, 8, 128), F32),
        V((2, 8, 128), F32),
    ]
    sems = [
        D(shape) for shape in (
            (7,), (3,), (8,), (7,),
            (2, ny), (2, 2), (), (2, 5), (), (), (), (2, 4),
            (2, 2, nz // 2), (2,), (2, 2, nz // 2), (2, 5),
            (), (2, 4), (2, 2, nz // 2), (4,), (2, 2),
            (2, 2, nz // 2), (2,), (5,), (2, nz // 2), (), (),
        )
    ]
    vm = pl.BlockSpec(memory_space=pltpu.VMEM)
    sm = pl.BlockSpec(memory_space=pltpu.SMEM)
    far = pl.BlockSpec(memory_space=pl.ANY)
    loss, grad = pl.pallas_call(
        functools.partial(kernel, nz, ny),
        out_shape=(
            jax.ShapeDtypeStruct((1, 1), F32),
            jax.ShapeDtypeStruct((strip_w, cols), F32),
        ),
        in_specs=[far] * 3,
        out_specs=(sm, vm),
        scratch_shapes=data + sems,
        compiler_params=pltpu.CompilerParams(
            collective_id=0, has_side_effects=True, vmem_limit_bytes=56 * 1024 * 1024
        ),
    )(student, weight, teacher)
    return loss.reshape(()), grad


def solution(mesh):
    placed = (P("dp", None), P("dp", "feat"), P("dp", "feat"))
    nz, ny = mesh.shape["dp"] // 4, mesh.shape["feat"] // 2
    return jax.shard_map(
        functools.partial(shards, nz, ny), mesh=mesh, in_specs=placed,
        out_specs=(P(), P("dp", "feat")), check_vma=False,
    )
```

```python
import functools

import jax
import jax.numpy as jnp
from jax import lax
from jax.experimental import pallas as pl
from jax.experimental.pallas import tpu as pltpu
from jax.sharding import PartitionSpec as P

OFF_WEIGHT = 0.5
NORM_EPS = 1e-05
LOSS_SCALE = 128.0
F32 = jnp.float32
BF16 = jnp.bfloat16
MESH = pl.DeviceIdType.MESH


def around(at, n):
    return lax.rem(at + n, n)


def kernel(
    nz, ny, x_hbm, w_hbm, t_hbm, loss_ref, g_ref,
    x_ref, tb, tn, rl, xp, wb, pj, sT,
    cc0, cc1, ca0, ca1, cb0, cb1, xs0, xs1, xr0, xr1, bs0, bs1, br0, br1, sl0, sl1, uu, gg, gs, gr, ga, gb, gxs, gxr, gcs, gcr,
    ar_t, ar_p, ar_u, ar_n, tst, nst, rowsum, lacc, lf, lc,
    out_s, in_s, ar_s, ar_r, tc_r, tx_r, to_r, ty_r, xc_r, wc_r, wx_r, wz_r,
    ca_r, cx_r, cb_r, bx_r, sx_r, sz_r, sr_r, sb_r, sy_r, ga_r, gx_r, gy_r, gb_r, gc_r, lc_r,
):
    cc, ca, cb, xs = (cc0, cc1), (ca0, ca1), (cb0, cb1), (xs0, xs1)
    xr, bs, br, sl = (xr0, xr1), (bs0, bs1), (br0, br1), (sl0, sl1)
    d = lax.axis_index("dp")
    f = lax.axis_index("feat")
    chips = 2 * nz
    feats = 2 * ny
    core = lax.rem(d, 2)
    chip = lax.div(d, 2)
    z = lax.rem(chip, nz)
    xl = lax.div(chip, nz)
    y = lax.rem(f, ny)
    xh = lax.div(f, ny)
    rows = x_ref.shape[0]
    cols = w_hbm.shape[1]
    half = cols // 2
    total_rows = float(rows * 2 * chips)
    width_all = cols * feats

    mate = (d + 1 - 2 * core, f)

    def dp_at(chip_at):
        return (chip_at * 2 + core, f)

    def z_at(at):
        return dp_at(xl * nz + at)

    def y_at(at):
        return (d, xh * ny + at)

    x_mate = dp_at((1 - xl) * nz + z)
    cross = ((1 - xl) * nz + z) * 2 + core
    x_diag = (cross, (1 - xh) * ny + y)
    x_next = (cross, jnp.where(xl == 0, xh, 1 - xh) * ny + y)
    x_prev = (cross, jnp.where(xl == 0, 1 - xh, xh) * ny + y)

    weigh = {}
    CHIP, WEIGHT, TEACH, CROSS, CORR, GRAD, LAST = range(7)

    def copy(src, dst, s, r, to):
        return pltpu.make_async_remote_copy(
            src_ref=src, dst_ref=dst, send_sem=s, recv_sem=r, device_id=to, device_id_type=MESH
        )

    def send(kind, src, dst, r, to):
        copy(src, dst, out_s.at[kind], r, to).start()
        size = src.dtype.itemsize
        for n in src.shape:
            size *= n
        weigh[kind] = weigh.get(kind, 0) + size

    def arrived(dst, r):
        copy(dst, dst, out_s.at[0], r, mate).wait_recv()

    top = nz // 2

    def hop(k):
        return z_at(around(z + k, nz))

    def arrived_all(ref, n, r):
        arrived(ref.at[pl.ds(0, n)], r)

    def ag_go(kind, slot, rs):
        for k, r in ((2, 2), (-2, 3), (1, 0), (-1, 0)):
            send(kind, slot(z), slot(z), rs.at[r], hop(k))

    def ag_on(kind, slot, rs, far=None):
        for dr in (0, 1):
            sgn = 1 - 2 * dr
            block = slot(around(z - 2 * sgn, nz))
            arrived(block, rs.at[2 + dr])
            if far is None:
                side = block.shape[-1] // 2
                part = block.at[:, pl.ds(dr * side, side)]
                send(kind, part, part, rs.at[1], hop(2 * sgn))
            elif far == dr:
                send(kind, block, block, rs.at[1], hop(2 * sgn))
            send(kind, block, block, rs.at[1], hop(sgn))

    def ag_end(like, rs):
        arrived_all(like, 2, rs.at[0])
        arrived_all(like, 3, rs.at[1])

    def agx_to(kind, slot, xr, offs):
        for off in offs:
            block = slot(around(z + off, nz))
            send(kind, block, block, xr, x_mate)

    def agx_go(kind, slot, rs, xr):
        ag_go(kind, slot, rs)
        agx_to(kind, slot, xr, (0,))

    def agx_on(kind, slot, rs, xr, like):
        ag_on(kind, slot, rs)
        agx_to(kind, slot, xr, (-2, 2))
        arrived_all(like, 2, rs.at[0])
        agx_to(kind, slot, xr, (-1, 1))

    def agx_end(kind, slot, rs, xr, like):
        arrived_all(like, 3, rs.at[1])
        agx_to(kind, slot, xr, (-3, 3, top))

    def far_step(kind, buf, local, rs):
        for dr in (0, 1):
            buf[dr, 2, 0] = local(dr, around(z + top, nz)).astype(buf.dtype)
            send(kind, buf.at[dr, 2, 0], buf.at[dr, 1, 0], rs.at[dr], hop(2 - 4 * dr))
        for dr in (0, 1):
            sgn = 1 - 2 * dr
            for st in (0, 1):
                buf[dr, 0, st] = local(st, around(z + 3 * sgn, nz)).astype(buf.dtype)
            send(kind, buf.at[dr, 0, pl.ds(0, 2)], buf.at[dr, 1, pl.ds(1, 2)], rs.at[dr], hop(sgn))

    def mid_step(kind, buf, local, rs):
        for dr in (0, 1):
            sgn = 1 - 2 * dr
            arrived(buf.at[dr, 1], rs.at[dr])
            for st in (0, 1):
                v = local(st, around(z + 2 * sgn, nz)) + buf[dr, 1, 1 + st].astype(F32)
                if st == dr:
                    v = v + buf[dr, 1, 0].astype(F32)
                buf[dr, 3, st] = v.astype(buf.dtype)
            send(kind, buf.at[dr, 3, pl.ds(0, 2)], buf.at[dr, 4, pl.ds(0, 2)], rs.at[2], hop(2 * sgn))

    def near_step(kind, buf, local, rs):
        for dr in (0, 1):
            sgn = 1 - 2 * dr
            for st in (0, 1):
                buf[dr, 6, st] = local(st, around(z + sgn, nz)).astype(buf.dtype)
            send(kind, buf.at[dr, 6, pl.ds(0, 2)], buf.at[dr, 5, pl.ds(0, 2)], rs.at[2], hop(sgn))

    def sum_end(buf, rs):
        arrived(buf.at[:, pl.ds(4, 2), pl.ds(0, 2)], rs.at[2])

    def sum_total(st, buf, local):
        v = local(st, z)
        for dr in (0, 1):
            v = v + buf[dr, 4, st].astype(F32) + buf[dr, 5, st].astype(F32)
        return v

    def ring_step(kind, s, buf, local, rs):
        for dr in (0, 1):
            sgn = 1 - 2 * dr
            p = around(z + sgn * (top - s), nz)
            if s == 1:
                arrived(buf.at[dr, s, dr], rs.at[dr, s - 1])
            elif s > 1:
                arrived(buf.at[dr, s], rs.at[dr, s - 1])
            for st in (dr,) if s == 0 else (0, 1):
                v = local(st, p)
                if s > 1 or (s == 1 and st == dr):
                    v = v + buf[dr, s, st].astype(F32)
                buf[dr, s, st] = v.astype(buf.dtype)
            if s == 0:
                send(kind, buf.at[dr, 0, dr], buf.at[dr, 1, dr], rs.at[dr, 0], hop(sgn))
            else:
                send(kind, buf.at[dr, s], buf.at[dr, s + 1], rs.at[dr, s], hop(sgn))

    def ring_end(buf, rs):
        for dr in (0, 1):
            arrived(buf.at[dr, top], rs.at[dr, top - 1])

    def ring_total(st, buf, local):
        return local(st, z) + buf[0, top, st].astype(F32) + buf[1, top, st].astype(F32)

    need = [top, 3, -3, 2, -2, 1, -1, 0]

    def need_at(k):
        return around(z + need[k], nz)

    def x_group(k):
        return (0, 0, 0, 1, 1, 2, 2, 3)[k]

    def x_wait(i, dst, rs):
        arrived_all(dst, (3, 2, 2, 1)[i], rs.at[i])

    def ar_copy(buf, i, k):
        return copy(buf.at[chip], buf.at[chip], ar_s.at[i], ar_r.at[i], dp_at(around(chip + k, chips)))

    def ar_start(buf, i):
        for k in range(1, chips):
            ar_copy(buf, i, k).start()

    def ar_wait(buf, i):
        arrived(buf.at[pl.ds(0, chips - 1)], ar_r.at[i])
        return jnp.sum(buf[...], axis=0)

    def ar_sent(buf, i, n):
        there = buf.at[pl.ds(0, n - 1)]
        copy(there, there, ar_s.at[i], ar_r.at[i], mate).wait_send()

    def f_start(buf, i):
        @pl.loop(1, feats)
        def _(k):
            copy(buf.at[f], buf.at[f], ar_s.at[i], ar_r.at[i], (d, around(f + k, feats))).start()

    def f_wait(buf, i):
        arrived(buf.at[pl.ds(0, feats - 1)], ar_r.at[i])

    lanes = cols // 128

    def pack(buf, at, row, v):
        for k in range(v.shape[1] // 128):
            buf[at, row + k:row + k + 1, :] = v[:, k * 128:(k + 1) * 128]

    def spread_out(v, row, n):
        return jnp.concatenate([v[row + k:row + k + 1, :] for k in range(n // 128)], axis=1)

    def norm_of(sums, squares):
        center = sums / total_rows
        spread = squares / total_rows - center * center
        return center, lax.rsqrt(spread + NORM_EPS)

    barrier = pltpu.get_barrier_semaphore()

    def greet(to):
        pl.semaphore_signal(barrier, inc=1, device_id=to, device_id_type=MESH)

    greet(mate)
    greet(x_diag)

    @pl.loop(1, feats)
    def _(k):
        greet((d, around(f + k, feats)))

    @pl.loop(1, chips)
    def _(k):
        greet(dp_at(around(chip + k, chips)))

    my_cols = pl.ds(pl.multiple_of(core * half, half), half)
    mate_cols = pl.ds(pl.multiple_of((1 - core) * half, half), half)
    w_in = pltpu.make_async_copy(w_hbm.at[:, my_cols], wb.at[xl, z, core], in_s.at[0])
    t_in = pltpu.make_async_copy(t_hbm, tb.at[0, y, 0], in_s.at[1])
    x_in = pltpu.make_async_copy(x_hbm, x_ref, in_s.at[2])
    w_in.start()
    t_in.start()
    x_in.start()
    rowsum[...] = jnp.zeros_like(rowsum)
    pl.semaphore_wait(barrier, feats + chips)

    send(WEIGHT, w_hbm.at[:, mate_cols], wb.at[xl, z, core], wc_r, mate)
    send(TEACH, t_hbm, tb.at[0, y, 1], tc_r.at[0, 0], mate)

    mid = rows // 2
    right, left = y_at(around(y + 1, ny)), y_at(around(y - 1, ny))
    offs = (0, -1, 1, 2)

    def t_at(st, e):
        return tb.at[st, around(y + offs[e], ny), 0]

    def t_hand(st, e):
        send(TEACH, t_at(st, e), tb.at[st, around(y + offs[e], ny), 1], tc_r.at[st, e], mate)

    high, low = pl.ds(0, mid), pl.ds(mid, mid)

    def t_round(st, src):
        there = t_at(st, 0)
        send(TEACH, src.at[high], there.at[high], ty_r.at[st, 0], right)
        send(TEACH, src.at[low], there.at[low], ty_r.at[st, 1], left)
        send(TEACH, src.at[low], there.at[low], ty_r.at[st, 3], right)
        send(TEACH, src.at[high], there.at[high], ty_r.at[st, 4], left)

    def t_pass(st):
        for e, part, to in ((1, high, right), (2, low, left)):
            part = t_at(st, e).at[part]
            arrived(part, ty_r.at[st, e - 1])
            send(TEACH, part, part, ty_r.at[st, 2], to)

    def t_near(st):
        for e, part in ((1, low), (2, high)):
            arrived(t_at(st, e).at[part], ty_r.at[st, e + 2])
            t_hand(st, e)

    def t_far(st):
        arrived(t_at(st, 3), ty_r.at[st, 2])
        t_hand(st, 3)

    quad = rows // 4
    ways = (x_next, x_prev)

    def t_cross(i):
        for dr in (0, 1):
            part = t_hbm.at[pl.ds((2 * dr + i) * quad, quad)]
            send(CROSS, part, rl.at[dr, i], tx_r.at[dr, i], ways[dr])

    def t_relay(i):
        for dr in (0, 1):
            arrived(rl.at[dr, i], tx_r.at[dr, i])
            there = t_at(1, 0).at[pl.ds((2 * dr + i) * quad, quad)]
            send(CROSS, rl.at[dr, i], there, to_r, ways[dr])

    def t_over():
        arrived(t_at(1, 0), to_r)
        t_round(1, t_at(1, 0))
        t_hand(1, 0)

    t_round(0, t_hbm)
    send(CHIP, x_hbm, xp, xc_r, mate)

    def t_normal(st, e, wait_mate=True):
        p = around(y + offs[e], ny)
        if wait_mate:
            arrived(tb.at[st, p, 1], tc_r.at[st, e])
        at = (xh if st == 0 else 1 - xh) * ny + p
        center = spread_out(tst[at], 0, cols)
        recip = spread_out(tst[at], lanes, cols)
        for slot in (0, 1):

            @pl.loop(0, rows // 64)
            def _(i):
                here = pl.multiple_of(i * 64, 64)
                v = tb[st, p, slot, pl.ds(here, 64), :].astype(F32)
                there = pl.multiple_of(slot * rows + i * 64, 64)
                tn[st, p, pl.ds(there, 64), :] = ((v - center) * recip).astype(BF16)

    def w_own(p):
        return wb.at[xl, p]

    def w_other(p):
        return wb.at[1 - xl, p]

    w_in.wait()
    arrived(wb.at[xl, z, 1 - core], wc_r)
    send(WEIGHT, w_own(z), w_own(z), wx_r, x_mate)
    ag_go(WEIGHT, w_own, wz_r.at[0])
    t_cross(0)
    t_cross(1)

    t_in.wait()
    arrived(tb.at[0, y, 1], tc_r.at[0, 0])

    def t_sum(i, carry):
        a, b = carry
        for slot in (0, 1):
            v = tb[0, y, slot, pl.ds(pl.multiple_of(i * 64, 64), 64), :].astype(F32).reshape(8, 8, cols)
            a = a + jnp.sum(v, axis=0)
            b = b + jnp.sum(v * v, axis=0)
        return a, b

    zero = jnp.zeros((8, cols), F32)
    a, b = lax.fori_loop(0, rows // 64, t_sum, (zero, zero))
    pack(ar_t, chip, 0, jnp.sum(a, axis=0, keepdims=True))
    pack(ar_t, chip, lanes, jnp.sum(b, axis=0, keepdims=True))
    ar_start(ar_t, 0)

    arrived(w_other(z), wx_r)
    ag_go(WEIGHT, w_other, wz_r.at[1])
    t_relay(0)
    ag_on(WEIGHT, w_own, wz_r.at[0], 0)
    t_pass(0)
    t_relay(1)
    ag_on(WEIGHT, w_other, wz_r.at[1], 1)
    sums = ar_wait(ar_t, 0)
    center, recip = norm_of(sums[0:lanes], sums[lanes:2 * lanes])
    tst[f, 0:lanes, :] = center
    tst[f, lanes:2 * lanes, :] = recip
    f_start(tst, 3)
    t_near(0)

    ag_end(wb.at[xl], wz_r.at[0])
    x_in.wait()
    arrived(xp, xc_r)
    t_over()
    wide = wb.shape[1] * wb.shape[2] * wb.shape[3]
    tile = min(256, rows)
    tiles = rows // tile
    narrow = jnp.zeros((8, half), F32)

    def project(ref, base, h, last):
        deep = pl.ds(pl.multiple_of(h * wide, wide), wide)

        def body(i, carry):
            here = pl.ds(pl.multiple_of(i * tile, tile), tile)
            there = pl.ds(pl.multiple_of(base + i * tile, tile), tile)
            v = jnp.dot(ref[here, deep], wb[h].reshape(wide, half), preferred_element_type=F32)
            if last:
                v = v + pj[there, :]
            pj[there, :] = v
            if not last:
                return carry
            v = v.reshape(tile // 8, 8, half)
            return carry[0] + jnp.sum(v, axis=0), carry[1] + jnp.sum(v * v, axis=0)

        return body

    lax.fori_loop(0, tiles, project(x_ref, 0, xl, False), 0)
    lax.fori_loop(0, tiles, project(xp, rows, xl, False), 0)
    ag_end(wb.at[1 - xl], wz_r.at[1])
    carry = lax.fori_loop(0, tiles, project(x_ref, 0, 1 - xl, True), (narrow, narrow))
    a, b = lax.fori_loop(0, tiles, project(xp, rows, 1 - xl, True), carry)
    ar_p[chip] = jnp.zeros((8, 128), F32)
    pack(ar_p, chip, 0, jnp.sum(a, axis=0, keepdims=True))
    pack(ar_p, chip, lanes // 2, jnp.sum(b, axis=0, keepdims=True))
    ar_start(ar_p, 1)
    t_far(0)
    f_wait(tst, 3)
    t_normal(0, 0, wait_mate=False)

    def n_sum(i, total):
        v = tn[0, y, pl.ds(pl.multiple_of(i * 64, 64), 64), :].astype(F32)
        return total + jnp.sum(v.reshape(8, 8, cols), axis=0)

    n_sums = lax.fori_loop(0, 2 * rows // 64, n_sum, zero)
    ar_n[chip] = jnp.zeros((8, 128), F32)
    pack(ar_n, chip, 0, jnp.sum(n_sums, axis=0, keepdims=True))
    ar_start(ar_n, 5)
    t_normal(0, 1)
    t_normal(0, 2)

    t_normal(1, 0)
    t_normal(0, 3)
    sums = ar_wait(ar_p, 1)
    p_center, p_recip = norm_of(spread_out(sums, 0, half), spread_out(sums, lanes // 2, half))
    all_tiles = 2 * tiles
    for i in range(all_tiles):
        v = (pj[i * tile:(i + 1) * tile, :] - p_center) * p_recip
        pj[i * tile:(i + 1) * tile, :] = v
        sT[:, i * tile:(i + 1) * tile] = v.T.astype(BF16)

    def half_cols(h):
        return pl.ds(pl.multiple_of(h * half, half), half)

    def correlate(g, h):
        def block(ref, at, n):
            cc[g][h, :, at:at + n] = jnp.dot(sT[...], ref, preferred_element_type=F32)

        if g == 0:
            for j in range(ny // 2):
                block(tn[0, h * (ny // 2) + j], j * cols, cols)
            block(tn[1, y, :, half_cols(h)], ny // 2 * cols, half)
        else:
            block(tn[1, around(y - 1 + 2 * h, ny)], 0, cols)
            block(tn[1, around(y + 2, ny), :, half_cols(h)], cols, half)

    quarter = half // 2
    piece = quarter // nz

    def rows_of(a, p):
        return pl.ds(pl.multiple_of(a * quarter + p * piece, piece), piece)

    def sides(g, st):
        side = cc[g].shape[2] // 2
        return slice(st * side, (st + 1) * side)

    def ca_local(g):
        return lambda st, p: cc[g][xl if st == 0 else 1 - xl, rows_of(0, p), :]

    def ca_far(g):
        far_step(CORR, ca[g], ca_local(g), ca_r.at[g, 0])

    def ca_mid(g):
        mid_step(CORR, ca[g], ca_local(g), ca_r.at[g, 0])

    def ca_near(g):
        near_step(CORR, ca[g], ca_local(g), ca_r.at[g, 0])

    def ca_ring(s):
        ring_step(CORR, s, ca[0], ca_local(0), ca_r.at[0])

    def ca_total(g, st):
        return (ring_total, sum_total)[g](st, ca[g], ca_local(g))

    def ca_over(g):
        (ring_end, sum_end)[g](ca[g], (ca_r.at[0], ca_r.at[1, 0])[g])
        xs[g][...] = ca_total(g, 1).astype(BF16)
        send(CORR, xs[g], xr[g], cx_r.at[g], x_mate)

    def cb_over(g):
        bs[g][...] = cc[g][1 - xl, quarter:half, :].astype(BF16).reshape(bs[g].shape)
        for k in range(nz):
            send(CORR, bs[g].at[need_at(k)], br[g].at[need_at(k)], bx_r.at[g, (k + 1) // 2 if g == 0 else x_group(k)], x_mate)

    def cb_local(g):
        return lambda st, p: cc[g][xl, rows_of(1, p), sides(g, st)] + br[g][p, :, sides(g, st)].astype(F32)

    def cb_ring(s):
        arrived_all(br[0], 2 if 0 < s < top else 1, bx_r.at[0, s])
        if s < top:
            ring_step(CORR, s, cb[0], cb_local(0), cb_r.at[0])

    def cb_total(g, st):
        return (ring_total, sum_total)[g](st, cb[g], cb_local(g))

    def cb_far(g):
        x_wait(0, br[g], bx_r.at[g])
        far_step(CORR, cb[g], cb_local(g), cb_r.at[g, 0])

    def cb_mid(g):
        x_wait(1, br[g], bx_r.at[g])
        mid_step(CORR, cb[g], cb_local(g), cb_r.at[g, 0])

    def cb_near(g):
        x_wait(2, br[g], bx_r.at[g])
        near_step(CORR, cb[g], cb_local(g), cb_r.at[g, 0])

    def slope(a, g):
        if a == 0:
            v = ca_total(g, 0)
            arrived(xr[g], cx_r.at[g])
            v = v + xr[g][...].astype(F32)
        else:
            (ring_end, sum_end)[g](cb[g], (cb_r.at[0], cb_r.at[1, 0])[g])
            if g == 0:
                cb_ring(top)
            else:
                x_wait(3, br[g], bx_r.at[g])
            v = jnp.concatenate([cb_total(g, st) for st in (0, 1)], axis=1)
        share = v / total_rows
        student_index = (
            f * cols + core * half + a * quarter + z * piece
            + lax.broadcasted_iota(jnp.int32, share.shape, 0)
        )
        col = lax.broadcasted_iota(jnp.int32, share.shape, 1)
        whole = ny // 2 * cols
        teacher_index = jnp.where(col < whole, (xh * 2 + xl) * whole + col, -1) if g == 0 else -1 - col
        on_diag = student_index == teacher_index
        part = jnp.where(on_diag, (1.0 - share) ** 2, OFF_WEIGHT * share * share)
        part = jnp.sum(part.reshape(piece // 8, 8, part.shape[1]), axis=0)
        lacc[g, a] = sum(part[:, k:k + 128] for k in range(0, part.shape[1], 128))
        lean = jnp.where(on_diag, -2.0 * (1.0 - share), 2.0 * OFF_WEIGHT * share).astype(BF16)
        sl[g][xl, a, z] = lean
        lean = lean.astype(F32)
        other = (1 - xh) * ny
        if g == 0:
            at = xh * ny + xl * (ny // 2)
            blocks, last = [at + k for k in range(ny // 2)], other + y
        else:
            blocks, last = [other + around(y - 1 + 2 * xl, ny)], other + around(y + 2, ny)
        n_row = [spread_out(nst[b], 0, cols) for b in blocks]
        last = spread_out(nst[last], 0, cols)
        n_row.append(jnp.where(xl == 0, last[:, 0:half], last[:, half:cols]))
        n_row = jnp.concatenate(n_row, axis=1)
        here = pl.ds(pl.multiple_of(z * piece, piece), piece)
        for k, v in ((a, lean * n_row), (2 + a, lean * share)):
            v = jnp.broadcast_to(jnp.sum(v, axis=1, keepdims=True), (piece, 128))
            rowsum[k, here, :] = v if g == 0 else rowsum[k, here, :] + v

    def slope_go(a, g):
        if (a, g) == (0, 1):
            there = sl[g].at[xl, 0, z]
            send(CORR, there, there, sx_r, x_mate)
            ag_go(CORR, sa_own(g), sz_r.at[0])
        else:
            if g == 0:
                s_ring(a, 0)
            else:
                agx_go(CORR, sb_own(a, g), sb_r, sy_r.at[g, a])

    def s_ring(a, s):
        own = sb_own(a, 0)
        side = sl[0].shape[-1] // 2
        if s == 0:
            agx_to(CORR, own, sy_r.at[0, a], (0,))
        for dr in (0, 1):
            sgn = 1 - 2 * dr
            block = own(around(z - sgn * s, nz))
            half_of = block.at[:, pl.ds(dr * side, side)]
            if s > 0:
                arrived(block if s < top else half_of, sr_r.at[a, dr, s - 1])
            if s < top:
                part = block if s < top - 1 else half_of
                send(CORR, part, part, sr_r.at[a, dr, s], hop(sgn))
        if s > 0:
            agx_to(CORR, own, sy_r.at[0, a], (-s, s) if s < top else (top,))

    def sa_own(g):
        return lambda p: sl[g].at[xl, 0, p]

    def sa_mate(g):
        return lambda p: sl[g].at[1 - xl, 0, p]

    def sb_own(a, g):
        return lambda p: sl[g].at[xl, a, p]

    def sa_other(g):
        arrived(sl[g].at[1 - xl, 0, z], sx_r)
        ag_go(CORR, sa_mate(g), sz_r.at[1])

    def sa_on(g):
        ag_on(CORR, sa_own(g), sz_r.at[0], 0)

    def sa_on_other(g):
        ag_on(CORR, sa_mate(g), sz_r.at[1], 1)

    def sa_end(g):
        ag_end(sl[g].at[0, 0], sz_r.at[0])
        ag_end(sl[g].at[0, 0], sz_r.at[1])

    def sb_on(a, g):
        agx_on(CORR, sb_own(a, g), sb_r, sy_r.at[g, a], sl[g].at[xl, a])

    def sb_end(a, g):
        agx_end(CORR, sb_own(a, g), sb_r, sy_r.at[g, a], sl[g].at[xl, a])

    def sb_last(a, g):
        arrived(sl[g].at[1 - xl, a], sy_r.at[g, a])

    def row_tile(i):
        return pl.ds(pl.multiple_of(i * tile, tile), tile)

    def times_slope(v, g, h, here):
        if g == 0:
            terms = [(tn[0, h * (ny // 2) + j, here, :], j * cols, cols) for j in range(ny // 2)]
            terms.append((tn[1, y, here, half_cols(h)], ny // 2 * cols, half))
        else:
            terms = [(tn[1, around(y - 1 + 2 * h, ny), here, :], 0, cols)]
            terms.append((tn[1, around(y + 2, ny), here, half_cols(h)], cols, half))
        for lhs, at, n in terms:
            rhs = sl[g][h, :, :, :, at:at + n].reshape(half, n)
            w = lax.dot_general(lhs, rhs, (((1,), (1,)), ((), ())), preferred_element_type=F32)
            v = w if v is None else v + w
        return v

    def upstream(*parts):
        @pl.loop(0, all_tiles)
        def _(i):
            v = None
            for g, h in parts:
                v = times_slope(v, g, h, row_tile(i))
            uu[row_tile(i), :] = v

    def u_start():
        for k in range(4):
            ar_u[chip, k:k + 1, :] = rowsum[k].T[0:1]
        ar_u[chip, lanes:2 * lanes, :] = jnp.zeros((lanes, 128), F32)
        part = lacc[0, 0] + lacc[0, 1] + lacc[1, 0] + lacc[1, 1]
        ar_u[chip, lanes:lanes + 1, :] = jnp.sum(part, axis=0, keepdims=True)
        ar_start(ar_u, 2)

    def delta():
        sums = ar_wait(ar_u, 2)
        mean_g = spread_out(sums, 0, half) / (total_rows * total_rows)
        mean_x = spread_out(sums, lanes // 2, half) / total_rows

        @pl.loop(0, all_tiles)
        def _(i):
            here = row_tile(i)
            v = times_slope(uu[here, :], 0, 1 - xl, here)
            v = times_slope(v, 1, 1 - xl, here) / total_rows
            v = p_recip * (v - mean_g - pj[here, :] * mean_x)
            sT[:, pl.ds(pl.multiple_of(i * tile, tile), tile)] = v.T.astype(BF16)

        return sums

    strip = gg.shape[2]

    def gradient(h, out, *pairs):
        @pl.loop(*pairs)
        def _(j):
            j = lax.rem(lax.div(z, 2) + top // 2 + j, nz // 2)
            here = pl.ds(pl.multiple_of(h * nz * strip + j * 2 * strip, 2 * strip), 2 * strip)
            v = jnp.dot(sT[:, 0:rows], x_ref[:, here], preferred_element_type=F32)
            v = v + jnp.dot(sT[:, rows:2 * rows], xp[:, here], preferred_element_type=F32)
            for k in (0, 1):
                out[2 * j + k] = v[:, k * strip:(k + 1) * strip]

    band, wide_band = ga.shape[4], gb.shape[3]
    split = 2 * band

    def ga_local(i):
        part = slice(i * band, (i + 1) * band)
        return lambda st, p: (gg if st == 0 else gs)[p, part, :]

    def ga_step(s):
        for i in (0, 1):
            ring_step(GRAD, s, ga.at[i], ga_local(i), ga_r.at[i])

    def ga_over():
        for i in (0, 1):
            ring_end(ga.at[i], ga_r.at[i])
            gxs[i] = ring_total(1, ga.at[i], ga_local(i))
            send(GRAD, gxs.at[i], gxr.at[i], gx_r.at[i], x_mate)

    def gb_over(*ks):
        for k in ks:
            part = gs.at[need_at(k), pl.ds(split, half - split)]
            send(GRAD, part, gr.at[need_at(k)], gy_r.at[(k + 1) // 2], x_mate)

    def gb_wait(s):
        arrived_all(gr, 2 if 0 < s < top else 1, gy_r.at[s])

    def gb_local(st, p):
        low = st * wide_band
        return gg[p, split + low:split + low + wide_band, :] + gr[p, low:low + wide_band, :]

    def gb_step(s):
        gb_wait(s)
        ring_step(GRAD, s, gb, gb_local, gb_r)

    mine = strip // 2
    first = core == 0

    def g_core():
        parts = []
        for i in (0, 1):
            v = ring_total(0, ga.at[i], ga_local(i))
            arrived(gxr.at[i], gx_r.at[i])
            parts.append(v + gxr[i])
        ring_end(gb, gb_r)
        gb_wait(top)
        parts += [ring_total(st, gb, gb_local) for st in (0, 1)]
        v = (LOSS_SCALE * jnp.concatenate(parts, axis=0)).T
        low, high = v[0:mine], v[mine:strip]
        gcs[...] = jnp.where(first, high, low)
        send(LAST, gcs, gcr, gc_r, mate)
        g_ref[:, my_cols] = jnp.where(first, low, high)

    def g_last():
        arrived(gcr, gc_r)
        g_ref[:, mate_cols] = gcr[...]

    t_pass(1)
    correlate(0, 1 - xl)
    cb_over(0)
    correlate(0, xl)
    ca_ring(0)
    nst[f] = ar_wait(ar_n, 5)
    f_start(nst, 6)
    cb_ring(0)
    ca_ring(1)
    t_near(1)
    cb_ring(1)
    ca_ring(2)
    t_far(1)
    cb_ring(2)
    t_normal(1, 1)
    t_normal(1, 2)
    ca_ring(3)
    t_normal(1, 3)
    correlate(1, 1 - xl)
    cb_over(1)
    correlate(1, xl)
    ca_far(1)
    cb_ring(3)
    ca_near(1)
    ca_over(0)
    cb_far(1)
    ca_mid(1)
    f_wait(nst, 6)
    slope(1, 0)
    slope(0, 0)
    slope_go(0, 0)
    cb_mid(1)
    slope_go(1, 0)
    cb_near(1)
    ca_over(1)
    s_ring(0, 1)
    s_ring(1, 1)
    slope(0, 1)
    slope_go(0, 1)
    s_ring(0, 2)
    slope(1, 1)
    slope_go(1, 1)
    u_start()
    s_ring(1, 2)
    sa_other(1)
    sa_on(1)
    s_ring(0, 3)
    sb_on(1, 1)
    s_ring(1, 3)
    sa_on_other(1)
    s_ring(0, 4)
    s_ring(1, 4)
    sb_end(1, 1)
    sa_end(1)
    upstream((0, xl), (1, xl))
    sb_last(0, 0)
    sb_last(1, 0)
    sb_last(1, 1)
    sums = delta()
    gradient(1 - xl, gs, 0, 1)
    gb_over(0)
    gradient(xl, gg, 0, 1)
    ga_step(0)
    gradient(1 - xl, gs, 1, nz // 2)
    gb_over(1, 2, 3, 4, 5, 6, 7)
    gradient(xl, gg, 1, nz // 2)
    lf[f] = jnp.broadcast_to(jnp.sum(sums[lanes:2 * lanes], axis=0, keepdims=True), (8, 128))
    f_start(lf, 4)
    gb_step(0)
    ga_step(1)
    gb_step(1)
    ga_step(2)
    gb_step(2)
    ga_step(3)
    gb_step(3)
    f_wait(lf, 4)
    lc[0] = jnp.sum(lf[...], axis=0)
    copy(lc.at[0], lc.at[1], ar_s.at[7], lc_r, mate).start()
    ga_over()
    g_core()
    arrived(lc.at[1], lc_r)
    loss_ref[0, 0] = jnp.sum((lc[0] + lc[1])[0:1]) / width_all
    g_last()
    ar_sent(ar_t, 0, chips)
    ar_sent(ar_p, 1, chips)
    ar_sent(ar_u, 2, chips)
    ar_sent(ar_n, 5, chips)
    ar_sent(nst, 6, feats)
    ar_sent(tst, 3, feats)
    ar_sent(lf, 4, feats)
    copy(lc.at[0], lc.at[1], ar_s.at[7], lc_r, mate).wait_send()
    for kind, size in weigh.items():
        there = pj if kind in (WEIGHT, LAST) else tn
        line = there.dtype.itemsize
        for n in there.shape[:-2] + there.shape[-1:]:
            line *= n
        assert size % line == 0 and size // line % 16 == 0
        there = there.at[(slice(None),) * (len(there.shape) - 2) + (pl.ds(0, size // line),)]
        copy(there, there, out_s.at[kind], lc_r, mate).wait_send()


def shards(nz, ny, student, weight, teacher):
    rows, wide = student.shape
    strip_w, cols = weight.shape
    half = cols // 2
    spans = ((ny + 1) * cols // 2, (ny - 1) * cols // 2)
    chips, feats = 2 * nz, 2 * ny
    strip = wide // chips
    quarter = half // 2
    piece = quarter // nz
    band = 7 * half // 32
    V = pltpu.VMEM
    D = pltpu.SemaphoreType.DMA
    data = [
        V((rows, wide), BF16),
        V((2, ny, 2, rows, cols), BF16),
        V((2, ny, 2 * rows, cols), BF16),
        V((2, 2, rows // 4, cols), BF16),
        V((rows, wide), BF16),
        V((2, nz, 2, strip_w, half), BF16),
        V((2 * rows, half), F32),
        V((half, 2 * rows), BF16),
        *[V((2, half, n), F32) for n in spans],
        V((2, nz // 2 + 1, 2, piece, spans[0]), BF16),
        V((2, 7, 3, piece, spans[1]), BF16),
        V((2, nz // 2 + 1, 2, piece, spans[0] // 2), BF16),
        V((2, 7, 3, piece, spans[1] // 2), BF16),
        *[V((piece, n), BF16) for n in spans],
        *[V((piece, n), BF16) for n in spans],
        *[V((nz, piece, n), BF16) for n in spans],
        *[V((nz, piece, n), BF16) for n in spans],
        *[V((2, 2, nz, piece, n), BF16) for n in spans],
        V((2 * rows, half), F32),
        V((nz, half, strip), F32),
        V((nz, half, strip), F32),
        V((nz, half - 2 * band, strip), F32),
        V((2, 2, nz // 2 + 1, 2, band, strip), F32),
        V((2, nz // 2 + 1, 2, half // 2 - band, strip), F32),
        V((2, band, strip), F32),
        V((2, band, strip), F32),
        V((strip // 2, half), F32),
        V((strip // 2, half), F32),
        V((chips, 8, 128), F32),
        V((chips, 8, 128), F32),
        V((chips, 8, 128), F32),
        V((chips, 8, 128), F32),
        V((feats, 8, 128), F32),
        V((feats, 8, 128), F32),
        V((4, 128, 128), F32),
        V((2, 2, 8, 128), F32),
        V((feats, 8, 128), F32),
        V((2, 8, 128), F32),
    ]
    sems = [
        D(shape) for shape in (
            (7,), (3,), (8,), (7,),
            (2, ny), (2, 2), (), (2, 5), (), (), (), (2, 4),
            (2, 2, nz // 2), (2,), (2, 2, nz // 2), (2, 5),
            (), (2, 4), (2, 2, nz // 2), (4,), (2, 2),
            (2, 2, nz // 2), (2,), (5,), (2, nz // 2), (), (),
        )
    ]
    vm = pl.BlockSpec(memory_space=pltpu.VMEM)
    sm = pl.BlockSpec(memory_space=pltpu.SMEM)
    far = pl.BlockSpec(memory_space=pl.ANY)
    loss, grad = pl.pallas_call(
        functools.partial(kernel, nz, ny),
        out_shape=(
            jax.ShapeDtypeStruct((1, 1), F32),
            jax.ShapeDtypeStruct((strip_w, cols), F32),
        ),
        in_specs=[far] * 3,
        out_specs=(sm, vm),
        scratch_shapes=data + sems,
        compiler_params=pltpu.CompilerParams(
            collective_id=0, has_side_effects=True, vmem_limit_bytes=56 * 1024 * 1024
        ),
    )(student, weight, teacher)
    return loss.reshape(()), grad


def solution(mesh):
    placed = (P("dp", None), P("dp", "feat"), P("dp", "feat"))
    nz, ny = mesh.shape["dp"] // 4, mesh.shape["feat"] // 2
    return jax.shard_map(
        functools.partial(shards, nz, ny), mesh=mesh, in_specs=placed,
        out_specs=(P(), P("dp", "feat")), check_vma=False,
    )
```

```python
import functools

import jax
import jax.numpy as jnp
from jax import lax
from jax.experimental import pallas as pl
from jax.experimental.pallas import tpu as pltpu
from jax.sharding import PartitionSpec as P

OFF_WEIGHT = 0.5
NORM_EPS = 1e-05
LOSS_SCALE = 128.0
F32 = jnp.float32
BF16 = jnp.bfloat16
MESH = pl.DeviceIdType.MESH


def around(at, n):
    return lax.rem(at + n, n)


def kernel(
    nz, ny, x_hbm, w_hbm, t_hbm, loss_ref, g_ref,
    x_ref, tb, tn, rl, xp, wb, pj, sT,
    cc0, cc1, ca0, ca1, cb0, cb1, xs0, xs1, xr0, xr1, bs0, bs1, br0, br1, sl0, sl1, uu, gg, gs, gr, ga, gb, gxs, gxr, gcs, gcr,
    ar_t, ar_p, ar_u, ar_n, tst, nst, rowsum, lacc, lf, lc,
    out_s, in_s, ar_s, ar_r, tc_r, tx_r, to_r, ty_r, xc_r, wc_r, wx_r, wz_r,
    ca_r, cx_r, cb_r, bx_r, sx_r, sz_r, sr_r, sb_r, sy_r, ga_r, gx_r, gy_r, gb_r, gc_r, lc_r,
):
    cc, ca, cb, xs = (cc0, cc1), (ca0, ca1), (cb0, cb1), (xs0, xs1)
    xr, bs, br, sl = (xr0, xr1), (bs0, bs1), (br0, br1), (sl0, sl1)
    d = lax.axis_index("dp")
    f = lax.axis_index("feat")
    chips = 2 * nz
    feats = 2 * ny
    core = lax.rem(d, 2)
    chip = lax.div(d, 2)
    z = lax.rem(chip, nz)
    xl = lax.div(chip, nz)
    y = lax.rem(f, ny)
    xh = lax.div(f, ny)
    rows = x_ref.shape[0]
    cols = w_hbm.shape[1]
    half = cols // 2
    total_rows = float(rows * 2 * chips)
    width_all = cols * feats

    mate = (d + 1 - 2 * core, f)

    def dp_at(chip_at):
        return (chip_at * 2 + core, f)

    def z_at(at):
        return dp_at(xl * nz + at)

    def y_at(at):
        return (d, xh * ny + at)

    x_mate = dp_at((1 - xl) * nz + z)
    cross = ((1 - xl) * nz + z) * 2 + core
    x_diag = (cross, (1 - xh) * ny + y)
    x_next = (cross, jnp.where(xl == 0, xh, 1 - xh) * ny + y)
    x_prev = (cross, jnp.where(xl == 0, 1 - xh, xh) * ny + y)

    weigh = {}
    CHIP, WEIGHT, TEACH, CROSS, CORR, GRAD, LAST = range(7)

    def copy(src, dst, s, r, to):
        return pltpu.make_async_remote_copy(
            src_ref=src, dst_ref=dst, send_sem=s, recv_sem=r, device_id=to, device_id_type=MESH
        )

    def send(kind, src, dst, r, to):
        copy(src, dst, out_s.at[kind], r, to).start()
        size = src.dtype.itemsize
        for n in src.shape:
            size *= n
        weigh[kind] = weigh.get(kind, 0) + size

    def arrived(dst, r):
        copy(dst, dst, out_s.at[0], r, mate).wait_recv()

    top = nz // 2

    def hop(k):
        return z_at(around(z + k, nz))

    def arrived_all(ref, n, r):
        arrived(ref.at[pl.ds(0, n)], r)

    def ag_go(kind, slot, rs):
        for k, r in ((2, 2), (-2, 3), (1, 0), (-1, 0)):
            send(kind, slot(z), slot(z), rs.at[r], hop(k))

    def ag_on(kind, slot, rs, far=None):
        for dr in (0, 1):
            sgn = 1 - 2 * dr
            block = slot(around(z - 2 * sgn, nz))
            arrived(block, rs.at[2 + dr])
            if far is None:
                side = block.shape[-1] // 2
                part = block.at[:, pl.ds(dr * side, side)]
                send(kind, part, part, rs.at[1], hop(2 * sgn))
            elif far == dr:
                send(kind, block, block, rs.at[1], hop(2 * sgn))
            send(kind, block, block, rs.at[1], hop(sgn))

    def ag_end(like, rs):
        arrived_all(like, 2, rs.at[0])
        arrived_all(like, 3, rs.at[1])

    def agx_to(kind, slot, xr, offs):
        for off in offs:
            block = slot(around(z + off, nz))
            send(kind, block, block, xr, x_mate)

    def agx_go(kind, slot, rs, xr):
        ag_go(kind, slot, rs)
        agx_to(kind, slot, xr, (0,))

    def agx_on(kind, slot, rs, xr, like):
        ag_on(kind, slot, rs)
        agx_to(kind, slot, xr, (-2, 2))
        arrived_all(like, 2, rs.at[0])
        agx_to(kind, slot, xr, (-1, 1))

    def agx_end(kind, slot, rs, xr, like):
        arrived_all(like, 3, rs.at[1])
        agx_to(kind, slot, xr, (-3, 3, top))

    def far_step(kind, buf, local, rs):
        for dr in (0, 1):
            buf[dr, 2, 0] = local(dr, around(z + top, nz)).astype(buf.dtype)
            send(kind, buf.at[dr, 2, 0], buf.at[dr, 1, 0], rs.at[dr], hop(2 - 4 * dr))
        for dr in (0, 1):
            sgn = 1 - 2 * dr
            for st in (0, 1):
                buf[dr, 0, st] = local(st, around(z + 3 * sgn, nz)).astype(buf.dtype)
            send(kind, buf.at[dr, 0, pl.ds(0, 2)], buf.at[dr, 1, pl.ds(1, 2)], rs.at[dr], hop(sgn))

    def mid_step(kind, buf, local, rs):
        for dr in (0, 1):
            sgn = 1 - 2 * dr
            arrived(buf.at[dr, 1], rs.at[dr])
            for st in (0, 1):
                v = local(st, around(z + 2 * sgn, nz)) + buf[dr, 1, 1 + st].astype(F32)
                if st == dr:
                    v = v + buf[dr, 1, 0].astype(F32)
                buf[dr, 3, st] = v.astype(buf.dtype)
            send(kind, buf.at[dr, 3, pl.ds(0, 2)], buf.at[dr, 4, pl.ds(0, 2)], rs.at[2], hop(2 * sgn))

    def near_step(kind, buf, local, rs):
        for dr in (0, 1):
            sgn = 1 - 2 * dr
            for st in (0, 1):
                buf[dr, 6, st] = local(st, around(z + sgn, nz)).astype(buf.dtype)
            send(kind, buf.at[dr, 6, pl.ds(0, 2)], buf.at[dr, 5, pl.ds(0, 2)], rs.at[2], hop(sgn))

    def sum_end(buf, rs):
        arrived(buf.at[:, pl.ds(4, 2), pl.ds(0, 2)], rs.at[2])

    def sum_total(st, buf, local):
        v = local(st, z)
        for dr in (0, 1):
            v = v + buf[dr, 4, st].astype(F32) + buf[dr, 5, st].astype(F32)
        return v

    def ring_step(kind, s, buf, local, rs):
        if s == 1:
            arrived(buf.at[0, s], rs.at[s - 1])
        elif s > 1:
            arrived(buf.at[:, s], rs.at[s - 1])
        for dr in (0, 1):
            sgn = 1 - 2 * dr
            p = around(z + sgn * (top - s), nz)
            for st in (dr,) if s == 0 else (0, 1):
                v = local(st, p)
                if s > 1 or (s == 1 and st == dr):
                    v = v + buf[dr, s, st].astype(F32)
                buf[dr, s, st] = v.astype(buf.dtype)
            if s == 0:
                send(kind, buf.at[dr, 0, dr], buf.at[dr, 1, dr], rs.at[0], hop(sgn))
            else:
                send(kind, buf.at[dr, s], buf.at[dr, s + 1], rs.at[s], hop(sgn))

    def ring_end(buf, rs):
        arrived(buf.at[:, top], rs.at[top - 1])

    def ring_total(st, buf, local):
        return local(st, z) + buf[0, top, st].astype(F32) + buf[1, top, st].astype(F32)

    need = [top, 3, -3, 2, -2, 1, -1, 0]

    def need_at(k):
        return around(z + need[k], nz)

    def x_group(k):
        return (0, 0, 0, 1, 1, 2, 2, 3)[k]

    def x_wait(i, dst, rs):
        arrived_all(dst, (3, 2, 2, 1)[i], rs.at[i])

    def ar_copy(buf, i, k):
        return copy(buf.at[chip], buf.at[chip], ar_s.at[i], ar_r.at[i], dp_at(around(chip + k, chips)))

    farthest = sorted(range(1, chips), key=lambda k: -min(k % nz, nz - k % nz))

    def ar_start(buf, i):
        for k in farthest:
            ar_copy(buf, i, k).start()

    def ar_wait(buf, i):
        arrived(buf.at[pl.ds(0, chips - 1)], ar_r.at[i])
        return jnp.sum(buf[...], axis=0)

    def ar_sent(buf, i, n):
        there = buf.at[pl.ds(0, n - 1)]
        copy(there, there, ar_s.at[i], ar_r.at[i], mate).wait_send()

    def f_start(buf, i):
        @pl.loop(1, feats)
        def _(k):
            copy(buf.at[f], buf.at[f], ar_s.at[i], ar_r.at[i], (d, around(f + k, feats))).start()

    def f_wait(buf, i):
        arrived(buf.at[pl.ds(0, feats - 1)], ar_r.at[i])

    lanes = cols // 128

    def pack(buf, at, row, v):
        for k in range(v.shape[1] // 128):
            buf[at, row + k:row + k + 1, :] = v[:, k * 128:(k + 1) * 128]

    def spread_out(v, row, n):
        return jnp.concatenate([v[row + k:row + k + 1, :] for k in range(n // 128)], axis=1)

    def norm_of(sums, squares):
        center = sums / total_rows
        spread = squares / total_rows - center * center
        return center, lax.rsqrt(spread + NORM_EPS)

    barrier = pltpu.get_barrier_semaphore()

    def greet(to):
        pl.semaphore_signal(barrier, inc=1, device_id=to, device_id_type=MESH)

    greet(mate)
    greet(x_diag)

    @pl.loop(1, feats)
    def _(k):
        greet((d, around(f + k, feats)))

    @pl.loop(1, chips)
    def _(k):
        greet(dp_at(around(chip + k, chips)))

    my_cols = pl.ds(pl.multiple_of(core * half, half), half)
    mate_cols = pl.ds(pl.multiple_of((1 - core) * half, half), half)
    w_in = pltpu.make_async_copy(w_hbm.at[:, my_cols], wb.at[xl, z, core], in_s.at[0])
    t_in = pltpu.make_async_copy(t_hbm, tb.at[0, y, 0], in_s.at[1])
    x_in = pltpu.make_async_copy(x_hbm, x_ref, in_s.at[2])
    w_in.start()
    t_in.start()
    x_in.start()
    rowsum[...] = jnp.zeros_like(rowsum)
    pl.semaphore_wait(barrier, feats + chips)

    send(WEIGHT, w_hbm.at[:, mate_cols], wb.at[xl, z, core], wc_r, mate)
    send(TEACH, t_hbm, tb.at[0, y, 1], tc_r.at[0, 0], mate)

    mid = rows // 2
    right, left = y_at(around(y + 1, ny)), y_at(around(y - 1, ny))
    offs = (0, -1, 1, 2)

    def t_at(st, e):
        return tb.at[st, around(y + offs[e], ny), 0]

    def t_hand(st, e):
        send(TEACH, t_at(st, e), tb.at[st, around(y + offs[e], ny), 1], tc_r.at[st, e], mate)

    high, low = pl.ds(0, mid), pl.ds(mid, mid)

    def t_round(st, src):
        there = t_at(st, 0)
        send(TEACH, src.at[high], there.at[high], ty_r.at[st, 0], right)
        send(TEACH, src.at[low], there.at[low], ty_r.at[st, 1], left)
        send(TEACH, src.at[low], there.at[low], ty_r.at[st, 3], right)
        send(TEACH, src.at[high], there.at[high], ty_r.at[st, 4], left)

    def t_pass(st):
        for e, part, to in ((1, high, right), (2, low, left)):
            part = t_at(st, e).at[part]
            arrived(part, ty_r.at[st, e - 1])
            send(TEACH, part, part, ty_r.at[st, 2], to)

    def t_near(st):
        for e, part in ((1, low), (2, high)):
            arrived(t_at(st, e).at[part], ty_r.at[st, e + 2])
            t_hand(st, e)

    def t_far(st):
        arrived(t_at(st, 3), ty_r.at[st, 2])
        t_hand(st, 3)

    quad = rows // 4
    ways = (x_next, x_prev)

    def t_cross(i):
        for dr in (0, 1):
            part = t_hbm.at[pl.ds((2 * dr + i) * quad, quad)]
            send(CROSS, part, rl.at[dr, i], tx_r.at[dr, i], ways[dr])

    def t_relay(i):
        for dr in (0, 1):
            arrived(rl.at[dr, i], tx_r.at[dr, i])
            there = t_at(1, 0).at[pl.ds((2 * dr + i) * quad, quad)]
            send(CROSS, rl.at[dr, i], there, to_r, ways[dr])

    def t_over():
        arrived(t_at(1, 0), to_r)
        t_round(1, t_at(1, 0))
        t_hand(1, 0)

    t_round(0, t_hbm)
    send(CHIP, x_hbm, xp, xc_r, mate)

    def t_normal(st, e, wait_mate=True):
        p = around(y + offs[e], ny)
        if wait_mate:
            arrived(tb.at[st, p, 1], tc_r.at[st, e])
        at = (xh if st == 0 else 1 - xh) * ny + p
        center = spread_out(tst[at], 0, cols)
        recip = spread_out(tst[at], lanes, cols)
        for slot in (0, 1):

            @pl.loop(0, rows // 64)
            def _(i):
                here = pl.multiple_of(i * 64, 64)
                v = tb[st, p, slot, pl.ds(here, 64), :].astype(F32)
                there = pl.multiple_of(slot * rows + i * 64, 64)
                tn[st, p, pl.ds(there, 64), :] = ((v - center) * recip).astype(BF16)

    def w_own(p):
        return wb.at[xl, p]

    def w_other(p):
        return wb.at[1 - xl, p]

    w_in.wait()
    arrived(wb.at[xl, z, 1 - core], wc_r)
    send(WEIGHT, w_own(z), w_own(z), wx_r, x_mate)
    ag_go(WEIGHT, w_own, wz_r.at[0])
    t_cross(0)
    t_cross(1)

    t_in.wait()
    arrived(tb.at[0, y, 1], tc_r.at[0, 0])

    def t_sum(i, carry):
        a, b = carry
        for slot in (0, 1):
            v = tb[0, y, slot, pl.ds(pl.multiple_of(i * 64, 64), 64), :].astype(F32).reshape(8, 8, cols)
            a = a + jnp.sum(v, axis=0)
            b = b + jnp.sum(v * v, axis=0)
        return a, b

    zero = jnp.zeros((8, cols), F32)
    a, b = lax.fori_loop(0, rows // 64, t_sum, (zero, zero))
    pack(ar_t, chip, 0, jnp.sum(a, axis=0, keepdims=True))
    pack(ar_t, chip, lanes, jnp.sum(b, axis=0, keepdims=True))
    ar_start(ar_t, 0)

    arrived(w_other(z), wx_r)
    ag_go(WEIGHT, w_other, wz_r.at[1])
    t_relay(0)
    ag_on(WEIGHT, w_own, wz_r.at[0], 0)
    t_pass(0)
    t_relay(1)
    ag_on(WEIGHT, w_other, wz_r.at[1], 1)
    sums = ar_wait(ar_t, 0)
    center, recip = norm_of(sums[0:lanes], sums[lanes:2 * lanes])
    tst[f, 0:lanes, :] = center
    tst[f, lanes:2 * lanes, :] = recip
    f_start(tst, 3)
    t_near(0)

    ag_end(wb.at[xl], wz_r.at[0])
    x_in.wait()
    arrived(xp, xc_r)
    t_over()
    wide = wb.shape[1] * wb.shape[2] * wb.shape[3]
    tile = min(256, rows)
    tiles = rows // tile
    narrow = jnp.zeros((8, half), F32)

    def project(ref, base, h, last):
        deep = pl.ds(pl.multiple_of(h * wide, wide), wide)

        def body(i, carry):
            here = pl.ds(pl.multiple_of(i * tile, tile), tile)
            there = pl.ds(pl.multiple_of(base + i * tile, tile), tile)
            v = jnp.dot(ref[here, deep], wb[h].reshape(wide, half), preferred_element_type=F32)
            if last:
                v = v + pj[there, :]
            pj[there, :] = v
            if not last:
                return carry
            v = v.reshape(tile // 8, 8, half)
            return carry[0] + jnp.sum(v, axis=0), carry[1] + jnp.sum(v * v, axis=0)

        return body

    lax.fori_loop(0, tiles, project(x_ref, 0, xl, False), 0)
    lax.fori_loop(0, tiles, project(xp, rows, xl, False), 0)
    ag_end(wb.at[1 - xl], wz_r.at[1])
    carry = lax.fori_loop(0, tiles, project(x_ref, 0, 1 - xl, True), (narrow, narrow))
    a, b = lax.fori_loop(0, tiles, project(xp, rows, 1 - xl, True), carry)
    ar_p[chip] = jnp.zeros((8, 128), F32)
    pack(ar_p, chip, 0, jnp.sum(a, axis=0, keepdims=True))
    pack(ar_p, chip, lanes // 2, jnp.sum(b, axis=0, keepdims=True))
    ar_start(ar_p, 1)
    t_far(0)
    f_wait(tst, 3)
    t_normal(0, 0, wait_mate=False)

    def n_sum(i, total):
        v = tn[0, y, pl.ds(pl.multiple_of(i * 64, 64), 64), :].astype(F32)
        return total + jnp.sum(v.reshape(8, 8, cols), axis=0)

    n_sums = lax.fori_loop(0, 2 * rows // 64, n_sum, zero)
    ar_n[chip] = jnp.zeros((8, 128), F32)
    pack(ar_n, chip, 0, jnp.sum(n_sums, axis=0, keepdims=True))
    ar_start(ar_n, 5)
    t_normal(0, 1)
    t_normal(0, 2)

    t_normal(1, 0)
    t_normal(0, 3)
    sums = ar_wait(ar_p, 1)
    p_center, p_recip = norm_of(spread_out(sums, 0, half), spread_out(sums, lanes // 2, half))
    all_tiles = 2 * tiles
    for i in range(all_tiles):
        v = (pj[i * tile:(i + 1) * tile, :] - p_center) * p_recip
        pj[i * tile:(i + 1) * tile, :] = v
        sT[:, i * tile:(i + 1) * tile] = v.T.astype(BF16)

    def half_cols(h):
        return pl.ds(pl.multiple_of(h * half, half), half)

    def correlate(g, h):
        def block(ref, at, n):
            cc[g][h, :, at:at + n] = jnp.dot(sT[...], ref, preferred_element_type=F32)

        if g == 0:
            for j in range(ny // 2):
                block(tn[0, h * (ny // 2) + j], j * cols, cols)
            block(tn[1, y, :, half_cols(h)], ny // 2 * cols, half)
        else:
            block(tn[1, around(y - 1 + 2 * h, ny)], 0, cols)
            block(tn[1, around(y + 2, ny), :, half_cols(h)], cols, half)

    quarter = half // 2
    piece = quarter // nz

    def rows_of(a, p):
        return pl.ds(pl.multiple_of(a * quarter + p * piece, piece), piece)

    def sides(g, st):
        side = cc[g].shape[2] // 2
        return slice(st * side, (st + 1) * side)

    def ca_local(g):
        return lambda st, p: cc[g][xl if st == 0 else 1 - xl, rows_of(0, p), :]

    def ca_far(g):
        far_step(CORR, ca[g], ca_local(g), ca_r.at[g])

    def ca_mid(g):
        mid_step(CORR, ca[g], ca_local(g), ca_r.at[g])

    def ca_near(g):
        near_step(CORR, ca[g], ca_local(g), ca_r.at[g])

    def ca_ring(s):
        ring_step(CORR, s, ca[0], ca_local(0), ca_r.at[0])

    def ca_total(g, st):
        return (ring_total, sum_total)[g](st, ca[g], ca_local(g))

    def ca_over(g):
        (ring_end, sum_end)[g](ca[g], ca_r.at[g])
        xs[g][...] = ca_total(g, 1).astype(BF16)
        send(CORR, xs[g], xr[g], cx_r.at[g], x_mate)

    def cb_over(g):
        bs[g][...] = cc[g][1 - xl, quarter:half, :].astype(BF16).reshape(bs[g].shape)
        for k in range(nz):
            send(CORR, bs[g].at[need_at(k)], br[g].at[need_at(k)], bx_r.at[g, (k + 1) // 2 if g == 0 else x_group(k)], x_mate)

    def cb_local(g):
        return lambda st, p: cc[g][xl, rows_of(1, p), sides(g, st)] + br[g][p, :, sides(g, st)].astype(F32)

    def cb_ring(s):
        arrived_all(br[0], 2 if 0 < s < top else 1, bx_r.at[0, s])
        if s < top:
            ring_step(CORR, s, cb[0], cb_local(0), cb_r.at[0])

    def cb_total(g, st):
        return (ring_total, sum_total)[g](st, cb[g], cb_local(g))

    def cb_far(g):
        x_wait(0, br[g], bx_r.at[g])
        far_step(CORR, cb[g], cb_local(g), cb_r.at[g])

    def cb_mid(g):
        x_wait(1, br[g], bx_r.at[g])
        mid_step(CORR, cb[g], cb_local(g), cb_r.at[g])

    def cb_near(g):
        x_wait(2, br[g], bx_r.at[g])
        near_step(CORR, cb[g], cb_local(g), cb_r.at[g])

    def slope(a, g):
        if a == 0:
            v = ca_total(g, 0)
            arrived(xr[g], cx_r.at[g])
            v = v + xr[g][...].astype(F32)
        else:
            (ring_end, sum_end)[g](cb[g], cb_r.at[g])
            if g == 0:
                cb_ring(top)
            else:
                x_wait(3, br[g], bx_r.at[g])
            v = jnp.concatenate([cb_total(g, st) for st in (0, 1)], axis=1)
        share = v / total_rows
        student_index = (
            f * cols + core * half + a * quarter + z * piece
            + lax.broadcasted_iota(jnp.int32, share.shape, 0)
        )
        col = lax.broadcasted_iota(jnp.int32, share.shape, 1)
        whole = ny // 2 * cols
        teacher_index = jnp.where(col < whole, (xh * 2 + xl) * whole + col, -1) if g == 0 else -1 - col
        on_diag = student_index == teacher_index
        part = jnp.where(on_diag, (1.0 - share) ** 2, OFF_WEIGHT * share * share)
        part = jnp.sum(part.reshape(piece // 8, 8, part.shape[1]), axis=0)
        lacc[g, a] = sum(part[:, k:k + 128] for k in range(0, part.shape[1], 128))
        lean = jnp.where(on_diag, -2.0 * (1.0 - share), 2.0 * OFF_WEIGHT * share).astype(BF16)
        sl[g][xl, a, z] = lean
        lean = lean.astype(F32)
        other = (1 - xh) * ny
        if g == 0:
            at = xh * ny + xl * (ny // 2)
            blocks, last = [at + k for k in range(ny // 2)], other + y
        else:
            blocks, last = [other + around(y - 1 + 2 * xl, ny)], other + around(y + 2, ny)
        n_row = [spread_out(nst[b], 0, cols) for b in blocks]
        last = spread_out(nst[last], 0, cols)
        n_row.append(jnp.where(xl == 0, last[:, 0:half], last[:, half:cols]))
        n_row = jnp.concatenate(n_row, axis=1)
        here = pl.ds(pl.multiple_of(z * piece, piece), piece)
        for k, v in ((a, lean * n_row), (2 + a, lean * share)):
            v = jnp.broadcast_to(jnp.sum(v, axis=1, keepdims=True), (piece, 128))
            rowsum[k, here, :] = v if g == 0 else rowsum[k, here, :] + v

    def slope_go(a, g):
        if (a, g) == (0, 1):
            there = sl[g].at[xl, 0, z]
            send(CORR, there, there, sx_r, x_mate)
            ag_go(CORR, sa_own(g), sz_r.at[0])
        else:
            if g == 0:
                s_ring(a, 0)
            else:
                agx_go(CORR, sb_own(a, g), sb_r, sy_r.at[g, a])

    def s_ring(a, s):
        own = sb_own(a, 0)
        side = sl[0].shape[-1] // 2
        if s == 0:
            agx_to(CORR, own, sy_r.at[0, a], (0,))
        for dr in (0, 1):
            sgn = 1 - 2 * dr
            block = own(around(z - sgn * s, nz))
            half_of = block.at[:, pl.ds(dr * side, side)]
            if s > 0:
                arrived(block if s < top else half_of, sr_r.at[a, dr, s - 1])
            if s < top:
                part = block if s < top - 1 else half_of
                send(CORR, part, part, sr_r.at[a, dr, s], hop(sgn))
        if s > 0:
            agx_to(CORR, own, sy_r.at[0, a], (-s, s) if s < top else (top,))

    def sa_own(g):
        return lambda p: sl[g].at[xl, 0, p]

    def sa_mate(g):
        return lambda p: sl[g].at[1 - xl, 0, p]

    def sb_own(a, g):
        return lambda p: sl[g].at[xl, a, p]

    def sa_other(g):
        arrived(sl[g].at[1 - xl, 0, z], sx_r)
        ag_go(CORR, sa_mate(g), sz_r.at[1])

    def sa_on(g):
        ag_on(CORR, sa_own(g), sz_r.at[0], 0)

    def sa_on_other(g):
        ag_on(CORR, sa_mate(g), sz_r.at[1], 1)

    def sa_end(g):
        ag_end(sl[g].at[0, 0], sz_r.at[0])
        ag_end(sl[g].at[0, 0], sz_r.at[1])

    def sb_on(a, g):
        agx_on(CORR, sb_own(a, g), sb_r, sy_r.at[g, a], sl[g].at[xl, a])

    def sb_end(a, g):
        agx_end(CORR, sb_own(a, g), sb_r, sy_r.at[g, a], sl[g].at[xl, a])

    def sb_last(a, g):
        arrived(sl[g].at[1 - xl, a], sy_r.at[g, a])

    def row_tile(i):
        return pl.ds(pl.multiple_of(i * tile, tile), tile)

    def times_slope(v, g, h, here):
        if g == 0:
            terms = [(tn[0, h * (ny // 2) + j, here, :], j * cols, cols) for j in range(ny // 2)]
            terms.append((tn[1, y, here, half_cols(h)], ny // 2 * cols, half))
        else:
            terms = [(tn[1, around(y - 1 + 2 * h, ny), here, :], 0, cols)]
            terms.append((tn[1, around(y + 2, ny), here, half_cols(h)], cols, half))
        for lhs, at, n in terms:
            rhs = sl[g][h, :, :, :, at:at + n].reshape(half, n)
            w = lax.dot_general(lhs, rhs, (((1,), (1,)), ((), ())), preferred_element_type=F32)
            v = w if v is None else v + w
        return v

    def upstream(*parts):
        @pl.loop(0, all_tiles)
        def _(i):
            v = None
            for g, h in parts:
                v = times_slope(v, g, h, row_tile(i))
            uu[row_tile(i), :] = v

    def u_start():
        for k in range(4):
            ar_u[chip, k:k + 1, :] = rowsum[k].T[0:1]
        ar_u[chip, lanes:2 * lanes, :] = jnp.zeros((lanes, 128), F32)
        part = lacc[0, 0] + lacc[0, 1] + lacc[1, 0] + lacc[1, 1]
        ar_u[chip, lanes:lanes + 1, :] = jnp.sum(part, axis=0, keepdims=True)
        ar_start(ar_u, 2)

    def delta():
        sums = ar_wait(ar_u, 2)
        mean_g = spread_out(sums, 0, half) / (total_rows * total_rows)
        mean_x = spread_out(sums, lanes // 2, half) / total_rows

        @pl.loop(0, all_tiles)
        def _(i):
            here = row_tile(i)
            v = times_slope(uu[here, :], 0, 1 - xl, here)
            v = times_slope(v, 1, 1 - xl, here) / total_rows
            v = p_recip * (v - mean_g - pj[here, :] * mean_x)
            sT[:, pl.ds(pl.multiple_of(i * tile, tile), tile)] = v.T.astype(BF16)

        return sums

    strip = gg.shape[2]

    def gradient(h, out, *pairs):
        @pl.loop(*pairs)
        def _(j):
            j = lax.rem(lax.div(z, 2) + top // 2 + j, nz // 2)
            here = pl.ds(pl.multiple_of(h * nz * strip + j * 2 * strip, 2 * strip), 2 * strip)
            v = jnp.dot(sT[:, 0:rows], x_ref[:, here], preferred_element_type=F32)
            v = v + jnp.dot(sT[:, rows:2 * rows], xp[:, here], preferred_element_type=F32)
            for k in (0, 1):
                out[2 * j + k] = v[:, k * strip:(k + 1) * strip]

    band, wide_band = ga.shape[4], gb.shape[3]
    split = 2 * band

    def ga_local(i):
        part = slice(i * band, (i + 1) * band)
        return lambda st, p: (gg if st == 0 else gs)[p, part, :]

    def ga_step(s):
        for i in (0, 1):
            ring_step(GRAD, s, ga.at[i], ga_local(i), ga_r.at[i])

    def ga_over():
        for i in (0, 1):
            ring_end(ga.at[i], ga_r.at[i])
            gxs[i] = ring_total(1, ga.at[i], ga_local(i))
            send(GRAD, gxs.at[i], gxr.at[i], gx_r.at[i], x_mate)

    def gb_over(*ks):
        for k in ks:
            part = gs.at[need_at(k), pl.ds(split, half - split)]
            send(GRAD, part, gr.at[need_at(k)], gy_r.at[(k + 1) // 2], x_mate)

    def gb_wait(s):
        arrived_all(gr, 2 if 0 < s < top else 1, gy_r.at[s])

    def gb_local(st, p):
        low = st * wide_band
        return gg[p, split + low:split + low + wide_band, :] + gr[p, low:low + wide_band, :]

    def gb_step(s):
        gb_wait(s)
        ring_step(GRAD, s, gb, gb_local, gb_r)

    mine = strip // 2
    first = core == 0

    def g_core(a):
        parts = []
        if a == 0:
            for i in (0, 1):
                v = ring_total(0, ga.at[i], ga_local(i))
                arrived(gxr.at[i], gx_r.at[i])
                parts.append(v + gxr[i])
        else:
            ring_end(gb, gb_r)
            gb_wait(top)
            parts = [ring_total(st, gb, gb_local) for st in (0, 1)]
        v = (LOSS_SCALE * jnp.concatenate(parts, axis=0)).T
        low, high = v[0:mine], v[mine:strip]
        gcs[a] = jnp.where(first, high, low)
        send(LAST, gcs.at[a], gcr.at[a], gc_r.at[a], mate)
        g_ref[:, pl.ds(pl.multiple_of(core * half + a * quarter, quarter), quarter)] = jnp.where(first, low, high)

    def g_last(a):
        arrived(gcr.at[a], gc_r.at[a])
        g_ref[:, pl.ds(pl.multiple_of((1 - core) * half + a * quarter, quarter), quarter)] = gcr[a]

    t_pass(1)
    correlate(0, 1 - xl)
    cb_over(0)
    correlate(0, xl)
    ca_ring(0)
    nst[f] = ar_wait(ar_n, 5)
    f_start(nst, 6)
    cb_ring(0)
    ca_ring(1)
    t_near(1)
    cb_ring(1)
    ca_ring(2)
    t_far(1)
    cb_ring(2)
    t_normal(1, 1)
    t_normal(1, 2)
    ca_ring(3)
    t_normal(1, 3)
    correlate(1, 1 - xl)
    cb_over(1)
    correlate(1, xl)
    ca_far(1)
    cb_ring(3)
    ca_near(1)
    ca_over(0)
    cb_far(1)
    ca_mid(1)
    f_wait(nst, 6)
    slope(1, 0)
    slope(0, 0)
    slope_go(0, 0)
    cb_mid(1)
    slope_go(1, 0)
    cb_near(1)
    ca_over(1)
    s_ring(0, 1)
    s_ring(1, 1)
    slope(0, 1)
    slope_go(0, 1)
    s_ring(0, 2)
    slope(1, 1)
    slope_go(1, 1)
    u_start()
    s_ring(1, 2)
    sa_other(1)
    sa_on(1)
    s_ring(0, 3)
    sb_on(1, 1)
    s_ring(1, 3)
    sa_on_other(1)
    s_ring(0, 4)
    s_ring(1, 4)
    sb_end(1, 1)
    sa_end(1)
    upstream((0, xl), (1, xl))
    sb_last(0, 0)
    sb_last(1, 0)
    sb_last(1, 1)
    sums = delta()
    gradient(1 - xl, gs, 0, 1)
    gb_over(0)
    gradient(xl, gg, 0, 1)
    ga_step(0)
    gradient(1 - xl, gs, 1, nz // 2)
    gb_over(1, 2, 3, 4, 5, 6, 7)
    gradient(xl, gg, 1, nz // 2)
    lf[f] = jnp.broadcast_to(jnp.sum(sums[lanes:2 * lanes], axis=0, keepdims=True), (8, 128))
    f_start(lf, 4)
    gb_step(0)
    ga_step(1)
    gb_step(1)
    ga_step(2)
    gb_step(2)
    ga_step(3)
    gb_step(3)
    f_wait(lf, 4)
    lc[0] = jnp.sum(lf[...], axis=0)
    copy(lc.at[0], lc.at[1], ar_s.at[7], lc_r, mate).start()
    ga_over()
    g_core(1)
    g_core(0)
    arrived(lc.at[1], lc_r)
    loss_ref[0, 0] = jnp.sum((lc[0] + lc[1])[0:1]) / width_all
    g_last(1)
    g_last(0)
    ar_sent(ar_t, 0, chips)
    ar_sent(ar_p, 1, chips)
    ar_sent(ar_u, 2, chips)
    ar_sent(ar_n, 5, chips)
    ar_sent(nst, 6, feats)
    ar_sent(tst, 3, feats)
    ar_sent(lf, 4, feats)
    copy(lc.at[0], lc.at[1], ar_s.at[7], lc_r, mate).wait_send()
    for kind, size in weigh.items():
        there = pj if kind in (WEIGHT, LAST) else tn
        line = there.dtype.itemsize
        for n in there.shape[:-2] + there.shape[-1:]:
            line *= n
        assert size % line == 0 and size // line % 16 == 0
        there = there.at[(slice(None),) * (len(there.shape) - 2) + (pl.ds(0, size // line),)]
        copy(there, there, out_s.at[kind], lc_r, mate).wait_send()


def shards(nz, ny, student, weight, teacher):
    rows, wide = student.shape
    strip_w, cols = weight.shape
    half = cols // 2
    spans = ((ny + 1) * cols // 2, (ny - 1) * cols // 2)
    chips, feats = 2 * nz, 2 * ny
    strip = wide // chips
    quarter = half // 2
    piece = quarter // nz
    band = half // 4
    V = pltpu.VMEM
    D = pltpu.SemaphoreType.DMA
    data = [
        V((rows, wide), BF16),
        V((2, ny, 2, rows, cols), BF16),
        V((2, ny, 2 * rows, cols), BF16),
        V((2, 2, rows // 4, cols), BF16),
        V((rows, wide), BF16),
        V((2, nz, 2, strip_w, half), BF16),
        V((2 * rows, half), F32),
        V((half, 2 * rows), BF16),
        *[V((2, half, n), F32) for n in spans],
        V((2, nz // 2 + 1, 2, piece, spans[0]), BF16),
        V((2, 7, 3, piece, spans[1]), BF16),
        V((2, nz // 2 + 1, 2, piece, spans[0] // 2), BF16),
        V((2, 7, 3, piece, spans[1] // 2), BF16),
        *[V((piece, n), BF16) for n in spans],
        *[V((piece, n), BF16) for n in spans],
        *[V((nz, piece, n), BF16) for n in spans],
        *[V((nz, piece, n), BF16) for n in spans],
        *[V((2, 2, nz, piece, n), BF16) for n in spans],
        V((2 * rows, half), F32),
        V((nz, half, strip), F32),
        V((nz, half, strip), F32),
        V((nz, half - 2 * band, strip), F32),
        V((2, 2, nz // 2 + 1, 2, band, strip), F32),
        V((2, nz // 2 + 1, 2, half // 2 - band, strip), F32),
        V((2, band, strip), F32),
        V((2, band, strip), F32),
        V((2, strip // 2, quarter), F32),
        V((2, strip // 2, quarter), F32),
        V((chips, 8, 128), F32),
        V((chips, 8, 128), F32),
        V((chips, 8, 128), F32),
        V((chips, 8, 128), F32),
        V((feats, 8, 128), F32),
        V((feats, 8, 128), F32),
        V((4, 128, 128), F32),
        V((2, 2, 8, 128), F32),
        V((feats, 8, 128), F32),
        V((2, 8, 128), F32),
    ]
    sems = [
        D(shape) for shape in (
            (7,), (3,), (8,), (7,),
            (2, ny), (2, 2), (), (2, 5), (), (), (), (2, 4),
            (2, nz // 2), (2,), (2, nz // 2), (2, 5),
            (), (2, 4), (2, 2, nz // 2), (4,), (2, 2),
            (2, nz // 2), (2,), (5,), (nz // 2,), (2,), (),
        )
    ]
    vm = pl.BlockSpec(memory_space=pltpu.VMEM)
    sm = pl.BlockSpec(memory_space=pltpu.SMEM)
    far = pl.BlockSpec(memory_space=pl.ANY)
    loss, grad = pl.pallas_call(
        functools.partial(kernel, nz, ny),
        out_shape=(
            jax.ShapeDtypeStruct((1, 1), F32),
            jax.ShapeDtypeStruct((strip_w, cols), F32),
        ),
        in_specs=[far] * 3,
        out_specs=(sm, vm),
        scratch_shapes=data + sems,
        compiler_params=pltpu.CompilerParams(
            collective_id=0, has_side_effects=True, vmem_limit_bytes=56 * 1024 * 1024
        ),
    )(student, weight, teacher)
    return loss.reshape(()), grad


def solution(mesh):
    placed = (P("dp", None), P("dp", "feat"), P("dp", "feat"))
    nz, ny = mesh.shape["dp"] // 4, mesh.shape["feat"] // 2
    return jax.shard_map(
        functools.partial(shards, nz, ny), mesh=mesh, in_specs=placed,
        out_specs=(P(), P("dp", "feat")), check_vma=False,
    )
```

```python
import functools

import jax
import jax.numpy as jnp
from jax import lax
from jax.experimental import pallas as pl
from jax.experimental.pallas import tpu as pltpu
from jax.sharding import PartitionSpec as P

OFF_WEIGHT = 0.5
NORM_EPS = 1e-05
LOSS_SCALE = 128.0
F32 = jnp.float32
BF16 = jnp.bfloat16
MESH = pl.DeviceIdType.MESH


def around(at, n):
    return lax.rem(at + n, n)


def kernel(
    nz, ny, x_hbm, w_hbm, t_hbm, loss_ref, g_ref,
    x_ref, tb, tn, rl, xp, wb, pj, sT,
    cc0, cc1, ca0, ca1, cb0, cb1, xs0, xs1, xr0, xr1, bs0, bs1, br0, br1, sl0, sl1, uu, gg, gs, gr, ga, gb, gxs, gxr, gcs, gcr,
    ar_t, ar_p, ar_u, ar_n, tst, nst, rowsum, lacc, lf, lc,
    out_s, in_s, ar_s, ar_r, tc_r, tx_r, to_r, ty_r, xc_r, wc_r, wx_r, wz_r,
    ca_r, cx_r, cb_r, bx_r, sx_r, sz_r, sr_r, sb_r, sy_r, ga_r, gx_r, gy_r, gb_r, gc_r, lc_r,
):
    cc, ca, cb, xs = (cc0, cc1), (ca0, ca1), (cb0, cb1), (xs0, xs1)
    xr, bs, br, sl = (xr0, xr1), (bs0, bs1), (br0, br1), (sl0, sl1)
    d = lax.axis_index("dp")
    f = lax.axis_index("feat")
    chips = 2 * nz
    feats = 2 * ny
    core = lax.rem(d, 2)
    chip = lax.div(d, 2)
    z = lax.rem(chip, nz)
    xl = lax.div(chip, nz)
    y = lax.rem(f, ny)
    xh = lax.div(f, ny)
    rows = x_ref.shape[0]
    cols = w_hbm.shape[1]
    half = cols // 2
    total_rows = float(rows * 2 * chips)
    width_all = cols * feats

    mate = (d + 1 - 2 * core, f)

    def dp_at(chip_at):
        return (chip_at * 2 + core, f)

    def z_at(at):
        return dp_at(xl * nz + at)

    def y_at(at):
        return (d, xh * ny + at)

    x_mate = dp_at((1 - xl) * nz + z)
    cross = ((1 - xl) * nz + z) * 2 + core
    x_diag = (cross, (1 - xh) * ny + y)
    x_next = (cross, jnp.where(xl == 0, xh, 1 - xh) * ny + y)
    x_prev = (cross, jnp.where(xl == 0, 1 - xh, xh) * ny + y)

    weigh = {}
    CHIP, WEIGHT, TEACH, CROSS, CORR, GRAD, LAST = range(7)

    def copy(src, dst, s, r, to):
        return pltpu.make_async_remote_copy(
            src_ref=src, dst_ref=dst, send_sem=s, recv_sem=r, device_id=to, device_id_type=MESH
        )

    def send(kind, src, dst, r, to):
        copy(src, dst, out_s.at[kind], r, to).start()
        size = src.dtype.itemsize
        for n in src.shape:
            size *= n
        weigh[kind] = weigh.get(kind, 0) + size

    def arrived(dst, r):
        copy(dst, dst, out_s.at[0], r, mate).wait_recv()

    top = nz // 2

    def hop(k):
        return z_at(around(z + k, nz))

    def arrived_all(ref, n, r):
        arrived(ref.at[pl.ds(0, n)], r)

    def ag_go(kind, slot, rs):
        for k, r in ((2, 2), (-2, 3), (1, 0), (-1, 0)):
            send(kind, slot(z), slot(z), rs.at[r], hop(k))

    def ag_on(kind, slot, rs, far=None):
        for dr in (0, 1):
            sgn = 1 - 2 * dr
            block = slot(around(z - 2 * sgn, nz))
            arrived(block, rs.at[2 + dr])
            if far is None:
                side = block.shape[-1] // 2
                part = block.at[:, pl.ds(dr * side, side)]
                send(kind, part, part, rs.at[1], hop(2 * sgn))
            elif far == dr:
                send(kind, block, block, rs.at[1], hop(2 * sgn))
            send(kind, block, block, rs.at[1], hop(sgn))

    def ag_end(like, rs):
        arrived_all(like, 2, rs.at[0])
        arrived_all(like, 3, rs.at[1])

    def agx_to(kind, slot, xr, offs):
        for off in offs:
            block = slot(around(z + off, nz))
            send(kind, block, block, xr, x_mate)

    def agx_go(kind, slot, rs, xr):
        ag_go(kind, slot, rs)
        agx_to(kind, slot, xr, (0,))

    def agx_on(kind, slot, rs, xr, like):
        ag_on(kind, slot, rs)
        agx_to(kind, slot, xr, (-2, 2))
        arrived_all(like, 2, rs.at[0])
        agx_to(kind, slot, xr, (-1, 1))

    def agx_end(kind, slot, rs, xr, like):
        arrived_all(like, 3, rs.at[1])
        agx_to(kind, slot, xr, (-3, 3, top))

    def far_step(kind, buf, local, rs):
        for dr in (0, 1):
            buf[dr, 2, 0] = local(dr, around(z + top, nz)).astype(buf.dtype)
            send(kind, buf.at[dr, 2, 0], buf.at[dr, 1, 0], rs.at[dr], hop(2 - 4 * dr))
        for dr in (0, 1):
            sgn = 1 - 2 * dr
            for st in (0, 1):
                buf[dr, 0, st] = local(st, around(z + 3 * sgn, nz)).astype(buf.dtype)
            send(kind, buf.at[dr, 0, pl.ds(0, 2)], buf.at[dr, 1, pl.ds(1, 2)], rs.at[dr], hop(sgn))

    def mid_step(kind, buf, local, rs):
        for dr in (0, 1):
            sgn = 1 - 2 * dr
            arrived(buf.at[dr, 1], rs.at[dr])
            for st in (0, 1):
                v = local(st, around(z + 2 * sgn, nz)) + buf[dr, 1, 1 + st].astype(F32)
                if st == dr:
                    v = v + buf[dr, 1, 0].astype(F32)
                buf[dr, 3, st] = v.astype(buf.dtype)
            send(kind, buf.at[dr, 3, pl.ds(0, 2)], buf.at[dr, 4, pl.ds(0, 2)], rs.at[2], hop(2 * sgn))

    def near_step(kind, buf, local, rs):
        for dr in (0, 1):
            sgn = 1 - 2 * dr
            for st in (0, 1):
                buf[dr, 6, st] = local(st, around(z + sgn, nz)).astype(buf.dtype)
            send(kind, buf.at[dr, 6, pl.ds(0, 2)], buf.at[dr, 5, pl.ds(0, 2)], rs.at[2], hop(sgn))

    def sum_end(buf, rs):
        arrived(buf.at[:, pl.ds(4, 2), pl.ds(0, 2)], rs.at[2])

    def sum_total(st, buf, local):
        v = local(st, z)
        for dr in (0, 1):
            v = v + buf[dr, 4, st].astype(F32) + buf[dr, 5, st].astype(F32)
        return v

    def ring_step(kind, s, buf, local, rs):
        for dr in (0, 1):
            sgn = 1 - 2 * dr
            p = around(z + sgn * (top - s), nz)
            if s == 1:
                arrived(buf.at[dr, s, dr], rs.at[dr, s - 1])
            elif s > 1:
                arrived(buf.at[dr, s], rs.at[dr, s - 1])
            for st in (dr,) if s == 0 else (0, 1):
                v = local(st, p)
                if s > 1 or (s == 1 and st == dr):
                    v = v + buf[dr, s, st].astype(F32)
                buf[dr, s, st] = v.astype(buf.dtype)
            if s == 0:
                send(kind, buf.at[dr, 0, dr], buf.at[dr, 1, dr], rs.at[dr, 0], hop(sgn))
            else:
                send(kind, buf.at[dr, s], buf.at[dr, s + 1], rs.at[dr, s], hop(sgn))

    def ring_end(buf, rs):
        for dr in (0, 1):
            arrived(buf.at[dr, top], rs.at[dr, top - 1])

    def ring_total(st, buf, local):
        return local(st, z) + buf[0, top, st].astype(F32) + buf[1, top, st].astype(F32)

    need = [top, 3, -3, 2, -2, 1, -1, 0]

    def need_at(k):
        return around(z + need[k], nz)

    def x_group(k):
        return (0, 0, 0, 1, 1, 2, 2, 3)[k]

    def x_wait(i, dst, rs):
        arrived_all(dst, (3, 2, 2, 1)[i], rs.at[i])

    def ar_copy(buf, i, k):
        return copy(buf.at[chip], buf.at[chip], ar_s.at[i], ar_r.at[i], dp_at(around(chip + k, chips)))

    def ar_start(buf, i):
        for k in range(1, chips):
            ar_copy(buf, i, k).start()

    def ar_wait(buf, i):
        arrived(buf.at[pl.ds(0, chips - 1)], ar_r.at[i])
        return jnp.sum(buf[...], axis=0)

    def ar_sent(buf, i, n):
        there = buf.at[pl.ds(0, n - 1)]
        copy(there, there, ar_s.at[i], ar_r.at[i], mate).wait_send()

    def f_start(buf, i):
        @pl.loop(1, feats)
        def _(k):
            copy(buf.at[f], buf.at[f], ar_s.at[i], ar_r.at[i], (d, around(f + k, feats))).start()

    def f_wait(buf, i):
        arrived(buf.at[pl.ds(0, feats - 1)], ar_r.at[i])

    lanes = cols // 128

    def pack(buf, at, row, v):
        for k in range(v.shape[1] // 128):
            buf[at, row + k:row + k + 1, :] = v[:, k * 128:(k + 1) * 128]

    def spread_out(v, row, n):
        return jnp.concatenate([v[row + k:row + k + 1, :] for k in range(n // 128)], axis=1)

    def norm_of(sums, squares):
        center = sums / total_rows
        spread = squares / total_rows - center * center
        return center, lax.rsqrt(spread + NORM_EPS)

    barrier = pltpu.get_barrier_semaphore()

    def greet(to):
        pl.semaphore_signal(barrier, inc=1, device_id=to, device_id_type=MESH)

    greet(mate)
    greet(x_diag)

    @pl.loop(1, feats)
    def _(k):
        greet((d, around(f + k, feats)))

    @pl.loop(1, chips)
    def _(k):
        greet(dp_at(around(chip + k, chips)))

    my_cols = pl.ds(pl.multiple_of(core * half, half), half)
    mate_cols = pl.ds(pl.multiple_of((1 - core) * half, half), half)
    w_in = pltpu.make_async_copy(w_hbm.at[:, my_cols], wb.at[xl, z, core], in_s.at[0])
    t_in = pltpu.make_async_copy(t_hbm, tb.at[0, y, 0], in_s.at[1])
    x_in = pltpu.make_async_copy(x_hbm, x_ref, in_s.at[2])
    w_in.start()
    t_in.start()
    x_in.start()
    rowsum[...] = jnp.zeros_like(rowsum)
    pl.semaphore_wait(barrier, feats + chips)

    send(WEIGHT, w_hbm.at[:, mate_cols], wb.at[xl, z, core], wc_r, mate)
    send(TEACH, t_hbm, tb.at[0, y, 1], tc_r.at[0, 0], mate)

    mid = rows // 2
    right, left = y_at(around(y + 1, ny)), y_at(around(y - 1, ny))
    offs = (0, -1, 1, 2)

    def t_at(st, e):
        return tb.at[st, around(y + offs[e], ny), 0]

    def t_hand(st, e):
        send(TEACH, t_at(st, e), tb.at[st, around(y + offs[e], ny), 1], tc_r.at[st, e], mate)

    high, low = pl.ds(0, mid), pl.ds(mid, mid)

    def t_round(st, src):
        there = t_at(st, 0)
        send(TEACH, src.at[high], there.at[high], ty_r.at[st, 0], right)
        send(TEACH, src.at[low], there.at[low], ty_r.at[st, 1], left)
        send(TEACH, src.at[low], there.at[low], ty_r.at[st, 3], right)
        send(TEACH, src.at[high], there.at[high], ty_r.at[st, 4], left)

    def t_pass(st):
        for e, part, to in ((1, high, right), (2, low, left)):
            part = t_at(st, e).at[part]
            arrived(part, ty_r.at[st, e - 1])
            send(TEACH, part, part, ty_r.at[st, 2], to)

    def t_near(st):
        for e, part in ((1, low), (2, high)):
            arrived(t_at(st, e).at[part], ty_r.at[st, e + 2])
            t_hand(st, e)

    def t_far(st):
        arrived(t_at(st, 3), ty_r.at[st, 2])
        t_hand(st, 3)

    quad = rows // 4
    ways = (x_next, x_prev)

    def t_cross(i):
        for dr in (0, 1):
            part = t_hbm.at[pl.ds((2 * dr + i) * quad, quad)]
            send(CROSS, part, rl.at[dr, i], tx_r.at[dr, i], ways[dr])

    def t_relay(i):
        for dr in (0, 1):
            arrived(rl.at[dr, i], tx_r.at[dr, i])
            there = t_at(1, 0).at[pl.ds((2 * dr + i) * quad, quad)]
            send(CROSS, rl.at[dr, i], there, to_r, ways[dr])

    def t_over():
        arrived(t_at(1, 0), to_r)
        t_round(1, t_at(1, 0))
        t_hand(1, 0)

    t_round(0, t_hbm)
    send(CHIP, x_hbm, xp, xc_r, mate)

    def t_normal(st, e, wait_mate=True):
        p = around(y + offs[e], ny)
        if wait_mate:
            arrived(tb.at[st, p, 1], tc_r.at[st, e])
        at = (xh if st == 0 else 1 - xh) * ny + p
        center = spread_out(tst[at], 0, cols)
        recip = spread_out(tst[at], lanes, cols)
        for slot in (0, 1):

            @pl.loop(0, rows // 64)
            def _(i):
                here = pl.multiple_of(i * 64, 64)
                v = tb[st, p, slot, pl.ds(here, 64), :].astype(F32)
                there = pl.multiple_of(slot * rows + i * 64, 64)
                tn[st, p, pl.ds(there, 64), :] = ((v - center) * recip).astype(BF16)

    def w_own(p):
        return wb.at[xl, p]

    def w_other(p):
        return wb.at[1 - xl, p]

    w_in.wait()
    arrived(wb.at[xl, z, 1 - core], wc_r)
    send(WEIGHT, w_own(z), w_own(z), wx_r, x_mate)
    ag_go(WEIGHT, w_own, wz_r.at[0])
    t_cross(0)
    t_cross(1)

    t_in.wait()
    arrived(tb.at[0, y, 1], tc_r.at[0, 0])

    def t_sum(i, carry):
        a, b = carry
        for slot in (0, 1):
            v = tb[0, y, slot, pl.ds(pl.multiple_of(i * 64, 64), 64), :].astype(F32).reshape(8, 8, cols)
            a = a + jnp.sum(v, axis=0)
            b = b + jnp.sum(v * v, axis=0)
        return a, b

    zero = jnp.zeros((8, cols), F32)
    a, b = lax.fori_loop(0, rows // 64, t_sum, (zero, zero))
    pack(ar_t, chip, 0, jnp.sum(a, axis=0, keepdims=True))
    pack(ar_t, chip, lanes, jnp.sum(b, axis=0, keepdims=True))
    ar_start(ar_t, 0)

    arrived(w_other(z), wx_r)
    ag_go(WEIGHT, w_other, wz_r.at[1])
    t_relay(0)
    ag_on(WEIGHT, w_own, wz_r.at[0], 0)
    t_pass(0)
    t_relay(1)
    ag_on(WEIGHT, w_other, wz_r.at[1], 1)
    sums = ar_wait(ar_t, 0)
    center, recip = norm_of(sums[0:lanes], sums[lanes:2 * lanes])
    tst[f, 0:lanes, :] = center
    tst[f, lanes:2 * lanes, :] = recip
    f_start(tst, 3)
    t_near(0)

    ag_end(wb.at[xl], wz_r.at[0])
    x_in.wait()
    arrived(xp, xc_r)
    t_over()
    wide = wb.shape[1] * wb.shape[2] * wb.shape[3]
    tile = min(256, rows)
    tiles = rows // tile
    narrow = jnp.zeros((8, half), F32)

    def project(ref, base, h, last):
        deep = pl.ds(pl.multiple_of(h * wide, wide), wide)

        def body(i, carry):
            here = pl.ds(pl.multiple_of(i * tile, tile), tile)
            there = pl.ds(pl.multiple_of(base + i * tile, tile), tile)
            v = jnp.dot(ref[here, deep], wb[h].reshape(wide, half), preferred_element_type=F32)
            if last:
                v = v + pj[there, :]
            pj[there, :] = v
            if not last:
                return carry
            v = v.reshape(tile // 8, 8, half)
            return carry[0] + jnp.sum(v, axis=0), carry[1] + jnp.sum(v * v, axis=0)

        return body

    lax.fori_loop(0, tiles, project(x_ref, 0, xl, False), 0)
    lax.fori_loop(0, tiles, project(xp, rows, xl, False), 0)
    ag_end(wb.at[1 - xl], wz_r.at[1])
    carry = lax.fori_loop(0, tiles, project(x_ref, 0, 1 - xl, True), (narrow, narrow))
    a, b = lax.fori_loop(0, tiles, project(xp, rows, 1 - xl, True), carry)
    ar_p[chip] = jnp.zeros((8, 128), F32)
    pack(ar_p, chip, 0, jnp.sum(a, axis=0, keepdims=True))
    pack(ar_p, chip, lanes // 2, jnp.sum(b, axis=0, keepdims=True))
    ar_start(ar_p, 1)
    t_far(0)
    f_wait(tst, 3)
    t_normal(0, 0, wait_mate=False)

    def n_sum(i, total):
        v = tn[0, y, pl.ds(pl.multiple_of(i * 64, 64), 64), :].astype(F32)
        return total + jnp.sum(v.reshape(8, 8, cols), axis=0)

    n_sums = lax.fori_loop(0, 2 * rows // 64, n_sum, zero)
    ar_n[chip] = jnp.zeros((8, 128), F32)
    pack(ar_n, chip, 0, jnp.sum(n_sums, axis=0, keepdims=True))
    ar_start(ar_n, 5)
    t_normal(0, 1)
    t_normal(0, 2)

    t_normal(1, 0)
    t_normal(0, 3)
    sums = ar_wait(ar_p, 1)
    p_center, p_recip = norm_of(spread_out(sums, 0, half), spread_out(sums, lanes // 2, half))
    all_tiles = 2 * tiles
    for i in range(all_tiles):
        v = (pj[i * tile:(i + 1) * tile, :] - p_center) * p_recip
        pj[i * tile:(i + 1) * tile, :] = v
        sT[:, i * tile:(i + 1) * tile] = v.T.astype(BF16)

    def half_cols(h):
        return pl.ds(pl.multiple_of(h * half, half), half)

    def correlate(g, h):
        def block(ref, at, n):
            cc[g][h, :, at:at + n] = jnp.dot(sT[...], ref, preferred_element_type=F32)

        if g == 0:
            for j in range(ny // 2):
                block(tn[0, h * (ny // 2) + j], j * cols, cols)
            block(tn[1, y, :, half_cols(h)], ny // 2 * cols, half)
        else:
            block(tn[1, around(y - 1 + 2 * h, ny)], 0, cols)
            block(tn[1, around(y + 2, ny), :, half_cols(h)], cols, half)

    quarter = half // 2
    piece = quarter // nz

    def rows_of(a, p):
        return pl.ds(pl.multiple_of(a * quarter + p * piece, piece), piece)

    def sides(g, st):
        side = cc[g].shape[2] // 2
        return slice(st * side, (st + 1) * side)

    def ca_local(g):
        return lambda st, p: cc[g][xl if st == 0 else 1 - xl, rows_of(0, p), :]

    def ca_far(g):
        far_step(CORR, ca[g], ca_local(g), ca_r.at[g, 0])

    def ca_mid(g):
        mid_step(CORR, ca[g], ca_local(g), ca_r.at[g, 0])

    def ca_near(g):
        near_step(CORR, ca[g], ca_local(g), ca_r.at[g, 0])

    def ca_ring(s):
        ring_step(CORR, s, ca[0], ca_local(0), ca_r.at[0])

    def ca_total(g, st):
        return (ring_total, sum_total)[g](st, ca[g], ca_local(g))

    def ca_over(g):
        (ring_end, sum_end)[g](ca[g], (ca_r.at[0], ca_r.at[1, 0])[g])
        xs[g][...] = ca_total(g, 1).astype(BF16)
        send(CORR, xs[g], xr[g], cx_r.at[g], x_mate)

    def cb_over(g):
        bs[g][...] = cc[g][1 - xl, quarter:half, :].astype(BF16).reshape(bs[g].shape)
        for k in range(nz):
            send(CORR, bs[g].at[need_at(k)], br[g].at[need_at(k)], bx_r.at[g, (k + 1) // 2 if g == 0 else x_group(k)], x_mate)

    def cb_local(g):
        return lambda st, p: cc[g][xl, rows_of(1, p), sides(g, st)] + br[g][p, :, sides(g, st)].astype(F32)

    def cb_ring(s):
        arrived_all(br[0], 2 if 0 < s < top else 1, bx_r.at[0, s])
        if s < top:
            ring_step(CORR, s, cb[0], cb_local(0), cb_r.at[0])

    def cb_total(g, st):
        return (ring_total, sum_total)[g](st, cb[g], cb_local(g))

    def cb_far(g):
        x_wait(0, br[g], bx_r.at[g])
        far_step(CORR, cb[g], cb_local(g), cb_r.at[g, 0])

    def cb_mid(g):
        x_wait(1, br[g], bx_r.at[g])
        mid_step(CORR, cb[g], cb_local(g), cb_r.at[g, 0])

    def cb_near(g):
        x_wait(2, br[g], bx_r.at[g])
        near_step(CORR, cb[g], cb_local(g), cb_r.at[g, 0])

    def slope(a, g):
        if a == 0:
            v = ca_total(g, 0)
            arrived(xr[g], cx_r.at[g])
            v = v + xr[g][...].astype(F32)
        else:
            (ring_end, sum_end)[g](cb[g], (cb_r.at[0], cb_r.at[1, 0])[g])
            if g == 0:
                cb_ring(top)
            else:
                x_wait(3, br[g], bx_r.at[g])
            v = jnp.concatenate([cb_total(g, st) for st in (0, 1)], axis=1)
        share = v / total_rows
        student_index = (
            f * cols + core * half + a * quarter + z * piece
            + lax.broadcasted_iota(jnp.int32, share.shape, 0)
        )
        col = lax.broadcasted_iota(jnp.int32, share.shape, 1)
        whole = ny // 2 * cols
        teacher_index = jnp.where(col < whole, (xh * 2 + xl) * whole + col, -1) if g == 0 else -1 - col
        on_diag = student_index == teacher_index
        part = jnp.where(on_diag, (1.0 - share) ** 2, OFF_WEIGHT * share * share)
        part = jnp.sum(part.reshape(piece // 8, 8, part.shape[1]), axis=0)
        lacc[g, a] = sum(part[:, k:k + 128] for k in range(0, part.shape[1], 128))
        lean = jnp.where(on_diag, -2.0 * (1.0 - share), 2.0 * OFF_WEIGHT * share).astype(BF16)
        sl[g][xl, a, z] = lean
        lean = lean.astype(F32)
        other = (1 - xh) * ny
        if g == 0:
            at = xh * ny + xl * (ny // 2)
            blocks, last = [at + k for k in range(ny // 2)], other + y
        else:
            blocks, last = [other + around(y - 1 + 2 * xl, ny)], other + around(y + 2, ny)
        n_row = [spread_out(nst[b], 0, cols) for b in blocks]
        last = spread_out(nst[last], 0, cols)
        n_row.append(jnp.where(xl == 0, last[:, 0:half], last[:, half:cols]))
        n_row = jnp.concatenate(n_row, axis=1)
        here = pl.ds(pl.multiple_of(z * piece, piece), piece)
        for k, v in ((a, lean * n_row), (2 + a, lean * share)):
            v = jnp.broadcast_to(jnp.sum(v, axis=1, keepdims=True), (piece, 128))
            rowsum[k, here, :] = v if g == 0 else rowsum[k, here, :] + v

    def slope_go(a, g):
        if (a, g) == (0, 1):
            there = sl[g].at[xl, 0, z]
            send(CORR, there, there, sx_r, x_mate)
            ag_go(CORR, sa_own(g), sz_r.at[0])
        else:
            if g == 0:
                s_ring(a, 0)
            else:
                agx_go(CORR, sb_own(a, g), sb_r, sy_r.at[g, a])

    def s_ring(a, s):
        own = sb_own(a, 0)
        side = sl[0].shape[-1] // 2
        if s == 0:
            agx_to(CORR, own, sy_r.at[0, a], (0,))
        for dr in (0, 1):
            sgn = 1 - 2 * dr
            block = own(around(z - sgn * s, nz))
            half_of = block.at[:, pl.ds(dr * side, side)]
            if s > 0:
                arrived(block if s < top else half_of, sr_r.at[a, dr, s - 1])
            if s < top:
                part = block if s < top - 1 else half_of
                send(CORR, part, part, sr_r.at[a, dr, s], hop(sgn))
        if s > 0:
            agx_to(CORR, own, sy_r.at[0, a], (-s, s) if s < top else (top,))

    def sa_own(g):
        return lambda p: sl[g].at[xl, 0, p]

    def sa_mate(g):
        return lambda p: sl[g].at[1 - xl, 0, p]

    def sb_own(a, g):
        return lambda p: sl[g].at[xl, a, p]

    def sa_other(g):
        arrived(sl[g].at[1 - xl, 0, z], sx_r)
        ag_go(CORR, sa_mate(g), sz_r.at[1])

    def sa_on(g):
        ag_on(CORR, sa_own(g), sz_r.at[0], 0)

    def sa_on_other(g):
        ag_on(CORR, sa_mate(g), sz_r.at[1], 1)

    def sa_end(g):
        ag_end(sl[g].at[0, 0], sz_r.at[0])
        ag_end(sl[g].at[0, 0], sz_r.at[1])

    def sb_on(a, g):
        agx_on(CORR, sb_own(a, g), sb_r, sy_r.at[g, a], sl[g].at[xl, a])

    def sb_end(a, g):
        agx_end(CORR, sb_own(a, g), sb_r, sy_r.at[g, a], sl[g].at[xl, a])

    def sb_last(a, g):
        arrived(sl[g].at[1 - xl, a], sy_r.at[g, a])

    def row_tile(i):
        return pl.ds(pl.multiple_of(i * tile, tile), tile)

    def times_slope(v, g, h, here):
        if g == 0:
            terms = [(tn[0, h * (ny // 2) + j, here, :], j * cols, cols) for j in range(ny // 2)]
            terms.append((tn[1, y, here, half_cols(h)], ny // 2 * cols, half))
        else:
            terms = [(tn[1, around(y - 1 + 2 * h, ny), here, :], 0, cols)]
            terms.append((tn[1, around(y + 2, ny), here, half_cols(h)], cols, half))
        for lhs, at, n in terms:
            rhs = sl[g][h, :, :, :, at:at + n].reshape(half, n)
            w = lax.dot_general(lhs, rhs, (((1,), (1,)), ((), ())), preferred_element_type=F32)
            v = w if v is None else v + w
        return v

    def upstream(*parts):
        @pl.loop(0, all_tiles)
        def _(i):
            v = None
            for g, h in parts:
                v = times_slope(v, g, h, row_tile(i))
            uu[row_tile(i), :] = v

    def u_start():
        for k in range(4):
            ar_u[chip, k:k + 1, :] = rowsum[k].T[0:1]
        ar_u[chip, lanes:2 * lanes, :] = jnp.zeros((lanes, 128), F32)
        part = lacc[0, 0] + lacc[0, 1] + lacc[1, 0] + lacc[1, 1]
        ar_u[chip, lanes:lanes + 1, :] = jnp.sum(part, axis=0, keepdims=True)
        ar_start(ar_u, 2)

    def delta():
        sums = ar_wait(ar_u, 2)
        mean_g = spread_out(sums, 0, half) / (total_rows * total_rows)
        mean_x = spread_out(sums, lanes // 2, half) / total_rows

        @pl.loop(0, all_tiles)
        def _(i):
            here = row_tile(i)
            v = times_slope(uu[here, :], 0, 1 - xl, here)
            v = times_slope(v, 1, 1 - xl, here) / total_rows
            v = p_recip * (v - mean_g - pj[here, :] * mean_x)
            sT[:, pl.ds(pl.multiple_of(i * tile, tile), tile)] = v.T.astype(BF16)

        return sums

    strip = gg.shape[2]

    def gradient(h, out, *pairs):
        @pl.loop(*pairs)
        def _(j):
            j = lax.rem(lax.div(z, 2) + top // 2 + j, nz // 2)
            here = pl.ds(pl.multiple_of(h * nz * strip + j * 2 * strip, 2 * strip), 2 * strip)
            v = jnp.dot(sT[:, 0:rows], x_ref[:, here], preferred_element_type=F32)
            v = v + jnp.dot(sT[:, rows:2 * rows], xp[:, here], preferred_element_type=F32)
            for k in (0, 1):
                out[2 * j + k] = v[:, k * strip:(k + 1) * strip]

    band, wide_band = ga.shape[4], gb.shape[3]
    split = 2 * band

    def ga_local(i):
        part = slice(i * band, (i + 1) * band)
        return lambda st, p: (gg if st == 0 else gs)[p, part, :]

    def ga_step(s):
        for i in (0, 1):
            ring_step(GRAD, s, ga.at[i], ga_local(i), ga_r.at[i])

    def ga_over():
        for i in (0, 1):
            ring_end(ga.at[i], ga_r.at[i])
            gxs[i] = ring_total(1, ga.at[i], ga_local(i))
            send(GRAD, gxs.at[i], gxr.at[i], gx_r.at[i], x_mate)

    def gb_over(*ks):
        for k in ks:
            part = gs.at[need_at(k), pl.ds(split, half - split)]
            send(GRAD, part, gr.at[need_at(k)], gy_r.at[(k + 1) // 2], x_mate)

    def gb_wait(s):
        arrived_all(gr, 2 if 0 < s < top else 1, gy_r.at[s])

    def gb_local(st, p):
        low = st * wide_band
        return gg[p, split + low:split + low + wide_band, :] + gr[p, low:low + wide_band, :]

    def gb_step(s):
        gb_wait(s)
        ring_step(GRAD, s, gb, gb_local, gb_r)

    mine = strip // 2
    first = core == 0

    def g_core():
        parts = []
        for i in (0, 1):
            v = ring_total(0, ga.at[i], ga_local(i))
            arrived(gxr.at[i], gx_r.at[i])
            parts.append(v + gxr[i])
        ring_end(gb, gb_r)
        gb_wait(top)
        parts += [ring_total(st, gb, gb_local) for st in (0, 1)]
        v = (LOSS_SCALE * jnp.concatenate(parts, axis=0)).T
        low, high = v[0:mine], v[mine:strip]
        gcs[...] = jnp.where(first, high, low)
        send(LAST, gcs, gcr, gc_r, mate)
        g_ref[:, my_cols] = jnp.where(first, low, high)

    def g_last():
        arrived(gcr, gc_r)
        g_ref[:, mate_cols] = gcr[...]

    t_pass(1)
    correlate(0, 1 - xl)
    cb_over(0)
    correlate(0, xl)
    ca_ring(0)
    nst[f] = ar_wait(ar_n, 5)
    f_start(nst, 6)
    cb_ring(0)
    ca_ring(1)
    t_near(1)
    cb_ring(1)
    ca_ring(2)
    t_far(1)
    cb_ring(2)
    t_normal(1, 1)
    t_normal(1, 2)
    ca_ring(3)
    t_normal(1, 3)
    correlate(1, 1 - xl)
    cb_over(1)
    correlate(1, xl)
    ca_far(1)
    cb_ring(3)
    ca_near(1)
    ca_over(0)
    cb_far(1)
    ca_mid(1)
    f_wait(nst, 6)
    slope(1, 0)
    slope(0, 0)
    slope_go(0, 0)
    cb_mid(1)
    slope_go(1, 0)
    cb_near(1)
    ca_over(1)
    s_ring(0, 1)
    s_ring(1, 1)
    slope(0, 1)
    slope_go(0, 1)
    s_ring(0, 2)
    slope(1, 1)
    slope_go(1, 1)
    u_start()
    s_ring(1, 2)
    sa_other(1)
    sa_on(1)
    s_ring(0, 3)
    sb_on(1, 1)
    s_ring(1, 3)
    sa_on_other(1)
    s_ring(0, 4)
    s_ring(1, 4)
    sb_end(1, 1)
    sa_end(1)
    upstream((0, xl), (1, xl))
    sb_last(0, 0)
    sb_last(1, 0)
    sb_last(1, 1)
    sums = delta()
    gradient(1 - xl, gs, 0, 1)
    gb_over(0)
    gradient(xl, gg, 0, 1)
    ga_step(0)
    gradient(1 - xl, gs, 1, nz // 2)
    gb_over(1, 2)
    gradient(xl, gg, 1, nz // 2)
    lf[f] = jnp.broadcast_to(jnp.sum(sums[lanes:2 * lanes], axis=0, keepdims=True), (8, 128))
    f_start(lf, 4)
    gb_step(0)
    gb_over(3, 4)
    ga_step(1)
    gb_step(1)
    gb_over(5, 6)
    ga_step(2)
    gb_step(2)
    gb_over(7)
    ga_step(3)
    gb_step(3)
    f_wait(lf, 4)
    lc[0] = jnp.sum(lf[...], axis=0)
    copy(lc.at[0], lc.at[1], ar_s.at[7], lc_r, mate).start()
    ga_over()
    g_core()
    arrived(lc.at[1], lc_r)
    loss_ref[0, 0] = jnp.sum((lc[0] + lc[1])[0:1]) / width_all
    g_last()
    ar_sent(ar_t, 0, chips)
    ar_sent(ar_p, 1, chips)
    ar_sent(ar_u, 2, chips)
    ar_sent(ar_n, 5, chips)
    ar_sent(nst, 6, feats)
    ar_sent(tst, 3, feats)
    ar_sent(lf, 4, feats)
    copy(lc.at[0], lc.at[1], ar_s.at[7], lc_r, mate).wait_send()
    for kind, size in weigh.items():
        there = pj if kind in (WEIGHT, LAST) else tn
        line = there.dtype.itemsize
        for n in there.shape[:-2] + there.shape[-1:]:
            line *= n
        assert size % line == 0 and size // line % 16 == 0
        there = there.at[(slice(None),) * (len(there.shape) - 2) + (pl.ds(0, size // line),)]
        copy(there, there, out_s.at[kind], lc_r, mate).wait_send()


def shards(nz, ny, student, weight, teacher):
    rows, wide = student.shape
    strip_w, cols = weight.shape
    half = cols // 2
    spans = ((ny + 1) * cols // 2, (ny - 1) * cols // 2)
    chips, feats = 2 * nz, 2 * ny
    strip = wide // chips
    quarter = half // 2
    piece = quarter // nz
    band = 7 * half // 32
    V = pltpu.VMEM
    D = pltpu.SemaphoreType.DMA
    data = [
        V((rows, wide), BF16),
        V((2, ny, 2, rows, cols), BF16),
        V((2, ny, 2 * rows, cols), BF16),
        V((2, 2, rows // 4, cols), BF16),
        V((rows, wide), BF16),
        V((2, nz, 2, strip_w, half), BF16),
        V((2 * rows, half), F32),
        V((half, 2 * rows), BF16),
        *[V((2, half, n), F32) for n in spans],
        V((2, nz // 2 + 1, 2, piece, spans[0]), BF16),
        V((2, 7, 3, piece, spans[1]), BF16),
        V((2, nz // 2 + 1, 2, piece, spans[0] // 2), BF16),
        V((2, 7, 3, piece, spans[1] // 2), BF16),
        *[V((piece, n), BF16) for n in spans],
        *[V((piece, n), BF16) for n in spans],
        *[V((nz, piece, n), BF16) for n in spans],
        *[V((nz, piece, n), BF16) for n in spans],
        *[V((2, 2, nz, piece, n), BF16) for n in spans],
        V((2 * rows, half), F32),
        V((nz, half, strip), F32),
        V((nz, half, strip), F32),
        V((nz, half - 2 * band, strip), F32),
        V((2, 2, nz // 2 + 1, 2, band, strip), F32),
        V((2, nz // 2 + 1, 2, half // 2 - band, strip), F32),
        V((2, band, strip), F32),
        V((2, band, strip), F32),
        V((strip // 2, half), F32),
        V((strip // 2, half), F32),
        V((chips, 8, 128), F32),
        V((chips, 8, 128), F32),
        V((chips, 8, 128), F32),
        V((chips, 8, 128), F32),
        V((feats, 8, 128), F32),
        V((feats, 8, 128), F32),
        V((4, 128, 128), F32),
        V((2, 2, 8, 128), F32),
        V((feats, 8, 128), F32),
        V((2, 8, 128), F32),
    ]
    sems = [
        D(shape) for shape in (
            (7,), (3,), (8,), (7,),
            (2, ny), (2, 2), (), (2, 5), (), (), (), (2, 4),
            (2, 2, nz // 2), (2,), (2, 2, nz // 2), (2, 5),
            (), (2, 4), (2, 2, nz // 2), (4,), (2, 2),
            (2, 2, nz // 2), (2,), (5,), (2, nz // 2), (), (),
        )
    ]
    vm = pl.BlockSpec(memory_space=pltpu.VMEM)
    sm = pl.BlockSpec(memory_space=pltpu.SMEM)
    far = pl.BlockSpec(memory_space=pl.ANY)
    loss, grad = pl.pallas_call(
        functools.partial(kernel, nz, ny),
        out_shape=(
            jax.ShapeDtypeStruct((1, 1), F32),
            jax.ShapeDtypeStruct((strip_w, cols), F32),
        ),
        in_specs=[far] * 3,
        out_specs=(sm, vm),
        scratch_shapes=data + sems,
        compiler_params=pltpu.CompilerParams(
            collective_id=0, has_side_effects=True, vmem_limit_bytes=56 * 1024 * 1024
        ),
    )(student, weight, teacher)
    return loss.reshape(()), grad


def solution(mesh):
    placed = (P("dp", None), P("dp", "feat"), P("dp", "feat"))
    nz, ny = mesh.shape["dp"] // 4, mesh.shape["feat"] // 2
    return jax.shard_map(
        functools.partial(shards, nz, ny), mesh=mesh, in_specs=placed,
        out_specs=(P(), P("dp", "feat")), check_vma=False,
    )
```
